256 devices in a mesh: dp: 16 (over y, x), tensor: 16 (over z, core).
Axes of the slice: x: 4, y: 4, z: 8, core: 2. Of those that a mesh axis runs over, the one named last changes fastest.
Arguments:
- tokens: bfloat16 [4096, 6144], P('dp'), may hold values from -6 to 6
- target: bfloat16 [4096, 6144], P('dp'), may hold values from -6 to 6
- pair_bias: float32 [4096, 32, 256], P('dp', 'tensor'), may hold values from -6 to 680
- neighbours: int32 [4096, 256], P('dp'), may hold values 0 or 1
- w_query: bfloat16 [6144, 4096], P('dp', 'tensor'), may hold values from -0.078125 to 0.078125
- w_key: bfloat16 [6144, 4096], P('dp', 'tensor'), may hold values from -0.078125 to 0.078125
- w_value: bfloat16 [6144, 4096], P('dp', 'tensor'), may hold values from -0.078125 to 0.078125
- w_out: bfloat16 [4096, 6144], P('tensor', 'dp'), may hold values from -0.09375 to 0.09375
- basis_value: float32 [6144, 4096], P('dp', 'tensor'), may hold values from -32 to 32
- basis_out: float32 [4096, 6144], P('tensor', 'dp'), may hold values from -32 to 32
- prior_value: float32 [6144, 4096], P('dp', 'tensor'), may hold values from -32 to 32
- prior_out: float32 [4096, 6144], P('tensor', 'dp'), may hold values from -32 to 32
- prior_beta: float32 [], replicated, may hold values from 10 to 60
Outputs:
- next_value: float32 [6144, 4096], P('dp', 'tensor')
- next_out: float32 [4096, 6144], P('tensor', 'dp')
- coefficients: float32 [2], replicated
The draws below stay inside these ranges and needn't reach their ends.
All inputs are finite; a program needn't handle non-finite values. No bound on the sum of `neighbours` on one device may be relied on, other than what follows from the above.
Results may differ from the reference program's by a relative error of at most 0.02.
Values may be sent and summed in bfloat16 or wider, within the bound.
A program may use at most 128 MiB of HBM per device.

```python
import math
import jax
import jax.numpy as jnp
from jax import lax

D = 6144
HEADS = 32
HEAD_DIM = 128
TOK_DEV = 256
AW = 4096
TOKENS = 4096
N_DP = 16
N_TENSOR = 16


def draw_pair_bias(key, part):
    key = jax.random.fold_in(key, 11)
    shape = (TOKENS, HEADS, TOK_DEV)
    return 1.5 * jax.random.truncated_normal(key, -4.0, 4.0, shape, jnp.float32)


def rising_field(key, shape, along, extent, rise):
    position = lax.broadcasted_iota(jnp.int32, shape, along).astype(jnp.float32) / float(extent)
    scale = jnp.exp(math.log(rise) * position)
    noise = jax.random.truncated_normal(key, -4.0, 4.0, shape, jnp.float32)
    return noise * scale


def draw_basis_value(key, part):
    key = jax.random.fold_in(key, 21)
    rise = 4.0
    return rising_field(key, (D, AW), 0, D, rise)


def draw_basis_out(key, part):
    key = jax.random.fold_in(key, 22)
    rise = 4.0
    return rising_field(key, (AW, D), 1, D, rise)


def draw_prior_value(key, part):
    key = jax.random.fold_in(key, 23)
    rise = 4.0
    return rising_field(key, (D, AW), 0, D, rise)


def draw_prior_out(key, part):
    key = jax.random.fold_in(key, 24)
    rise = 4.0
    return rising_field(key, (AW, D), 1, D, rise)


def with_ends(result, rng, least, largest):
    spot = [jax.random.randint(jax.random.fold_in(rng, axis), (), 0, length) for axis, length in enumerate(result.shape)]
    main_axis = result.shape.index(max(result.shape))
    neighbour = spot[:main_axis] + [(spot[main_axis] + 1) % result.shape[main_axis]] + spot[main_axis + 1:]
    return result.at[tuple(spot)].set(least).at[tuple(neighbour)].set(largest)


def level_of(own_key, dims, cuts, least, high):
    def one(dim, parts):
        steps = jax.random.uniform(jax.random.fold_in(jax.random.fold_in(own_key, 6), dim), (parts,), jnp.float32, least / len(cuts), high / len(cuts))
        return jnp.repeat(jnp.exp(steps), dims[dim] // parts).reshape((-1,) + (1,) * (len(dims) - dim - 1))

    level = one(*cuts[0])
    for cut in cuts[1:]:
        level = level * one(*cut)
    return level


def normal_values(own_key, shape, scale, reach, split=(), held_as=jnp.bfloat16):
    drawn = scale * jax.random.normal(own_key, shape, jnp.float32)
    if split:
        drawn = drawn * level_of(own_key, shape, split, -0.22, 0.18)
    return jnp.clip(drawn, -reach, reach).astype(held_as)


def setup_inputs(seed: int = 0) -> dict:
    key_list = jax.random.split(jax.random.key(seed), 14)
    tokens = normal_values(key_list[0], (TOKENS, D), 1.0, 6.0, ((0, 16),))
    target = normal_values(key_list[1], (TOKENS, D), 1.0, 6.0, ((0, 16),))
    pair_bias = draw_pair_bias(jax.random.fold_in(key_list[13], 71), 0)
    neighbours = with_ends((jax.random.randint(key_list[3], (TOKENS, TOK_DEV), 0, 2) < 1).astype(jnp.int32), jax.random.fold_in(key_list[3], 1), 0, 1)
    w_query = normal_values(key_list[4], (D, AW), D ** -0.5, 0.078125, ((0, 16), (1, 16)))
    w_key = normal_values(key_list[5], (D, AW), D ** -0.5, 0.078125, ((0, 16), (1, 16)))
    w_value = normal_values(key_list[6], (D, AW), D ** -0.5, 0.078125, ((0, 16), (1, 16)))
    w_out = normal_values(key_list[7], (AW, D), AW ** -0.5, 0.09375, ((0, 16), (1, 16)))
    basis_value = draw_basis_value(jax.random.fold_in(key_list[13], 71), 0)
    basis_out = draw_basis_out(jax.random.fold_in(key_list[13], 71), 0)
    prior_value = draw_prior_value(jax.random.fold_in(key_list[13], 71), 0)
    prior_out = draw_prior_out(jax.random.fold_in(key_list[13], 71), 0)
    prior_beta = jnp.clip(jax.random.uniform(key_list[12], (), jnp.float32, 10.0, 60.0), 10.0, 60.0)
    return dict(tokens=tokens, target=target, pair_bias=pair_bias, neighbours=neighbours, w_query=w_query, w_key=w_key, w_value=w_value, w_out=w_out, basis_value=basis_value, basis_out=basis_out, prior_value=prior_value, prior_out=prior_out, prior_beta=prior_beta)


loss_gain = 32.0
epsilon = 1e-06

def block_round(terms):
    rounded = lax.optimization_barrier(terms.astype(jnp.bfloat16))
    return lax.optimization_barrier(jnp.sum(rounded.astype(jnp.float32), axis=0))

def group_curvature(tokens, target, pair_bias, neighbours, w_query, w_key, w_value, w_out, tangent_value, tangent_out):
    count = tokens.shape[0]
    width = w_query.shape[1]
    blocks = N_TENSOR
    block_width = width // blocks
    xf = tokens.astype(jnp.float32)
    normed = (xf * lax.rsqrt(lax.optimization_barrier(jnp.mean(xf * xf, axis=1, keepdims=True)) + epsilon)).astype(jnp.bfloat16)
    query = jnp.dot(normed, w_query, preferred_element_type=jnp.float32).astype(jnp.bfloat16)
    keys = jnp.dot(normed, w_key, preferred_element_type=jnp.float32).astype(jnp.bfloat16)
    values = jnp.dot(normed, w_value, preferred_element_type=jnp.float32).astype(jnp.bfloat16)
    tangent_values = (jnp.dot(normed, tangent_value, preferred_element_type=jnp.float32) / math.sqrt(D)).astype(jnp.bfloat16)
    shape3 = (count, HEADS, HEAD_DIM)
    scores = jnp.einsum('thd,shd->ths', query.reshape(shape3).astype(jnp.float32), keys.reshape(shape3).astype(jnp.float32))
    scores = scores / math.sqrt(HEAD_DIM) + pair_bias
    rows = lax.broadcasted_iota(jnp.int32, (count, count), 0)
    cols = lax.broadcasted_iota(jnp.int32, (count, count), 1)
    allowed = (neighbours == 1) | (jnp.abs(rows - cols) <= 1)
    scores = jnp.where(allowed[:, None, :], scores, -jnp.inf)
    probs = jax.nn.softmax(scores, axis=2).astype(jnp.bfloat16)
    probs_f = probs.astype(jnp.float32)
    mixed = jnp.einsum('ths,shd->thd', probs_f, values.reshape(shape3).astype(jnp.float32)).astype(jnp.bfloat16).reshape(count, width)
    tangent_mixed = jnp.einsum('ths,shd->thd', probs_f, tangent_values.reshape(shape3).astype(jnp.float32)).astype(jnp.bfloat16).reshape(count, width)
    mixed_b = mixed.astype(jnp.float32).reshape(count, blocks, block_width)
    tmixed_b = tangent_mixed.astype(jnp.float32).reshape(count, blocks, block_width)
    out_b = w_out.astype(jnp.float32).reshape(blocks, block_width, -1)
    tout_b = tangent_out.astype(jnp.float32).reshape(blocks, block_width, -1)
    attn = block_round(jnp.einsum('tna,nad->ntd', mixed_b, out_b))
    tangent_attn = block_round(jnp.einsum('tna,nad->ntd', mixed_b, tout_b) / math.sqrt(width) + jnp.einsum('tna,nad->ntd', tmixed_b, out_b))
    factor = loss_gain * width / TOKENS
    error = ((xf + attn - target.astype(jnp.float32)) * factor).astype(jnp.bfloat16)
    tangent_error = (tangent_attn * factor).astype(jnp.bfloat16)
    error_f = error.astype(jnp.float32)
    terror_f = tangent_error.astype(jnp.float32)
    out_term = (jnp.einsum('ta,td->ad', tangent_mixed.astype(jnp.float32), error_f) + jnp.einsum('ta,td->ad', mixed.astype(jnp.float32), terror_f)) / math.sqrt(width)
    back_tangent = (jnp.einsum('td,ad->ta', terror_f, w_out.astype(jnp.float32)) + jnp.einsum('td,ad->ta', error_f, tangent_out.astype(jnp.float32)) / math.sqrt(width)).astype(jnp.bfloat16)
    value_back = jnp.einsum('ths,thd->shd', probs_f, back_tangent.reshape(shape3).astype(jnp.float32)).astype(jnp.bfloat16).reshape(count, width)
    value_term = jnp.einsum('ti,ta->ia', normed.astype(jnp.float32), value_back.astype(jnp.float32)) / math.sqrt(D)
    return (value_term.astype(jnp.bfloat16), out_term.astype(jnp.bfloat16))

def reference(tokens, target, pair_bias, neighbours, w_query, w_key, w_value, w_out, basis_value, basis_out, prior_value, prior_out, prior_beta):
    tangent_value = basis_value.astype(jnp.bfloat16)
    tangent_out = basis_out.astype(jnp.bfloat16)

    def step(carry, index):

        def group_rows(array):
            return lax.dynamic_slice_in_dim(array, index * TOK_DEV, TOK_DEV, 0)
        value_term, out_term = group_curvature(group_rows(tokens), group_rows(target), group_rows(pair_bias), group_rows(neighbours), w_query, w_key, w_value, w_out, tangent_value, tangent_out)
        return ((carry[0] + value_term.astype(jnp.float32), carry[1] + out_term.astype(jnp.float32)), None)
    start = (jnp.zeros(basis_value.shape, jnp.float32), jnp.zeros(basis_out.shape, jnp.float32))
    (curv_value, curv_out), unused = lax.scan(step, start, jnp.arange(N_DP, dtype=jnp.int32))
    count = 2.0 * D * AW
    alpha = (jnp.sum(basis_value * curv_value) + jnp.sum(basis_out * curv_out)) / count
    rest_value = curv_value - alpha * basis_value - prior_beta * prior_value
    rest_out = curv_out - alpha * basis_out - prior_beta * prior_out
    beta = jnp.sqrt((jnp.sum(rest_value * rest_value) + jnp.sum(rest_out * rest_out)) / count + epsilon)
    return (rest_value / beta, rest_out / beta, jnp.stack([alpha, beta]))
```

```python
import math

import jax
import jax.numpy as jnp
from jax import lax
from jax.experimental import pallas as pl
from jax.experimental.pallas import tpu as pltpu
from jax.sharding import PartitionSpec as P

HEAD_DIM = 128
SIDE = 4
ROWS = 16

loss_gain = 32.0
epsilon = 1e-06

MESH = pl.DeviceIdType.MESH
BF = jnp.bfloat16
F32 = jnp.float32
VMEM = pl.BlockSpec(memory_space=pltpu.VMEM)
SMEM = pl.BlockSpec(memory_space=pltpu.SMEM)
DMA = pltpu.SemaphoreType.DMA


def coords():
    dp = lax.axis_index("dp")
    t = lax.axis_index("tensor")
    return dp // SIDE, dp % SIDE, t


def at(y, x, t):
    return (((y + 2 * SIDE) % SIDE) * SIDE + (x + 2 * SIDE) % SIDE, (t + 32) % 16)


def along_x(j):
    y, x, t = coords()
    return at(y, x + j, t)


def along_y(j):
    y, x, t = coords()
    return at(y + j, x, t)


def along_t(k):
    y, x, t = coords()
    return at(y, x, t + k)


def along_z(k):
    y, x, t = coords()
    return at(y, x, t + 2 * k)


def other_core():
    y, x, t = coords()
    return at(y, x, t + 1 - 2 * (t % 2))


def greet(peers):
    barrier = pltpu.get_barrier_semaphore()
    for peer in peers:
        pl.semaphore_signal(barrier, inc=1, device_id=peer, device_id_type=MESH)
    pl.semaphore_wait(barrier, len(peers))


def send(src, dst, ssem, rsem, peer):
    copy = pltpu.make_async_remote_copy(
        src_ref=src,
        dst_ref=dst,
        send_sem=ssem,
        recv_sem=rsem,
        device_id=peer,
        device_id_type=MESH,
    )
    copy.start()
    return copy


def call(kernel, number, out_shape, scratch, *args, in_specs=None):
    return pl.pallas_call(
        kernel,
        out_shape=out_shape,
        in_specs=in_specs or [VMEM] * len(args),
        out_specs=jax.tree.map(lambda _: VMEM, out_shape),
        scratch_shapes=scratch,
        compiler_params=pltpu.CompilerParams(
            collective_id=number, has_side_effects=True, vmem_limit_bytes=48 * 2**20
        ),
    )(*args)


def shape(dims, dtype):
    return jax.ShapeDtypeStruct(dims, dtype)


NEAR = (1, 3, 2)


def spread_kernel(piece, wqk, wvt, diff, rows, gqk, gvt, diffs, ps, pr, ws, wr, ds, dr, zs, zr, cs, cr, ls):
    y, x, t = coords()
    peers = [along_x(j) for j in NEAR] + [along_y(j) for j in NEAR]
    corners = [at(y + i, x + j, t) for i in NEAR for j in NEAR]
    greet(peers + corners + [along_z(1), along_z(-1), other_core()])
    copies = []
    pieces = []
    for j in NEAR:
        pieces.append(
            send(piece.at[j - 1], rows.at[j - 1, t], ps.at[j - 1], pr.at[j - 1], along_x(j))
        )
        pieces.append(
            send(piece.at[j + 2], rows.at[j + 2, t], ps.at[j + 2], pr.at[j + 2], along_y(j))
        )
    for j in NEAR:
        copies.append(send(wqk, gqk.at[y], ws.at[j - 1], wr.at[j - 1], along_y(j)))
        copies.append(send(wvt, gvt.at[x], ws.at[j + 2], wr.at[j + 2], along_x(j)))
    me = y * SIDE + x
    k = 0
    for i in range(SIDE):
        for j in range(SIDE):
            if i or j:
                yy, xx = (y + i) % SIDE, (x + j) % SIDE
                copies.append(
                    send(
                        diff.at[yy * SIDE + xx],
                        diffs.at[me],
                        ds.at[k],
                        dr.at[k],
                        (yy * SIDE + xx, t),
                    )
                )
                k += 1
    mine = [
        pltpu.make_async_copy(wqk, gqk.at[y], ls.at[0]),
        pltpu.make_async_copy(wvt, gvt.at[x], ls.at[1]),
        pltpu.make_async_copy(diff.at[me], diffs.at[me], ls.at[2]),
    ]
    for copy in mine:
        copy.start()
    for copy in pieces:
        copy.wait_recv()
    c = t % 2
    own = rows.at[:, t]
    copies.append(send(own, own, zs.at[0, 0], zr.at[0, 0], along_z(1)))
    copies.append(send(own, own, zs.at[1, 0], zr.at[1, 0], along_z(-1)))
    copies.append(send(own, own, cs.at[0], cr.at[0], other_core()))
    for step in range(1, 4):
        for way in range(2):
            sign = 1 - 2 * way
            slot = (t - 2 * sign * step + 32) % 16
            got = rows.at[:, slot]
            arrived = pltpu.make_async_remote_copy(
                src_ref=got,
                dst_ref=got,
                send_sem=zs.at[way, step - 1],
                recv_sem=zr.at[way, step - 1],
                device_id=along_z(-sign),
                device_id_type=MESH,
            )
            arrived.wait_recv()
            part = got if step < 3 else rows.at[pl.ds(3 * way, 3), slot]
            copies.append(send(part, part, zs.at[way, step], zr.at[way, step], along_z(sign)))
            k = 2 * step - 1 + way
            copies.append(send(got, got, cs.at[k], cr.at[k], other_core()))
    far = (t + 8) % 16
    for way in range(2):
        part = rows.at[pl.ds(3 * way, 3), far]
        pltpu.make_async_remote_copy(
            src_ref=part,
            dst_ref=part,
            send_sem=zs.at[way, 3],
            recv_sem=zr.at[way, 3],
            device_id=along_z(1),
            device_id_type=MESH,
        ).wait_recv()
    far_ref = rows.at[:, far]
    copies.append(send(far_ref, far_ref, cs.at[7], cr.at[7], other_core()))
    for copy in pieces:
        copy.wait_send()
    for copy in mine:
        copy.wait()
    for copy in copies[:21]:
        copy.wait()
    for copy in copies[21:]:
        copy.wait_send()
    for k in range(8):
        step, way = (k + 1) // 2, (k + 1) % 2
        shift = 8 if k == 7 else 2 * step * (1 - 2 * way)
        slot = (t + 1 - 2 * c - shift + 32) % 16
        got = rows.at[:, slot]
        pltpu.make_async_remote_copy(
            src_ref=got,
            dst_ref=got,
            send_sem=cs.at[k],
            recv_sem=cr.at[k],
            device_id=other_core(),
            device_id_type=MESH,
        ).wait_recv()


def spread(piece, wqk, wvt, diff):
    wide = piece.shape[2]
    return call(
        spread_kernel,
        0,
        (
            shape((6, 16, ROWS, wide), BF),
            shape((SIDE,) + wqk.shape, BF),
            shape((SIDE,) + wvt.shape, BF),
            shape(diff.shape, F32),
        ),
        [
            DMA((6,)),
            DMA((6,)),
            DMA((6,)),
            DMA((6,)),
            DMA((15,)),
            DMA((15,)),
            DMA((2, 4)),
            DMA((2, 4)),
            DMA((8,)),
            DMA((8,)),
            DMA((3,)),
        ],
        piece,
        wqk,
        wvt,
        diff,
    )


def swap_kernel(sign, whole, a, b, ra, rb, ss, rs):
    greet([along_x(j) for j in NEAR] + [along_y(j) for j in NEAR])
    copies = []
    for j in NEAR:
        src = a if whole else a.at[j - 1]
        copies.append(send(src, ra.at[j - 1], ss.at[j - 1], rs.at[j - 1], along_x(sign * j)))
        src = b if whole else b.at[j - 1]
        copies.append(send(src, rb.at[j - 1], ss.at[j + 2], rs.at[j + 2], along_y(sign * j)))
    for copy in copies:
        copy.wait()


def swap(number, sign, whole, a, b):
    def kernel(*refs):
        swap_kernel(sign, whole, *refs)

    lead = (3,) if whole else ()
    return call(
        kernel,
        number,
        (shape(lead + a.shape, a.dtype), shape(lead + b.shape, b.dtype)),
        [DMA((6,)), DMA((6,))],
        a,
        b,
    )


def mix_kernel(mix, full, ts, tr, as_, ar, bs, br, ls):
    y, x, t = coords()
    greet(
        [along_t(k) for k in range(1, 16)]
        + [along_x(j) for j in NEAR]
        + [along_y(j) for j in NEAR]
    )
    copies = []
    for k in range(1, 16):
        to = (t + k) % 16
        copies.append(
            send(
                mix.at[pl.ds(pl.multiple_of(to * ROWS, ROWS), ROWS)],
                full.at[y, x, t],
                ts.at[k],
                tr.at[k],
                along_t(k),
            )
        )
    own = pltpu.make_async_copy(
        mix.at[pl.ds(pl.multiple_of(t * ROWS, ROWS), ROWS)], full.at[y, x, t], ls.at[0]
    )
    own.start()
    own.wait()
    for copy in copies:
        copy.wait_recv()
    low, high = pl.ds(0, 8), pl.ds(8, 8)
    first, second = [], []
    a, b = full.at[y, x, low], full.at[y, x, high]
    for j in NEAR:
        first.append(send(a, a, as_.at[0, j - 1], ar.at[0, j - 1], along_x(j)))
        first.append(send(b, b, bs.at[0, j - 1], br.at[0, j - 1], along_y(j)))
    for j in NEAR:
        second.append(send(a, a, as_.at[1, j - 1], ar.at[1, j - 1], along_y(j)))
        second.append(send(b, b, bs.at[1, j - 1], br.at[1, j - 1], along_x(j)))
    for i in NEAR:
        k = NEAR.index(i) * 2
        first[k].wait_recv()
        first[k + 1].wait_recv()
        a = full.at[y, (x - i + SIDE) % SIDE, low]
        b = full.at[(y - i + SIDE) % SIDE, x, high]
        for j in NEAR:
            second.append(send(a, a, as_.at[1 + i, j - 1], ar.at[1 + i, j - 1], along_y(j)))
            second.append(send(b, b, bs.at[1 + i, j - 1], br.at[1 + i, j - 1], along_x(j)))
    for copy in second:
        copy.wait()
    for copy in first + copies:
        copy.wait_send()


def spread_mix(mix):
    return call(
        mix_kernel,
        1,
        shape((SIDE, SIDE, 16, ROWS, mix.shape[1]), BF),
        [DMA((16,)), DMA((16,)), DMA((5, 3)), DMA((5, 3)), DMA((5, 3)), DMA((5, 3)), DMA((1,))],
        mix,
    )


def back_kernel(part, out, ra, rb, sa, sb, qa, qb, done, s1, r1, s2, r2, ts, tr, ls):
    y, x, t = coords()
    half = part.shape[3] // 2
    low, high = pl.ds(0, half), pl.ds(half, half)
    greet(
        [along_t(k) for k in range(1, 16)]
        + [along_x(j) for j in NEAR]
        + [along_y(j) for j in NEAR]
    )
    first, second, third = [], [], []
    for j in NEAR:
        first.append(
            send(part.at[(y + j) % SIDE, :, :, low], ra.at[j - 1], s1.at[0, j - 1], r1.at[0, j - 1], along_y(j))
        )
        first.append(
            send(part.at[:, (x + j) % SIDE, :, high], rb.at[j - 1], s1.at[1, j - 1], r1.at[1, j - 1], along_x(j))
        )
    for copy in first:
        copy.wait_recv()
    for i in range(SIDE):
        total = part[y, i, :, :half].astype(F32)
        for j in range(3):
            total = total + ra[j, i].astype(F32)
        sa[i] = total.astype(BF)
        total = part[i, x, :, half:].astype(F32)
        for j in range(3):
            total = total + rb[j, i].astype(F32)
        sb[i] = total.astype(BF)
    for j in NEAR:
        second.append(send(sa.at[(x + j) % SIDE], qa.at[j - 1], s2.at[0, j - 1], r2.at[0, j - 1], along_x(j)))
        second.append(send(sb.at[(y + j) % SIDE], qb.at[j - 1], s2.at[1, j - 1], r2.at[1, j - 1], along_y(j)))
    for copy in second:
        copy.wait_recv()
    total = sa[x].astype(F32)
    for j in range(3):
        total = total + qa[j].astype(F32)
    wide = out.shape[2]
    for k in range(8):
        done[k] = total[:, k * wide : (k + 1) * wide].astype(BF)
    total = sb[y].astype(F32)
    for j in range(3):
        total = total + qb[j].astype(F32)
    for k in range(8):
        done[8 + k] = total[:, k * wide : (k + 1) * wide].astype(BF)
    for k in range(1, 16):
        third.append(send(done.at[(t + k) % 16], out.at[t], ts.at[k], tr.at[k], along_t(k)))
    own = pltpu.make_async_copy(done.at[t], out.at[t], ls.at[0])
    own.start()
    own.wait()
    for copy in third:
        copy.wait()
    for copy in first + second:
        copy.wait_send()


def collect_back(part):
    half = part.shape[3] // 2
    return call(
        back_kernel,
        2,
        shape((16, ROWS, part.shape[3] // 16), BF),
        [
            pltpu.VMEM((3, SIDE, ROWS, half), BF),
            pltpu.VMEM((3, SIDE, ROWS, half), BF),
            pltpu.VMEM((SIDE, ROWS, half), BF),
            pltpu.VMEM((SIDE, ROWS, half), BF),
            pltpu.VMEM((3, ROWS, half), BF),
            pltpu.VMEM((3, ROWS, half), BF),
            pltpu.VMEM((16, ROWS, part.shape[3] // 16), BF),
            DMA((2, 3)),
            DMA((2, 3)),
            DMA((2, 3)),
            DMA((2, 3)),
            DMA((16,)),
            DMA((16,)),
            DMA((1,)),
        ],
        part,
    )


def last_kernel(
    entries, cv, co, bv, bo, pv, po, pb, nv, no, coef, one, two, s1, r1, s2, r2
):
    y, x, t = coords()
    me = y * SIDE + x
    greet(
        [along_t(k) for k in range(1, 16)]
        + [at(y + i, x + j, t) for i in range(SIDE) for j in range(SIDE) if i or j]
    )

    def total(value, turn):
        one[turn, t] = jnp.full((8, 128), value, F32)
        copies = []
        for k in range(1, 16):
            copies.append(
                send(one.at[turn, t], one.at[turn, t], s1.at[turn, k], r1.at[turn, k], along_t(k))
            )
        for copy in copies:
            copy.wait()
        two[turn, me] = jnp.sum(one[turn], axis=0)
        copies = []
        k = 0
        for i in range(SIDE):
            for j in range(SIDE):
                if i or j:
                    copies.append(
                        send(
                            two.at[turn, me],
                            two.at[turn, me],
                            s2.at[turn, k],
                            r2.at[turn, k],
                            at(y + i, x + j, t),
                        )
                    )
                    k += 1
        for copy in copies:
            copy.wait()
        return jnp.sum(two[turn], axis=0)[0:1, 0:1] / entries

    alpha = total(jnp.sum(bv[...] * cv[...]) + jnp.sum(bo[...] * co[...]), 0)
    nv[...] = cv[...] - alpha * bv[...] - pb[0, 0] * pv[...]
    no[...] = co[...] - alpha * bo[...] - pb[0, 0] * po[...]
    squares = total(jnp.sum(nv[...] * nv[...]) + jnp.sum(no[...] * no[...]), 1)
    beta = jnp.sqrt(squares + epsilon)
    nv[...] = nv[...] / beta
    no[...] = no[...] / beta
    coef[0:1] = jnp.broadcast_to(alpha, (1, 128))
    coef[1:2] = jnp.broadcast_to(beta, (1, 128))


def finish(entries, cv, co, bv, bo, pv, po, pb):
    def kernel(*refs):
        last_kernel(entries, *refs)

    nv, no, coef = call(
        kernel,
        3,
        (shape(cv.shape, F32), shape(co.shape, F32), shape((8, 128), F32)),
        [
            pltpu.VMEM((2, 16, 8, 128), F32),
            pltpu.VMEM((2, 16, 8, 128), F32),
            DMA((2, 16)),
            DMA((2, 16)),
            DMA((2, 15)),
            DMA((2, 15)),
        ],
        cv,
        co,
        bv,
        bo,
        pv,
        po,
        pb.reshape(1, 1),
        in_specs=[VMEM] * 6 + [SMEM],
    )
    return nv, no, coef[:2, 0]


def pick(array, index, axis):
    return lax.dynamic_index_in_dim(array, index, axis, keepdims=False)


def body(
    tokens,
    target,
    pair_bias,
    neighbours,
    w_query,
    w_key,
    w_value,
    w_out,
    basis_value,
    basis_out,
    prior_value,
    prior_out,
    prior_beta,
):
    count, features = tokens.shape
    local_width = w_query.shape[1]
    heads_here = local_width // HEAD_DIM
    full_width = local_width * lax.axis_size("tensor")
    groups = lax.axis_size("dp")
    total_tokens = count * groups
    block = features // groups
    dp = lax.axis_index("dp")
    t = lax.axis_index("tensor")
    y, x = dp // SIDE, dp % SIDE
    scale_out = 1.0 / math.sqrt(full_width)
    scale_value = 1.0 / math.sqrt(features)

    out_all = lax.all_gather(
        jnp.concatenate([w_out, basis_out.astype(BF)], axis=1), "tensor", axis=0, tiled=False
    )

    xf = tokens.astype(F32)
    normed = (xf * lax.rsqrt(jnp.mean(xf * xf, axis=1, keepdims=True) + epsilon)).astype(BF)
    split = normed.reshape(count, SIDE, SIDE, block)
    own_x = pick(split, x, 2).reshape(count, SIDE * block)
    own_y = pick(split, y, 1).reshape(count, SIDE * block)
    few = lax.dynamic_slice_in_dim(split, t * ROWS, ROWS, 0)
    piece = jnp.stack(
        [pick(few, (x + j) % SIDE, 2).reshape(ROWS, SIDE * block) for j in (1, 2, 3)]
        + [pick(few, (y + j) % SIDE, 1).reshape(ROWS, SIDE * block) for j in (1, 2, 3)]
    )
    few_x = lax.dynamic_slice_in_dim(tokens, t * ROWS, ROWS, 0).astype(F32)
    few_t = lax.dynamic_slice_in_dim(target, t * ROWS, ROWS, 0).astype(F32)
    diff = (few_x - few_t).reshape(ROWS, groups, block).transpose(1, 0, 2)
    rows, gqk, gvt, diffs = spread(
        piece,
        jnp.concatenate([w_query, w_key], axis=1),
        jnp.concatenate([w_value, basis_value.astype(BF)], axis=1),
        diff,
    )
    wide = SIDE * block
    rows_x = rows[:3].reshape(3 * count, wide)
    rows_y = rows[3:].reshape(3 * count, wide)
    gqk = gqk.reshape(wide, 2 * local_width)
    gvt = gvt.reshape(wide, 2 * local_width)

    def dot(a, b):
        return jnp.dot(a, b, preferred_element_type=F32)

    qk_else = dot(rows_x, gqk).astype(BF).reshape(3, count, 2 * local_width)
    vt_else = dot(rows_y, gvt).astype(BF).reshape(3, count, 2 * local_width)
    qk_got, vt_got = swap(4, -1, False, qk_else, vt_else)
    qk = dot(own_x, gqk) + jnp.sum(qk_got.astype(F32), axis=0)
    vt = dot(own_y, gvt) + jnp.sum(vt_got.astype(F32), axis=0)
    shape3 = (count, heads_here, HEAD_DIM)
    query = qk[:, :local_width].astype(BF).reshape(shape3)
    keys = qk[:, local_width:].astype(BF).reshape(shape3)
    values = vt[:, :local_width].astype(BF).reshape(shape3)
    tangent_values = (vt[:, local_width:] / math.sqrt(features)).astype(BF).reshape(shape3)

    scores = (
        jnp.einsum("thd,shd->ths", query, keys, preferred_element_type=F32) / math.sqrt(HEAD_DIM)
        + pair_bias
    )
    at_row = lax.broadcasted_iota(jnp.int32, (count, count), 0)
    at_col = lax.broadcasted_iota(jnp.int32, (count, count), 1)
    allowed = (neighbours == 1) | (jnp.abs(at_row - at_col) <= 1)
    scores = jnp.where(allowed[:, None, :], scores, -jnp.inf)
    probs = jax.nn.softmax(scores, axis=2).astype(BF)
    mixed = jnp.einsum("ths,shd->thd", probs, values, preferred_element_type=F32)
    tangent_mixed = jnp.einsum("ths,shd->thd", probs, tangent_values, preferred_element_type=F32)
    mix = jnp.concatenate(
        [
            mixed.astype(BF).reshape(count, local_width),
            tangent_mixed.astype(BF).reshape(count, local_width),
        ],
        axis=1,
    )

    full = spread_mix(mix).reshape(groups, 16, ROWS, 2 * local_width)
    full = full.transpose(0, 2, 1, 3).reshape(groups * ROWS, 16, 2, local_width)
    mixed_all = full[:, :, 0].reshape(groups * ROWS, full_width)
    tangent_all = full[:, :, 1].reshape(groups * ROWS, full_width)
    out_all = out_all.reshape(full_width, 2 * block)
    out_full, tangent_out = out_all[:, :block], out_all[:, block:]
    attn = dot(mixed_all, out_full)
    tangent_attn = dot(mixed_all, tangent_out) * scale_out + dot(tangent_all, out_full)
    factor = loss_gain * full_width / total_tokens
    error = ((diffs.reshape(groups * ROWS, block) + attn) * factor).astype(BF)
    tangent_error = (tangent_attn * factor).astype(BF)

    back_part = jnp.einsum(
        "td,ad->ta", tangent_error, out_full, preferred_element_type=F32
    ) + scale_out * jnp.einsum("td,ad->ta", error, tangent_out, preferred_element_type=F32)
    curv_out_part = (
        jnp.einsum("ta,td->ad", tangent_all, error, preferred_element_type=F32)
        + jnp.einsum("ta,td->ad", mixed_all, tangent_error, preferred_element_type=F32)
    ) * scale_out
    curv_out = lax.psum_scatter(
        curv_out_part.astype(BF), "tensor", scatter_dimension=0, tiled=True
    ).astype(F32)
    back_tangent = collect_back(
        back_part.astype(BF).reshape(SIDE, SIDE, ROWS, full_width)
    ).reshape(shape3)

    value_back = (
        jnp.einsum("ths,thd->shd", probs, back_tangent, preferred_element_type=F32)
        .astype(BF)
        .reshape(count, local_width)
    )
    back_x, back_y = value_back[:, :HEAD_DIM], value_back[:, HEAD_DIM:]
    got_x, got_y = swap(5, 1, True, back_x, back_y)

    def outer(own, rest, mine, got):
        return (
            jnp.einsum("td,ta->da", own, mine, preferred_element_type=F32)
            + jnp.einsum(
                "td,ta->da", rest, got.reshape(3 * count, HEAD_DIM), preferred_element_type=F32
            )
        ) * scale_value

    curv_x = outer(own_x, rows_x, back_x, got_x).reshape(SIDE, block, HEAD_DIM)
    curv_y = outer(own_y, rows_y, back_y, got_y).reshape(SIDE, block, HEAD_DIM)

    def others(array, mine):
        return jnp.stack([pick(array, (mine + j) % SIDE, 0) for j in (1, 2, 3)]).astype(BF)

    sum_y, sum_x = swap(6, 1, False, others(curv_y, x), others(curv_x, y))
    curv_value = jnp.concatenate(
        [
            pick(curv_x, y, 0) + jnp.sum(sum_x.astype(F32), axis=0),
            pick(curv_y, x, 0) + jnp.sum(sum_y.astype(F32), axis=0),
        ],
        axis=1,
    )
    entries = 2.0 * features * full_width
    return finish(
        entries, curv_value, curv_out, basis_value, basis_out, prior_value, prior_out, prior_beta
    )


def solution(mesh):
    placed = (
        P("dp", None),
        P("dp", None),
        P("dp", "tensor", None),
        P("dp", None),
        P("dp", "tensor"),
        P("dp", "tensor"),
        P("dp", "tensor"),
        P("tensor", "dp"),
        P("dp", "tensor"),
        P("tensor", "dp"),
        P("dp", "tensor"),
        P("tensor", "dp"),
        P(),
    )
    return jax.shard_map(
        body,
        mesh=mesh,
        in_specs=placed,
        out_specs=(P("dp", "tensor"), P("tensor", "dp"), P()),
        check_vma=False,
    )
```

```python
import math

import jax
import jax.numpy as jnp
from jax import lax
from jax.experimental import pallas as pl
from jax.experimental.pallas import tpu as pltpu
from jax.sharding import PartitionSpec as P

HEAD_DIM = 128
SIDE = 4
ROWS = 16

loss_gain = 32.0
epsilon = 1e-06

MESH = pl.DeviceIdType.MESH
BF = jnp.bfloat16
F32 = jnp.float32
VMEM = pl.BlockSpec(memory_space=pltpu.VMEM)
ANY = pl.BlockSpec(memory_space=pl.ANY)
SMEM = pl.BlockSpec(memory_space=pltpu.SMEM)
DMA = pltpu.SemaphoreType.DMA


def coords():
    dp = lax.axis_index("dp")
    t = lax.axis_index("tensor")
    return dp // SIDE, dp % SIDE, t


def at(y, x, t):
    return (((y + 2 * SIDE) % SIDE) * SIDE + (x + 2 * SIDE) % SIDE, (t + 32) % 16)


def along_x(j):
    y, x, t = coords()
    return at(y, x + j, t)


def along_y(j):
    y, x, t = coords()
    return at(y + j, x, t)


def along_t(k):
    y, x, t = coords()
    return at(y, x, t + k)


def along_z(k):
    y, x, t = coords()
    return at(y, x, t + 2 * k)


def other_core():
    y, x, t = coords()
    return at(y, x, t + 1 - 2 * (t % 2))


def greet(peers):
    barrier = pltpu.get_barrier_semaphore()
    for peer in peers:
        pl.semaphore_signal(barrier, inc=1, device_id=peer, device_id_type=MESH)
    pl.semaphore_wait(barrier, len(peers))


def send(src, dst, ssem, rsem, peer):
    copy = pltpu.make_async_remote_copy(
        src_ref=src,
        dst_ref=dst,
        send_sem=ssem,
        recv_sem=rsem,
        device_id=peer,
        device_id_type=MESH,
    )
    copy.start()
    return copy


NEAR = (1, 3, 2)
WIDE = 256
HALF = 128
BLOCK = 384
COUNT = 256


def dot(a, b):
    return jnp.dot(a, b, preferred_element_type=F32)


def dot_t(a, b):
    return lax.dot_general(a, b, (((1,), (1,)), ((), ())), preferred_element_type=F32)


def arrival(ref, ssem, rsem):
    y, x, t = coords()
    return pltpu.make_async_remote_copy(
        src_ref=ref,
        dst_ref=ref,
        send_sem=ssem,
        recv_sem=rsem,
        device_id=at(y, x, t + 2),
        device_id_type=MESH,
    )


class Ring:
    def __init__(self, slot, half, zs, zr, cs, cr):
        self.slot, self.half = slot, half
        self.zs, self.zr, self.cs, self.cr = zs, zr, cs, cr
        self.sent = []

    def start(self):
        y, x, t = coords()
        own = self.slot(t)
        for way in range(2):
            self.sent.append(
                send(own, own, self.zs.at[way, 0], self.zr.at[way, 0], along_z(1 - 2 * way))
            )
        self.sent.append(send(own, own, self.cs.at[0], self.cr.at[0], other_core()))

    def step(self, step):
        y, x, t = coords()
        for way in range(2):
            sign = 1 - 2 * way
            slot = (t - 2 * sign * step + 32) % 16
            got = self.slot(slot)
            arrival(got, self.zs.at[way, step - 1], self.zr.at[way, step - 1]).wait_recv()
            part = got if step < 3 else self.half(slot, way)
            self.sent.append(
                send(part, part, self.zs.at[way, step], self.zr.at[way, step], along_z(sign))
            )
            k = 2 * step - 1 + way
            self.sent.append(send(got, got, self.cs.at[k], self.cr.at[k], other_core()))

    def finish(self):
        y, x, t = coords()
        far = (t + 8) % 16
        for way in range(2):
            part = self.half(far, way)
            arrival(part, self.zs.at[way, 3], self.zr.at[way, 3]).wait_recv()
        got = self.slot(far)
        self.sent.append(send(got, got, self.cs.at[7], self.cr.at[7], other_core()))

    def settle(self):
        y, x, t = coords()
        for copy in self.sent:
            copy.wait_send()
        for k in range(8):
            step, way = (k + 1) // 2, (k + 1) % 2
            shift = 8 if k == 7 else 2 * step * (1 - 2 * way)
            got = self.slot((t + 1 - 2 * (t % 2) - shift + 32) % 16)
            arrival(got, self.cs.at[k], self.cr.at[k]).wait_recv()


def step_kernel(
    tokens, target, bias, near, wq, wk, wv, wo, bv, bo, pv, po, pb,
    nv, no, coef,
    tok16, tgt16, tok, n16, diff, diffs, rows, gqk, gvt, nx, ny, uall,
    bvv, bov, pvv, pov, nearv, biasv,
    pq, pt, rq, rv, accq, accv, qk, vt, probs, mix, full,
    acc1, acc2, err, terr, errt, terrt, bp, ra, rb, sa, sb, qa, qb, done, bt,
    co, rc, sc, rz, vb, gx, gy, cxf, cyf, cxb, cyb, hx, hy, cv, cw, one, two,
    ls, ps, pr, ws, wr, ds, dr, zs, zr, cs, cr, us, ur, vs, vr, xs, xr, ts, tr,
    as_, ar, bs, br, s1, r1, s2, r2, s3, r3, s4, r4, s5, r5, s6, r6, s7, r7, o1, i1, o2, i2,
):
    y, x, t = coords()
    c = t % 2
    z = t // 2
    me = y * SIDE + x
    full_width = 16 * WIDE
    features = 16 * BLOCK
    scale_out = 1.0 / math.sqrt(full_width)
    scale_value = 1.0 / math.sqrt(features)
    factor = loss_gain * full_width / (16 * COUNT)
    entries = 2.0 * features * full_width

    plane = [(i, j) for i in range(SIDE) for j in range(SIDE) if i or j]
    barrier = pltpu.get_barrier_semaphore()
    for i, j in plane:
        pl.semaphore_signal(barrier, inc=1, device_id=at(y + i, x + j, t), device_id_type=MESH)
    for k in range(1, 16):
        pl.semaphore_signal(barrier, inc=1, device_id=along_t(k), device_id_type=MESH)

    some = pl.ds(pl.multiple_of(t * ROWS, ROWS), ROWS)
    left, right = pl.ds(0, WIDE), pl.ds(WIDE, WIDE)
    loads = [
        (tokens.at[some], tok16),
        (target.at[some], tgt16),
        (wq, gqk.at[y, :, left]),
        (wk, gqk.at[y, :, right]),
        (wv, gvt.at[x, :, left]),
        (bv, bvv),
        (tokens, tok),
        (wo, uall.at[t, :, pl.ds(0, BLOCK)]),
        (bo, bov),
        (near, nearv),
        (bias, biasv),
        (pv, pvv),
        (po, pov),
    ]
    loads = [pltpu.make_async_copy(a, b, ls.at[k]) for k, (a, b) in enumerate(loads)]
    for copy in loads:
        copy.start()

    loads[0].wait()
    loads[1].wait()
    xf = tok16[...].astype(F32)
    inv = lax.rsqrt(jnp.mean(xf * xf, axis=1, keepdims=True) + epsilon)
    for k in range(16):
        cut = slice(k * BLOCK, (k + 1) * BLOCK)
        part = tok16[:, cut].astype(F32)
        n16[k // SIDE, k % SIDE] = (part * inv).astype(BF)
        diff[k] = part - tgt16[:, cut].astype(F32)
    pl.semaphore_wait(barrier, 30)

    pieces, weights, others = [], [], []
    for j in NEAR:
        pieces.append(
            send(n16.at[:, (x + j) % SIDE], rows.at[j - 1, t], ps.at[j - 1], pr.at[j - 1], along_x(j))
        )
        pieces.append(
            send(n16.at[(y + j) % SIDE], rows.at[j + 2, t], ps.at[j + 2], pr.at[j + 2], along_y(j))
        )
    for k in (2, 3, 4, 5):
        loads[k].wait()
    gvt[x, :, WIDE:] = bvv[...].astype(BF)
    for j in NEAR:
        weights.append(send(gqk.at[y], gqk.at[y], ws.at[j - 1], wr.at[j - 1], along_y(j)))
        weights.append(send(gvt.at[x], gvt.at[x], ws.at[j + 2], wr.at[j + 2], along_x(j)))
    for k, (i, j) in enumerate(plane):
        yy, xx = (y + i) % SIDE, (x + j) % SIDE
        others.append(
            send(diff.at[yy * SIDE + xx], diffs.at[me], ds.at[k], dr.at[k], (yy * SIDE + xx, t))
        )
    diffs[me] = diff[me]

    ring = Ring(
        lambda n: rows.at[:, n], lambda n, way: rows.at[pl.ds(3 * way, 3), n], zs, zr, cs, cr
    )
    for copy in pieces:
        copy.wait_recv()
    ring.start()

    loads[6].wait()

    def normalise(r, _):
        at_r = pl.ds(pl.multiple_of(r * ROWS, ROWS), ROWS)
        xf = tok[at_r].astype(F32)
        inv = lax.rsqrt(jnp.mean(xf * xf, axis=1, keepdims=True) + epsilon)
        for b in range(SIDE):
            cut = pl.ds(pl.multiple_of((b * SIDE + x) * BLOCK, HALF), BLOCK)
            nx[b, at_r] = (tok[at_r, cut].astype(F32) * inv).astype(BF)
            cut = pl.ds(pl.multiple_of((y * SIDE + b) * BLOCK, HALF), BLOCK)
            ny[b, at_r] = (tok[at_r, cut].astype(F32) * inv).astype(BF)
        return 0

    lax.fori_loop(0, COUNT // ROWS, normalise, 0)
    ring.step(1)
    loads[7].wait()
    loads[8].wait()
    uall[t, :, BLOCK:] = bov[...].astype(BF)
    ring.step(2)
    ring.step(3)
    for copy in weights:
        copy.wait_recv()
    for lhs, w, acc in ((nx, gqk, accq), (ny, gvt, accv)):
        total = dot(lhs[0], w[0])
        for b in range(1, SIDE):
            total = total + dot(lhs[b], w[b])
        acc[...] = total
    uring = Ring(
        lambda n: uall.at[n], lambda n, way: uall.at[n, pl.ds(HALF * way, HALF)], us, ur, vs, vr
    )
    ring.finish()
    uring.start()
    ring.settle()

    partial = []
    for j in NEAR:
        for w, k, out, got, peer in (
            (gqk, j - 1, pq, rq, along_x(-j)),
            (gvt, j + 2, pt, rv, along_y(-j)),
        ):
            total = dot(rows[k, :, 0].reshape(COUNT, BLOCK), w[0])
            for b in range(1, SIDE):
                total = total + dot(rows[k, :, b].reshape(COUNT, BLOCK), w[b])
            out[j - 1] = total.astype(BF)
            partial.append(send(out.at[j - 1], got.at[j - 1], xs.at[k], xr.at[k], peer))
    for copy in partial:
        copy.wait_recv()

    def add_up(r, _):
        at_r = pl.ds(pl.multiple_of(r * 32, 32), 32)
        total = accq[at_r]
        for j in range(3):
            total = total + rq[j, at_r].astype(F32)
        qk[at_r] = total.astype(BF)
        total = accv[at_r]
        for j in range(3):
            total = total + rv[j, at_r].astype(F32)
        vt[at_r, :WIDE] = total[:, :WIDE].astype(BF)
        vt[at_r, WIDE:] = (total[:, WIDE:] / math.sqrt(features)).astype(BF)
        return 0

    lax.fori_loop(0, COUNT // 32, add_up, 0)
    uring.step(1)

    loads[9].wait()
    loads[10].wait()
    at_row = lax.broadcasted_iota(jnp.int32, (COUNT, COUNT), 0)
    at_col = lax.broadcasted_iota(jnp.int32, (COUNT, COUNT), 1)
    allowed = (nearv[...] == 1) | (jnp.abs(at_row - at_col) <= 1)
    for h in range(2):
        cut = slice(h * HALF, (h + 1) * HALF)
        cut2 = slice(WIDE + h * HALF, WIDE + (h + 1) * HALF)
        scores = dot_t(qk[:, cut], qk[:, cut2]) / math.sqrt(HEAD_DIM) + biasv[h]
        scores = jnp.where(allowed, scores, -jnp.inf)
        e = jnp.exp(scores - jnp.max(scores, axis=1, keepdims=True))
        p = (e / jnp.sum(e, axis=1, keepdims=True)).astype(BF)
        probs[h] = p
        mix[:, cut] = dot(p, vt[:, cut]).astype(BF)
        mix[:, cut2] = dot(p, vt[:, cut2]).astype(BF)

    moved = []
    for k in range(1, 16):
        to = pl.ds(pl.multiple_of(((t + k) % 16) * ROWS, ROWS), ROWS)
        moved.append(send(mix.at[to], full.at[y, x, t], ts.at[k], tr.at[k], along_t(k)))
    full[y, x, t] = mix[some]
    for copy in moved:
        copy.wait_recv()
    low, high = pl.ds(0, 8), pl.ds(8, 8)
    first, second = [], []
    a, b = full.at[y, x, low], full.at[y, x, high]
    for j in NEAR:
        first.append(send(a, a, as_.at[0, j - 1], ar.at[0, j - 1], along_x(j)))
        first.append(send(b, b, bs.at[0, j - 1], br.at[0, j - 1], along_y(j)))
    for j in NEAR:
        second.append(send(a, a, as_.at[1, j - 1], ar.at[1, j - 1], along_y(j)))
        second.append(send(b, b, bs.at[1, j - 1], br.at[1, j - 1], along_x(j)))
    uring.step(2)
    for k, i in enumerate(NEAR):
        first[2 * k].wait_recv()
        first[2 * k + 1].wait_recv()
        a = full.at[y, (x - i + SIDE) % SIDE, low]
        b = full.at[(y - i + SIDE) % SIDE, x, high]
        for j in NEAR:
            second.append(send(a, a, as_.at[1 + i, j - 1], ar.at[1 + i, j - 1], along_y(j)))
            second.append(send(b, b, bs.at[1 + i, j - 1], br.at[1 + i, j - 1], along_x(j)))
    uring.step(3)
    uring.finish()
    uring.settle()
    for copy in second:
        copy.wait_recv()

    acc1[...] = jnp.zeros_like(acc1)
    acc2[...] = jnp.zeros_like(acc2)

    def forward(n, _):
        both = full[:, :, n].reshape(COUNT, 2 * WIDE)
        acc1[...] += dot(both[:, :WIDE], uall[n])
        acc2[...] += dot(both[:, WIDE:], uall[n, :, :BLOCK])
        return 0

    lax.fori_loop(0, 16, forward, 0)
    for copy in others:
        copy.wait_recv()
    err[...] = ((diffs[...].reshape(COUNT, BLOCK) + acc1[:, :BLOCK]) * factor).astype(BF)
    terr[...] = ((acc1[:, BLOCK:] * scale_out + acc2[...]) * factor).astype(BF)

    def backward(n, _):
        part = dot_t(terr[...], uall[n, :, :BLOCK]) + scale_out * dot_t(err[...], uall[n, :, BLOCK:])
        bp[n] = part.astype(BF).reshape(SIDE, SIDE, ROWS, WIDE)
        return 0

    lax.fori_loop(0, 16, backward, 0)
    first_b = []
    for j in NEAR:
        first_b.append(
            send(bp.at[low, (y + j) % SIDE], ra.at[j - 1], s1.at[0, j - 1], r1.at[0, j - 1], along_y(j))
        )
        first_b.append(
            send(bp.at[high, :, (x + j) % SIDE], rb.at[j - 1], s1.at[1, j - 1], r1.at[1, j - 1], along_x(j))
        )

    errt[...] = err[...].astype(F32).T.astype(BF)
    terrt[...] = terr[...].astype(F32).T.astype(BF)

    def outer(n, _):
        both = full[:, :, n].reshape(COUNT, 2 * WIDE)
        part = dot(errt[...], both[:, WIDE:]) + dot(terrt[...], both[:, :WIDE])
        co[n // 2, n % 2] = (part * scale_out).astype(BF)
        return 0

    lax.fori_loop(0, 16, outer, 0)
    swapped = send(co.at[:, 1 - c], rc, s7.at[0], r7.at[0], other_core())

    for copy in first_b:
        copy.wait_recv()
    for i in range(SIDE):
        total = bp[0:8, y, i].astype(F32)
        for j in range(3):
            total = total + ra[j, :, i].astype(F32)
        sa[i] = total.astype(BF)
        total = bp[8:16, i, x].astype(F32)
        for j in range(3):
            total = total + rb[j, :, i].astype(F32)
        sb[i] = total.astype(BF)
    second_b = []
    for j in NEAR:
        second_b.append(
            send(sa.at[(x + j) % SIDE], qa.at[j - 1], s2.at[0, j - 1], r2.at[0, j - 1], along_x(j))
        )
        second_b.append(
            send(sb.at[(y + j) % SIDE], qb.at[j - 1], s2.at[1, j - 1], r2.at[1, j - 1], along_y(j))
        )
    for copy in second_b:
        copy.wait_recv()
    total = sa[x].astype(F32)
    for j in range(3):
        total = total + qa[j].astype(F32)
    done[0:8] = total.astype(BF)
    total = sb[y].astype(F32)
    for j in range(3):
        total = total + qb[j].astype(F32)
    done[8:16] = total.astype(BF)
    third = []
    for k in range(1, 16):
        third.append(send(done.at[(t + k) % 16], bt.at[t], s3.at[k], r3.at[k], along_t(k)))
    bt[t] = done[t]

    swapped.wait_recv()

    def pair(k, _):
        sc[k] = (co[k, c].astype(F32) + rc[k].astype(F32)).astype(BF)
        return 0

    lax.fori_loop(0, 8, pair, 0)
    shares = []
    for k in (1, 7, 2, 6, 3, 5, 4):
        shares.append(send(sc.at[(z + k) % 8], rz.at[k - 1], s4.at[k], r4.at[k], along_z(k)))

    for copy in third:
        copy.wait_recv()
    back = bt[...].reshape(COUNT, WIDE).astype(F32).T.astype(BF)
    fourth = []
    for h in range(2):
        vb[h] = dot(back[h * HALF : (h + 1) * HALF], probs[h]).astype(BF)
        got, along = ((gx, along_x), (gy, along_y))[h]
        for j in NEAR:
            fourth.append(
                send(vb.at[h], got.at[j - 1], s5.at[h, j - 1], r5.at[h, j - 1], along(j))
            )
    for copy in fourth:
        copy.wait_recv()
    for b in range(SIDE):
        for h, own, got, outf, outb in ((0, nx, gx, cxf, cxb), (1, ny, gy, cyf, cyb)):
            total = dot(vb[h], own[b])
            for j in range(3):
                total = total + dot(got[j], rows[3 * h + j, :, b].reshape(COUNT, BLOCK))
            total = total * scale_value
            outf[b] = total
            outb[b] = total.astype(BF)
    fifth = []
    for j in NEAR:
        fifth.append(
            send(cxb.at[(y + j) % SIDE], hx.at[j - 1], s6.at[0, j - 1], r6.at[0, j - 1], along_y(j))
        )
        fifth.append(
            send(cyb.at[(x + j) % SIDE], hy.at[j - 1], s6.at[1, j - 1], r6.at[1, j - 1], along_x(j))
        )
    for copy in shares:
        copy.wait_recv()
    total = sc[z].astype(F32)
    for j in range(7):
        total = total + rz[j].astype(F32)
    cw[...] = total.T
    loads[11].wait()
    loads[12].wait()
    for copy in fifth:
        copy.wait_recv()
    for h, (own, got, mine) in enumerate(((cxf, hx, y), (cyf, hy, x))):
        total = own[mine]
        for j in range(3):
            total = total + got[j].astype(F32)
        cv[:, h * HALF : (h + 1) * HALF] = total.T

    def everywhere(value, turn):
        one[turn, t] = jnp.full((8, 128), value, F32)
        copies = []
        for k in range(1, 16):
            part = one.at[turn, t]
            copies.append(send(part, part, o1.at[turn, k], i1.at[turn, k], along_t(k)))
        for copy in copies:
            copy.wait()
        two[turn, me] = jnp.sum(one[turn], axis=0)
        copies = []
        for k, (i, j) in enumerate(plane):
            part = two.at[turn, me]
            copies.append(
                send(part, part, o2.at[turn, k], i2.at[turn, k], at(y + i, x + j, t))
            )
        for copy in copies:
            copy.wait()
        return jnp.sum(two[turn], axis=0)[0:1, 0:1] / entries

    beta_before = pb[0, 0]
    alpha = everywhere(jnp.sum(bvv[...] * cv[...]) + jnp.sum(bov[...] * cw[...]), 0)
    nv[...] = cv[...] - alpha * bvv[...] - beta_before * pvv[...]
    no[...] = cw[...] - alpha * bov[...] - beta_before * pov[...]
    squares = everywhere(jnp.sum(nv[...] * nv[...]) + jnp.sum(no[...] * no[...]), 1)
    beta = jnp.sqrt(squares + epsilon)
    nv[...] = nv[...] / beta
    no[...] = no[...] / beta
    coef[0:1] = jnp.broadcast_to(alpha, (1, 128))
    coef[1:2] = jnp.broadcast_to(beta, (1, 128))
    for copy in (
        pieces + weights + others + partial + moved + first + second + first_b + second_b
        + third + [swapped] + shares + fourth + fifth
    ):
        copy.wait_send()


def body(
    tokens,
    target,
    pair_bias,
    neighbours,
    w_query,
    w_key,
    w_value,
    w_out,
    basis_value,
    basis_out,
    prior_value,
    prior_out,
    prior_beta,
):
    def vm(dtype, *dims):
        return pltpu.VMEM(dims, dtype)

    features = 16 * BLOCK
    scratch = [
        vm(BF, ROWS, features),
        vm(BF, ROWS, features),
        vm(BF, COUNT, features),
        vm(BF, SIDE, SIDE, ROWS, BLOCK),
        vm(F32, 16, ROWS, BLOCK),
        vm(F32, 16, ROWS, BLOCK),
        vm(BF, 6, 16, SIDE, ROWS, BLOCK),
        vm(BF, SIDE, BLOCK, 2 * WIDE),
        vm(BF, SIDE, BLOCK, 2 * WIDE),
        vm(BF, SIDE, COUNT, BLOCK),
        vm(BF, SIDE, COUNT, BLOCK),
        vm(BF, 16, WIDE, 2 * BLOCK),
        vm(F32, BLOCK, WIDE),
        vm(F32, WIDE, BLOCK),
        vm(F32, BLOCK, WIDE),
        vm(F32, WIDE, BLOCK),
        vm(jnp.int32, COUNT, COUNT),
        vm(F32, 2, COUNT, COUNT),
        vm(BF, 3, COUNT, 2 * WIDE),
        vm(BF, 3, COUNT, 2 * WIDE),
        vm(BF, 3, COUNT, 2 * WIDE),
        vm(BF, 3, COUNT, 2 * WIDE),
        vm(F32, COUNT, 2 * WIDE),
        vm(F32, COUNT, 2 * WIDE),
        vm(BF, COUNT, 2 * WIDE),
        vm(BF, COUNT, 2 * WIDE),
        vm(BF, 2, COUNT, COUNT),
        vm(BF, COUNT, 2 * WIDE),
        vm(BF, SIDE, SIDE, 16, ROWS, 2 * WIDE),
        vm(F32, COUNT, 2 * BLOCK),
        vm(F32, COUNT, BLOCK),
        vm(BF, COUNT, BLOCK),
        vm(BF, COUNT, BLOCK),
        vm(BF, BLOCK, COUNT),
        vm(BF, BLOCK, COUNT),
        vm(BF, 16, SIDE, SIDE, ROWS, WIDE),
        vm(BF, 3, 8, SIDE, ROWS, WIDE),
        vm(BF, 3, 8, SIDE, ROWS, WIDE),
        vm(BF, SIDE, 8, ROWS, WIDE),
        vm(BF, SIDE, 8, ROWS, WIDE),
        vm(BF, 3, 8, ROWS, WIDE),
        vm(BF, 3, 8, ROWS, WIDE),
        vm(BF, 16, ROWS, WIDE),
        vm(BF, 16, ROWS, WIDE),
        vm(BF, 8, 2, BLOCK, WIDE),
        vm(BF, 8, BLOCK, WIDE),
        vm(BF, 8, BLOCK, WIDE),
        vm(BF, 7, BLOCK, WIDE),
        vm(BF, 2, HALF, COUNT),
        vm(BF, 3, HALF, COUNT),
        vm(BF, 3, HALF, COUNT),
        vm(F32, SIDE, HALF, BLOCK),
        vm(F32, SIDE, HALF, BLOCK),
        vm(BF, SIDE, HALF, BLOCK),
        vm(BF, SIDE, HALF, BLOCK),
        vm(BF, 3, HALF, BLOCK),
        vm(BF, 3, HALF, BLOCK),
        vm(F32, BLOCK, WIDE),
        vm(F32, WIDE, BLOCK),
        vm(F32, 2, 16, 8, 128),
        vm(F32, 2, 16, 8, 128),
        DMA((13,)),
        DMA((6,)), DMA((6,)),
        DMA((6,)), DMA((6,)),
        DMA((15,)), DMA((15,)),
        DMA((2, 4)), DMA((2, 4)), DMA((8,)), DMA((8,)),
        DMA((2, 4)), DMA((2, 4)), DMA((8,)), DMA((8,)),
        DMA((6,)), DMA((6,)),
        DMA((16,)), DMA((16,)),
        DMA((5, 3)), DMA((5, 3)), DMA((5, 3)), DMA((5, 3)),
        DMA((2, 3)), DMA((2, 3)),
        DMA((2, 3)), DMA((2, 3)),
        DMA((16,)), DMA((16,)),
        DMA((8,)), DMA((8,)),
        DMA((2, 3)), DMA((2, 3)),
        DMA((2, 3)), DMA((2, 3)),
        DMA((1,)), DMA((1,)),
        DMA((2, 16)), DMA((2, 16)), DMA((2, 15)), DMA((2, 15)),
    ]
    next_value, next_out, coef = pl.pallas_call(
        step_kernel,
        out_shape=(
            jax.ShapeDtypeStruct((BLOCK, WIDE), F32),
            jax.ShapeDtypeStruct((WIDE, BLOCK), F32),
            jax.ShapeDtypeStruct((8, 128), F32),
        ),
        in_specs=[ANY] * 12 + [SMEM],
        out_specs=(VMEM, VMEM, VMEM),
        scratch_shapes=scratch,
        compiler_params=pltpu.CompilerParams(
            collective_id=0, has_side_effects=True, vmem_limit_bytes=58 * 2**20
        ),
    )(
        tokens,
        target,
        pair_bias.transpose(1, 0, 2),
        neighbours,
        w_query,
        w_key,
        w_value,
        w_out,
        basis_value,
        basis_out,
        prior_value,
        prior_out,
        prior_beta.reshape(1, 1),
    )
    return next_value, next_out, coef[:2, 0]


def solution(mesh):
    placed = (
        P("dp", None),
        P("dp", None),
        P("dp", "tensor", None),
        P("dp", None),
        P("dp", "tensor"),
        P("dp", "tensor"),
        P("dp", "tensor"),
        P("tensor", "dp"),
        P("dp", "tensor"),
        P("tensor", "dp"),
        P("dp", "tensor"),
        P("tensor", "dp"),
        P(),
    )
    return jax.shard_map(
        body,
        mesh=mesh,
        in_specs=placed,
        out_specs=(P("dp", "tensor"), P("tensor", "dp"), P()),
        check_vma=False,
    )
```

```python
import math

import jax
import jax.numpy as jnp
from jax import lax
from jax.experimental import pallas as pl
from jax.experimental.pallas import tpu as pltpu
from jax.sharding import PartitionSpec as P

HEAD_DIM = 128
SIDE = 4
ROWS = 16

loss_gain = 32.0
epsilon = 1e-06

MESH = pl.DeviceIdType.MESH
BF = jnp.bfloat16
F32 = jnp.float32
VMEM = pl.BlockSpec(memory_space=pltpu.VMEM)
ANY = pl.BlockSpec(memory_space=pl.ANY)
SMEM = pl.BlockSpec(memory_space=pltpu.SMEM)
DMA = pltpu.SemaphoreType.DMA


def coords():
    dp = lax.axis_index("dp")
    t = lax.axis_index("tensor")
    return dp // SIDE, dp % SIDE, t


def at(y, x, t):
    return (((y + 2 * SIDE) % SIDE) * SIDE + (x + 2 * SIDE) % SIDE, (t + 32) % 16)


def along_x(j):
    y, x, t = coords()
    return at(y, x + j, t)


def along_y(j):
    y, x, t = coords()
    return at(y + j, x, t)


def along_t(k):
    y, x, t = coords()
    return at(y, x, t + k)


def along_z(k):
    y, x, t = coords()
    return at(y, x, t + 2 * k)


def other_core():
    y, x, t = coords()
    return at(y, x, t + 1 - 2 * (t % 2))


def greet(peers):
    barrier = pltpu.get_barrier_semaphore()
    for peer in peers:
        pl.semaphore_signal(barrier, inc=1, device_id=peer, device_id_type=MESH)
    pl.semaphore_wait(barrier, len(peers))


def send(src, dst, ssem, rsem, peer):
    copy = pltpu.make_async_remote_copy(
        src_ref=src,
        dst_ref=dst,
        send_sem=ssem,
        recv_sem=rsem,
        device_id=peer,
        device_id_type=MESH,
    )
    copy.start()
    return copy


NEAR = (1, 3, 2)
WIDE = 256
HALF = 128
BLOCK = 384
COUNT = 256


def dot(a, b):
    return jnp.dot(a, b, preferred_element_type=F32)


def dot_t(a, b):
    return lax.dot_general(a, b, (((1,), (1,)), ((), ())), preferred_element_type=F32)


def arrival(ref, ssem, rsem):
    y, x, t = coords()
    return pltpu.make_async_remote_copy(
        src_ref=ref,
        dst_ref=ref,
        send_sem=ssem,
        recv_sem=rsem,
        device_id=at(y, x, t + 2),
        device_id_type=MESH,
    )


class Ring:
    def __init__(self, slot, half, zs, zr, cs, cr):
        self.slot, self.half = slot, half
        self.zs, self.zr, self.cs, self.cr = zs, zr, cs, cr
        self.sent = []

    def start(self):
        y, x, t = coords()
        own = self.slot(t)
        for way in range(2):
            self.sent.append(
                send(own, own, self.zs.at[way, 0], self.zr.at[way, 0], along_z(1 - 2 * way))
            )
        self.sent.append(send(own, own, self.cs.at[0], self.cr.at[0], other_core()))

    def step(self, step):
        y, x, t = coords()
        for way in range(2):
            sign = 1 - 2 * way
            slot = (t - 2 * sign * step + 32) % 16
            got = self.slot(slot)
            arrival(got, self.zs.at[way, step - 1], self.zr.at[way, step - 1]).wait_recv()
            part = got if step < 3 else self.half(slot, way)
            self.sent.append(
                send(part, part, self.zs.at[way, step], self.zr.at[way, step], along_z(sign))
            )
            k = 2 * step - 1 + way
            self.sent.append(send(got, got, self.cs.at[k], self.cr.at[k], other_core()))

    def finish(self):
        y, x, t = coords()
        far = (t + 8) % 16
        for way in range(2):
            part = self.half(far, way)
            arrival(part, self.zs.at[way, 3], self.zr.at[way, 3]).wait_recv()
        got = self.slot(far)
        self.sent.append(send(got, got, self.cs.at[7], self.cr.at[7], other_core()))

    def cores(self, some):
        y, x, t = coords()
        for k in some:
            step, way = (k + 1) // 2, (k + 1) % 2
            shift = 8 if k == 7 else 2 * step * (1 - 2 * way)
            got = self.slot((t + 1 - 2 * (t % 2) - shift + 32) % 16)
            arrival(got, self.cs.at[k], self.cr.at[k]).wait_recv()

    def settle(self):
        for copy in self.sent:
            copy.wait_send()


class Sweep:
    OFFSETS = (0, -1, 1, 2)

    def __init__(self, part, full, sp, rp, ss, rs):
        y, x, t = coords()
        self.sent = []
        self.sp, self.rp, self.ss, self.rs = sp, rp, ss, rs
        self.first, self.then = (along_x, along_y) if part == 0 else (along_y, along_x)
        self.base = 8 * part

        def block(p, s, half=None):
            rng = pl.ds(self.base, 8) if half is None else pl.ds(self.base + 4 * half, 4)
            dy, dx = (s, p) if part == 0 else (p, s)
            return full.at[(y + dy + SIDE) % SIDE, (x + dx + SIDE) % SIDE, rng]

        self.block = block

    def push(self, ref, ssem, rsem, peer):
        self.sent.append(send(ref, ref, ssem, rsem, peer))

    def start(self):
        own = self.block(0, 0)
        for k in range(2):
            self.push(own, self.sp.at[k], self.rp.at[k], self.first(1 - 2 * k))

    def across(self, q):
        own = self.block(self.OFFSETS[q], 0)
        for k in range(2):
            self.push(own, self.ss.at[q, k], self.rs.at[q, k], self.then(1 - 2 * k))

    def relay(self):
        for k in range(2):
            off = 2 * k - 1
            arrival(self.block(off, 0), self.sp.at[k], self.rp.at[k]).wait_recv()
            half = self.block(off, 0, k)
            self.push(half, self.sp.at[2 + k], self.rp.at[2 + k], self.first(1 - 2 * k))

    def relay_across(self, q):
        p = self.OFFSETS[q]
        for k in range(2):
            off = 2 * k - 1
            arrival(self.block(p, off), self.ss.at[q, k], self.rs.at[q, k]).wait_recv()
            half = self.block(p, off, k)
            self.push(half, self.ss.at[q, 2 + k], self.rs.at[q, 2 + k], self.then(1 - 2 * k))

    def far(self):
        for k in range(2):
            arrival(self.block(2, 0, k), self.sp.at[2 + k], self.rp.at[2 + k]).wait_recv()

    def last(self):
        for q in range(4):
            for k in range(2):
                arrival(
                    self.block(self.OFFSETS[q], 2, k), self.ss.at[q, 2 + k], self.rs.at[q, 2 + k]
                ).wait_recv()


def step_kernel(
    tokens, target, bias, near, wq, wk, wv, wo, bv, bo, pv, po, pb,
    nv, no, coef,
    tok16, tgt16, tok, n16, diff, diffs, rows, gqk, gvt, nx, ny, uall,
    bvv, bov, pvv, pov, nearv, biasv,
    pq, pt, rq, rv, accq, accv, qk, vt, probs, mix, full,
    acc1, acc2, err, terr, errt, terrt, bp, ra, rb, sa, sb, qa, qb, done, bt,
    co, rc, sc, rz, tx, vb, gx, gy, cxf, cyf, cxb, cyb, hx, hy, cv, cw, one, two,
    ls, ps, pr, ws, wr, ds, dr, zs, zr, cs, cr, us, ur, vs, vr, xs, xr, ts, tr,
    as_, ar, bs, br, s1, r1, s2, r2, s3, r3, s4, r4, s5, r5, s6, r6, s7, r7, o1, i1, o2, i2,
):
    y, x, t = coords()
    c = t % 2
    z = t // 2
    me = y * SIDE + x
    full_width = 16 * WIDE
    features = 16 * BLOCK
    scale_out = 1.0 / math.sqrt(full_width)
    scale_value = 1.0 / math.sqrt(features)
    factor = loss_gain * full_width / (16 * COUNT)
    entries = 2.0 * features * full_width

    plane = [(i, j) for i in range(SIDE) for j in range(SIDE) if i or j]
    barrier = pltpu.get_barrier_semaphore()
    for i, j in plane:
        pl.semaphore_signal(barrier, inc=1, device_id=at(y + i, x + j, t), device_id_type=MESH)
    for k in range(1, 16):
        pl.semaphore_signal(barrier, inc=1, device_id=along_t(k), device_id_type=MESH)

    some = pl.ds(pl.multiple_of(t * ROWS, ROWS), ROWS)
    left, right = pl.ds(0, WIDE), pl.ds(WIDE, WIDE)
    loads = [
        (tokens.at[some], tok16),
        (target.at[some], tgt16),
        (wq, gqk.at[y, :, left]),
        (wk, gqk.at[y, :, right]),
        (wv, gvt.at[x, :, left]),
        (bv, bvv),
        (tokens, tok),
        (wo, uall.at[t, :, pl.ds(0, BLOCK)]),
        (bo, bov),
        (near, nearv),
        (bias.at[:, 0], biasv.at[0]),
        (bias.at[:, 1], biasv.at[1]),
        (pv, pvv),
        (po, pov),
    ]
    loads = [pltpu.make_async_copy(a, b, ls.at[k]) for k, (a, b) in enumerate(loads)]
    for copy in loads[:2]:
        copy.start()
    for copy in loads[2:]:
        copy.start()

    loads[0].wait()
    loads[1].wait()
    xf = tok16[...].astype(F32)
    inv = lax.rsqrt(jnp.mean(xf * xf, axis=1, keepdims=True) + epsilon)
    for k in range(16):
        cut = slice(k * BLOCK, (k + 1) * BLOCK)
        part = tok16[:, cut].astype(F32)
        n16[k // SIDE, k % SIDE] = (part * inv).astype(BF)
        diff[k] = part - tgt16[:, cut].astype(F32)
    pl.semaphore_wait(barrier, 30)

    pieces, weights, others = [], [], []
    for j in NEAR:
        pieces.append(
            send(n16.at[:, (x + j) % SIDE], rows.at[j - 1, t], ps.at[j - 1], pr.at[j - 1], along_x(j))
        )
        pieces.append(
            send(n16.at[(y + j) % SIDE], rows.at[j + 2, t], ps.at[j + 2], pr.at[j + 2], along_y(j))
        )
    for k in (2, 3, 4, 5):
        loads[k].wait()
    gvt[x, :, WIDE:] = bvv[...].astype(BF)
    for j in NEAR:
        weights.append(send(gqk.at[y], gqk.at[y], ws.at[j - 1], wr.at[j - 1], along_y(j)))
        weights.append(send(gvt.at[x], gvt.at[x], ws.at[j + 2], wr.at[j + 2], along_x(j)))
    for k, (i, j) in enumerate(plane):
        yy, xx = (y + i) % SIDE, (x + j) % SIDE
        others.append(
            send(diff.at[yy * SIDE + xx], diffs.at[me], ds.at[k], dr.at[k], (yy * SIDE + xx, t))
        )
    diffs[me] = diff[me]

    ring = Ring(
        lambda n: rows.at[:, n], lambda n, way: rows.at[pl.ds(3 * way, 3), n], zs, zr, cs, cr
    )
    for copy in pieces:
        copy.wait_recv()
    ring.start()

    loads[6].wait()

    def normalise(r, _):
        at_r = pl.ds(pl.multiple_of(r * ROWS, ROWS), ROWS)
        xf = tok[at_r].astype(F32)
        inv = lax.rsqrt(jnp.mean(xf * xf, axis=1, keepdims=True) + epsilon)
        for b in range(SIDE):
            cut = pl.ds(pl.multiple_of((b * SIDE + x) * BLOCK, HALF), BLOCK)
            nx[b, at_r] = (tok[at_r, cut].astype(F32) * inv).astype(BF)
            cut = pl.ds(pl.multiple_of((y * SIDE + b) * BLOCK, HALF), BLOCK)
            ny[b, at_r] = (tok[at_r, cut].astype(F32) * inv).astype(BF)
        return 0

    lax.fori_loop(0, COUNT // ROWS, normalise, 0)
    ring.step(1)
    loads[7].wait()
    loads[8].wait()
    uall[t, :, BLOCK:] = bov[...].astype(BF)
    ring.step(2)
    for copy in weights:
        copy.wait_recv()
    for lhs, w, acc in ((nx, gqk, accq), (ny, gvt, accv)):
        total = dot(lhs[0], w[0])
        for b in range(1, SIDE):
            total = total + dot(lhs[b], w[b])
        acc[...] = total
    ring.step(3)

    order = []
    for off in (0, -1, 1, -2, 2, -3, 3, 4):
        base = ((z + off + 8) % 8) * 2
        order += [base + c, base + 1 - c]
    partial = []

    def products(part, lo, hi):
        for w, k0, out, got, along in ((gqk, 0, pq, rq, along_x), (gvt, 3, pt, rv, along_y)):
            total = None
            for b in range(SIDE):
                lhs = jnp.concatenate(
                    [rows[k0 + j, n, b] for j in range(3) for n in order[lo:hi]], axis=0
                )
                more = dot(lhs, w[b])
                total = more if total is None else total + more
            size = (hi - lo) * ROWS
            for j in range(3):
                out[j, lo * ROWS : hi * ROWS] = total[j * size : (j + 1) * size].astype(BF)
            cut = pl.ds(lo * ROWS, size)
            for j in NEAR:
                sem = (part, k0 + j - 1)
                partial.append(
                    send(out.at[j - 1, cut], got.at[j - 1, cut], xs.at[sem], xr.at[sem], along(-j))
                )

    ring.cores(range(5))
    products(0, 0, 10)
    uring = Ring(
        lambda n: uall.at[n], lambda n, way: uall.at[n, pl.ds(HALF * way, HALF)], us, ur, vs, vr
    )
    ring.finish()
    uring.start()
    ring.cores(range(5, 8))
    products(1, 10, 16)
    uring.step(1)
    for copy in partial:
        copy.wait_recv()

    for p, n in enumerate(order):
        at_n = pl.ds(pl.multiple_of(n * ROWS, ROWS), ROWS)
        at_p = slice(p * ROWS, (p + 1) * ROWS)
        total = accq[at_n]
        for j in range(3):
            total = total + rq[j, at_p].astype(F32)
        qk[at_n] = total.astype(BF)
        total = accv[at_n]
        for j in range(3):
            total = total + rv[j, at_p].astype(F32)
        vt[at_n, :WIDE] = total[:, :WIDE].astype(BF)
        vt[at_n, WIDE:] = (total[:, WIDE:] / math.sqrt(features)).astype(BF)

    loads[9].wait()
    loads[10].wait()
    loads[11].wait()
    at_row = lax.broadcasted_iota(jnp.int32, (COUNT, COUNT), 0)
    at_col = lax.broadcasted_iota(jnp.int32, (COUNT, COUNT), 1)
    allowed = (nearv[...] == 1) | (jnp.abs(at_row - at_col) <= 1)
    for h in range(2):
        cut = slice(h * HALF, (h + 1) * HALF)
        cut2 = slice(WIDE + h * HALF, WIDE + (h + 1) * HALF)
        scores = dot_t(qk[:, cut], qk[:, cut2]) / math.sqrt(HEAD_DIM) + biasv[h]
        scores = jnp.where(allowed, scores, -jnp.inf)
        e = jnp.exp(scores - jnp.max(scores, axis=1, keepdims=True))
        p = (e / jnp.sum(e, axis=1, keepdims=True)).astype(BF)
        probs[h] = p
        mix[:, cut] = dot(p, vt[:, cut]).astype(BF)
        mix[:, cut2] = dot(p, vt[:, cut2]).astype(BF)

    moved = []
    for k in range(1, 16):
        to = pl.ds(pl.multiple_of(((t + k) % 16) * ROWS, ROWS), ROWS)
        moved.append(send(mix.at[to], full.at[y, x, t], ts.at[k], tr.at[k], along_t(k)))
    full[y, x, t] = mix[some]
    uring.step(2)
    for copy in moved:
        copy.wait_recv()
    sweeps = [
        Sweep(0, full, as_.at[0], ar.at[0], bs.at[0], br.at[0]),
        Sweep(1, full, as_.at[1], ar.at[1], bs.at[1], br.at[1]),
    ]
    for sweep in sweeps:
        sweep.start()
    for sweep in sweeps:
        sweep.across(0)
    for sweep in sweeps:
        sweep.relay()
    for sweep in sweeps:
        sweep.across(1)
        sweep.across(2)
    uring.step(3)
    for sweep in sweeps:
        sweep.relay_across(0)
    for sweep in sweeps:
        sweep.far()
        sweep.across(3)
    uring.finish()
    for q in (1, 2, 3):
        for sweep in sweeps:
            sweep.relay_across(q)
    uring.cores(range(8))
    for sweep in sweeps:
        sweep.last()

    acc1[...] = jnp.zeros_like(acc1)
    acc2[...] = jnp.zeros_like(acc2)

    def forward(k, _):
        at_k = pl.ds(k * 4, 4)
        parts = [full[:, :, k * 4 + i].reshape(COUNT, 2 * WIDE) for i in range(4)]
        w = uall[at_k].reshape(4 * WIDE, 2 * BLOCK)
        acc1[...] += dot(jnp.concatenate([p[:, :WIDE] for p in parts], axis=1), w)
        acc2[...] += dot(jnp.concatenate([p[:, WIDE:] for p in parts], axis=1), w[:, :BLOCK])
        return 0

    lax.fori_loop(0, 4, forward, 0)
    for copy in others:
        copy.wait_recv()
    err[...] = ((diffs[...].reshape(COUNT, BLOCK) + acc1[:, :BLOCK]) * factor).astype(BF)
    terr[...] = ((acc1[:, BLOCK:] * scale_out + acc2[...]) * factor).astype(BF)

    def backward(n, _):
        part = dot_t(terr[...], uall[n, :, :BLOCK]) + scale_out * dot_t(err[...], uall[n, :, BLOCK:])
        bp[n] = part.astype(BF).reshape(SIDE, SIDE, ROWS, WIDE)
        return 0

    low, high = pl.ds(0, 8), pl.ds(8, 8)
    first_b = []
    lax.fori_loop(0, 8, backward, 0)
    for j in NEAR:
        src = bp.at[low, (y + j) % SIDE]
        first_b.append(send(src, ra.at[j - 1], s1.at[0, j - 1], r1.at[0, j - 1], along_y(j)))
    lax.fori_loop(8, 16, backward, 0)
    for j in NEAR:
        src = bp.at[high, :, (x + j) % SIDE]
        first_b.append(send(src, rb.at[j - 1], s1.at[1, j - 1], r1.at[1, j - 1], along_x(j)))

    errt[...] = err[...].astype(F32).T.astype(BF)
    terrt[...] = terr[...].astype(F32).T.astype(BF)

    def outer(n, _):
        both = full[:, :, n].reshape(COUNT, 2 * WIDE)
        part = dot(errt[...], both[:, WIDE:]) + dot(terrt[...], both[:, :WIDE])
        co[n // 2, n % 2] = (part * scale_out).astype(BF)
        return 0

    lax.fori_loop(0, 16, outer, 0)
    swapped = send(co.at[:, 1 - c], rc, s7.at[0], r7.at[0], other_core())

    for copy in first_b:
        copy.wait_recv()
    for i in range(SIDE):
        total = bp[0:8, y, i].astype(F32)
        for j in range(3):
            total = total + ra[j, :, i].astype(F32)
        sa[i] = total.astype(BF)
        total = bp[8:16, i, x].astype(F32)
        for j in range(3):
            total = total + rb[j, :, i].astype(F32)
        sb[i] = total.astype(BF)
    second_b = []
    for j in NEAR:
        second_b.append(
            send(sa.at[(x + j) % SIDE], qa.at[j - 1], s2.at[0, j - 1], r2.at[0, j - 1], along_x(j))
        )
        second_b.append(
            send(sb.at[(y + j) % SIDE], qb.at[j - 1], s2.at[1, j - 1], r2.at[1, j - 1], along_y(j))
        )

    swapped.wait_recv()

    def pair(k, _):
        sc[k] = (co[k, c].astype(F32) + rc[k].astype(F32)).astype(BF)
        return 0

    lax.fori_loop(0, 8, pair, 0)
    shares = []

    def pass_on(step):
        for way in range(2):
            sign = 1 - 2 * way
            slot = (z + sign * (4 - step) + 8) % 8
            if step == 0:
                cut = pl.ds(way * (BLOCK // 2), BLOCK // 2)
                src, dst = sc.at[slot, cut], rz.at[way, 0, cut]
            else:
                shares[2 * (step - 1) + way].wait_recv()
                if step == 1:
                    a, b = way * (BLOCK // 2), (way + 1) * (BLOCK // 2)
                    tx[way, 0] = sc[slot]
                    total = sc[slot, a:b].astype(F32) + rz[way, 0, a:b].astype(F32)
                    tx[way, 0, a:b] = total.astype(BF)
                else:
                    total = sc[slot].astype(F32) + rz[way, step - 1].astype(F32)
                    tx[way, step - 1] = total.astype(BF)
                src, dst = tx.at[way, step - 1], rz.at[way, step]
            shares.append(
                send(src, dst, s4.at[way, step], r4.at[way, step], along_z(sign))
            )

    pass_on(0)
    for copy in second_b:
        copy.wait_recv()
    total = sa[x].astype(F32)
    for j in range(3):
        total = total + qa[j].astype(F32)
    done[0:8] = total.astype(BF)
    total = sb[y].astype(F32)
    for j in range(3):
        total = total + qb[j].astype(F32)
    done[8:16] = total.astype(BF)
    third = []
    for k in range(1, 16):
        third.append(send(done.at[(t + k) % 16], bt.at[t], s3.at[k], r3.at[k], along_t(k)))
    bt[t] = done[t]

    pass_on(1)
    for copy in third:
        copy.wait_recv()
    back = bt[...].reshape(COUNT, WIDE).astype(F32).T.astype(BF)
    fourth = []
    for h in range(2):
        vb[h] = dot(back[h * HALF : (h + 1) * HALF], probs[h]).astype(BF)
        got, along = ((gx, along_x), (gy, along_y))[h]
        for j in NEAR:
            fourth.append(
                send(vb.at[h], got.at[j - 1], s5.at[h, j - 1], r5.at[h, j - 1], along(j))
            )
    pass_on(2)
    for copy in fourth:
        copy.wait_recv()
    for b in range(SIDE):
        for h, own, got, outf, outb in ((0, nx, gx, cxf, cxb), (1, ny, gy, cyf, cyb)):
            total = dot(vb[h], own[b])
            for j in range(3):
                total = total + dot(got[j], rows[3 * h + j, :, b].reshape(COUNT, BLOCK))
            total = total * scale_value
            outf[b] = total
            outb[b] = total.astype(BF)
    fifth = []
    for j in NEAR:
        fifth.append(
            send(cxb.at[(y + j) % SIDE], hx.at[j - 1], s6.at[0, j - 1], r6.at[0, j - 1], along_y(j))
        )
        fifth.append(
            send(cyb.at[(x + j) % SIDE], hy.at[j - 1], s6.at[1, j - 1], r6.at[1, j - 1], along_x(j))
        )
    pass_on(3)
    loads[12].wait()
    loads[13].wait()
    for copy in fifth:
        copy.wait_recv()
    for h, (own, got, mine) in enumerate(((cxf, hx, y), (cyf, hy, x))):
        total = own[mine]
        for j in range(3):
            total = total + got[j].astype(F32)
        cv[:, h * HALF : (h + 1) * HALF] = total.T
    for copy in shares[6:]:
        copy.wait_recv()
    total = sc[z].astype(F32)
    for way in range(2):
        total = total + rz[way, 3].astype(F32)
    cw[...] = total.T

    def inner(a1, b1, a2, b2):
        total = jnp.zeros((8, 128), F32)
        for a, b in ((a1, b1), (a2, b2)):
            prod = a[...] * b[...]
            prod = jnp.sum(prod.reshape(prod.shape[0] // 8, 8, prod.shape[1]), axis=0)
            for k in range(prod.shape[1] // 128):
                total = total + prod[:, k * 128 : (k + 1) * 128]
        return jnp.sum(total, axis=0, keepdims=True)

    pairs = ((cv, bvv, cw, bov), (cv, cv, cw, cw), (cv, pvv, cw, pov))
    pairs += ((bvv, bvv, bov, bov), (bvv, pvv, bov, pov), (pvv, pvv, pov, pov))
    for k, args in enumerate(pairs):
        one[t, k : k + 1] = inner(*args)
    one[t, 6:8] = jnp.zeros((2, 128), F32)
    rounds = []
    for k in range(1, 16):
        rounds.append(send(one.at[t], one.at[t], o1.at[k], i1.at[k], along_t(k)))
    for copy in rounds:
        copy.wait_recv()
    two[me] = jnp.sum(one[...], axis=0)
    for k, (i, j) in enumerate(plane):
        peer = at(y + i, x + j, t)
        rounds.append(send(two.at[me], two.at[me], o2.at[k], i2.at[k], peer))
    for copy in rounds[15:]:
        copy.wait_recv()
    sums = jnp.sum(jnp.sum(two[...], axis=0), axis=1, keepdims=True) / entries
    beta_before = pb[0, 0]
    cb, cc, cp, bb, bq, pp = (sums[k : k + 1] for k in range(6))
    alpha = cb
    squares = cc + alpha * alpha * bb + beta_before * beta_before * pp
    squares = squares - 2.0 * (alpha * cb + beta_before * (cp - alpha * bq))
    beta = jnp.sqrt(jnp.maximum(squares, 0.0) + epsilon)
    scale = 1.0 / beta
    nv[...] = (cv[...] - alpha * bvv[...] - beta_before * pvv[...]) * scale
    no[...] = (cw[...] - alpha * bov[...] - beta_before * pov[...]) * scale
    coef[0:1] = jnp.broadcast_to(alpha, (1, 128))
    coef[1:2] = jnp.broadcast_to(beta, (1, 128))
    for copy in (
        pieces + weights + others + partial + moved + first_b + second_b
        + third + [swapped] + shares + fourth + fifth + rounds
    ):
        copy.wait_send()
    ring.settle()
    uring.settle()
    for sweep in sweeps:
        for copy in sweep.sent:
            copy.wait_send()


def body(
    tokens,
    target,
    pair_bias,
    neighbours,
    w_query,
    w_key,
    w_value,
    w_out,
    basis_value,
    basis_out,
    prior_value,
    prior_out,
    prior_beta,
):
    def vm(dtype, *dims):
        return pltpu.VMEM(dims, dtype)

    features = 16 * BLOCK
    scratch = [
        vm(BF, ROWS, features),
        vm(BF, ROWS, features),
        vm(BF, COUNT, features),
        vm(BF, SIDE, SIDE, ROWS, BLOCK),
        vm(F32, 16, ROWS, BLOCK),
        vm(F32, 16, ROWS, BLOCK),
        vm(BF, 6, 16, SIDE, ROWS, BLOCK),
        vm(BF, SIDE, BLOCK, 2 * WIDE),
        vm(BF, SIDE, BLOCK, 2 * WIDE),
        vm(BF, SIDE, COUNT, BLOCK),
        vm(BF, SIDE, COUNT, BLOCK),
        vm(BF, 16, WIDE, 2 * BLOCK),
        vm(F32, BLOCK, WIDE),
        vm(F32, WIDE, BLOCK),
        vm(F32, BLOCK, WIDE),
        vm(F32, WIDE, BLOCK),
        vm(jnp.int32, COUNT, COUNT),
        vm(F32, 2, COUNT, COUNT),
        vm(BF, 3, COUNT, 2 * WIDE),
        vm(BF, 3, COUNT, 2 * WIDE),
        vm(BF, 3, COUNT, 2 * WIDE),
        vm(BF, 3, COUNT, 2 * WIDE),
        vm(F32, COUNT, 2 * WIDE),
        vm(F32, COUNT, 2 * WIDE),
        vm(BF, COUNT, 2 * WIDE),
        vm(BF, COUNT, 2 * WIDE),
        vm(BF, 2, COUNT, COUNT),
        vm(BF, COUNT, 2 * WIDE),
        vm(BF, SIDE, SIDE, 16, ROWS, 2 * WIDE),
        vm(F32, COUNT, 2 * BLOCK),
        vm(F32, COUNT, BLOCK),
        vm(BF, COUNT, BLOCK),
        vm(BF, COUNT, BLOCK),
        vm(BF, BLOCK, COUNT),
        vm(BF, BLOCK, COUNT),
        vm(BF, 16, SIDE, SIDE, ROWS, WIDE),
        vm(BF, 3, 8, SIDE, ROWS, WIDE),
        vm(BF, 3, 8, SIDE, ROWS, WIDE),
        vm(BF, SIDE, 8, ROWS, WIDE),
        vm(BF, SIDE, 8, ROWS, WIDE),
        vm(BF, 3, 8, ROWS, WIDE),
        vm(BF, 3, 8, ROWS, WIDE),
        vm(BF, 16, ROWS, WIDE),
        vm(BF, 16, ROWS, WIDE),
        vm(BF, 8, 2, BLOCK, WIDE),
        vm(BF, 8, BLOCK, WIDE),
        vm(BF, 8, BLOCK, WIDE),
        vm(BF, 2, 4, BLOCK, WIDE),
        vm(BF, 2, 3, BLOCK, WIDE),
        vm(BF, 2, HALF, COUNT),
        vm(BF, 3, HALF, COUNT),
        vm(BF, 3, HALF, COUNT),
        vm(F32, SIDE, HALF, BLOCK),
        vm(F32, SIDE, HALF, BLOCK),
        vm(BF, SIDE, HALF, BLOCK),
        vm(BF, SIDE, HALF, BLOCK),
        vm(BF, 3, HALF, BLOCK),
        vm(BF, 3, HALF, BLOCK),
        vm(F32, BLOCK, WIDE),
        vm(F32, WIDE, BLOCK),
        vm(F32, 16, 8, 128),
        vm(F32, 16, 8, 128),
        DMA((14,)),
        DMA((6,)), DMA((6,)),
        DMA((6,)), DMA((6,)),
        DMA((15,)), DMA((15,)),
        DMA((2, 4)), DMA((2, 4)), DMA((8,)), DMA((8,)),
        DMA((2, 4)), DMA((2, 4)), DMA((8,)), DMA((8,)),
        DMA((2, 6)), DMA((2, 6)),
        DMA((16,)), DMA((16,)),
        DMA((2, 4)), DMA((2, 4)), DMA((2, 4, 4)), DMA((2, 4, 4)),
        DMA((2, 3)), DMA((2, 3)),
        DMA((2, 3)), DMA((2, 3)),
        DMA((16,)), DMA((16,)),
        DMA((2, 4)), DMA((2, 4)),
        DMA((2, 3)), DMA((2, 3)),
        DMA((2, 3)), DMA((2, 3)),
        DMA((1,)), DMA((1,)),
        DMA((16,)), DMA((16,)), DMA((15,)), DMA((15,)),
    ]
    next_value, next_out, coef = pl.pallas_call(
        step_kernel,
        out_shape=(
            jax.ShapeDtypeStruct((BLOCK, WIDE), F32),
            jax.ShapeDtypeStruct((WIDE, BLOCK), F32),
            jax.ShapeDtypeStruct((8, 128), F32),
        ),
        in_specs=[ANY] * 12 + [SMEM],
        out_specs=(VMEM, VMEM, VMEM),
        scratch_shapes=scratch,
        compiler_params=pltpu.CompilerParams(
            collective_id=0, has_side_effects=True, vmem_limit_bytes=58 * 2**20
        ),
    )(
        tokens,
        target,
        pair_bias,
        neighbours,
        w_query,
        w_key,
        w_value,
        w_out,
        basis_value,
        basis_out,
        prior_value,
        prior_out,
        prior_beta.reshape(1, 1),
    )
    return next_value, next_out, coef[:2, 0]


def solution(mesh):
    placed = (
        P("dp", None),
        P("dp", None),
        P("dp", "tensor", None),
        P("dp", None),
        P("dp", "tensor"),
        P("dp", "tensor"),
        P("dp", "tensor"),
        P("tensor", "dp"),
        P("dp", "tensor"),
        P("tensor", "dp"),
        P("dp", "tensor"),
        P("tensor", "dp"),
        P(),
    )
    return jax.shard_map(
        body,
        mesh=mesh,
        in_specs=placed,
        out_specs=(P("dp", "tensor"), P("tensor", "dp"), P()),
        check_vma=False,
    )
```

```python
import math

import jax
import jax.numpy as jnp
from jax import lax
from jax.experimental import pallas as pl
from jax.experimental.pallas import tpu as pltpu
from jax.sharding import PartitionSpec as P

HEAD_DIM = 128
SIDE = 4
ROWS = 16

loss_gain = 32.0
epsilon = 1e-06

MESH = pl.DeviceIdType.MESH
BF = jnp.bfloat16
F32 = jnp.float32
VMEM = pl.BlockSpec(memory_space=pltpu.VMEM)
ANY = pl.BlockSpec(memory_space=pl.ANY)
SMEM = pl.BlockSpec(memory_space=pltpu.SMEM)
DMA = pltpu.SemaphoreType.DMA


def coords():
    dp = lax.axis_index("dp")
    t = lax.axis_index("tensor")
    return dp // SIDE, dp % SIDE, t


def at(y, x, t):
    return (((y + 2 * SIDE) % SIDE) * SIDE + (x + 2 * SIDE) % SIDE, (t + 32) % 16)


def along_x(j):
    y, x, t = coords()
    return at(y, x + j, t)


def along_y(j):
    y, x, t = coords()
    return at(y + j, x, t)


def along_t(k):
    y, x, t = coords()
    return at(y, x, t + k)


def along_z(k):
    y, x, t = coords()
    return at(y, x, t + 2 * k)


def other_core():
    y, x, t = coords()
    return at(y, x, t + 1 - 2 * (t % 2))


def greet(peers):
    barrier = pltpu.get_barrier_semaphore()
    for peer in peers:
        pl.semaphore_signal(barrier, inc=1, device_id=peer, device_id_type=MESH)
    pl.semaphore_wait(barrier, len(peers))


def send(src, dst, ssem, rsem, peer):
    copy = pltpu.make_async_remote_copy(
        src_ref=src,
        dst_ref=dst,
        send_sem=ssem,
        recv_sem=rsem,
        device_id=peer,
        device_id_type=MESH,
    )
    copy.start()
    return copy


NEAR = (1, 3, 2)
WIDE = 256
HALF = 128
BLOCK = 384
COUNT = 256


def dot(a, b):
    return jnp.dot(a, b, preferred_element_type=F32)


def dot_t(a, b):
    return lax.dot_general(a, b, (((1,), (1,)), ((), ())), preferred_element_type=F32)


def arrival(ref, ssem, rsem):
    y, x, t = coords()
    return pltpu.make_async_remote_copy(
        src_ref=ref,
        dst_ref=ref,
        send_sem=ssem,
        recv_sem=rsem,
        device_id=at(y, x, t + 2),
        device_id_type=MESH,
    )


class Ring:
    def __init__(self, slot, part, zs, zr, cs, cr):
        self.slot, self.part = slot, part
        self.zs, self.zr, self.cs, self.cr = zs, zr, cs, cr
        self.sent = []

    def start(self):
        y, x, t = coords()
        for i in range(2):
            own = self.part(t, i)
            for way in range(2):
                sem = (way, 0, i)
                self.sent.append(
                    send(own, own, self.zs.at[sem], self.zr.at[sem], along_z(1 - 2 * way))
                )
        self.core(t, 0)

    def core(self, slot, k):
        got = self.slot(slot)
        self.sent.append(send(got, got, self.cs.at[k], self.cr.at[k], other_core()))

    def step(self, step, onward):
        y, x, t = coords()
        slots = [(t - 2 * (1 - 2 * way) * step + 32) % 16 for way in range(2)]
        for i in range(2):
            for way in range(2):
                part = self.part(slots[way], i)
                sem = (way, step - 1, i)
                arrival(part, self.zs.at[sem], self.zr.at[sem]).wait_recv()
                if i in onward[way]:
                    sem = (way, step, i)
                    self.sent.append(
                        send(part, part, self.zs.at[sem], self.zr.at[sem], along_z(1 - 2 * way))
                    )
        for way in range(2):
            self.core(slots[way], 2 * step - 1 + way)

    def finish(self):
        y, x, t = coords()
        far = (t + 8) % 16
        for way in range(2):
            sem = (way, 3, way)
            arrival(self.part(far, way), self.zs.at[sem], self.zr.at[sem]).wait_recv()
        self.core(far, 7)

    def cores(self, some):
        y, x, t = coords()
        for k in some:
            step, way = (k + 1) // 2, (k + 1) % 2
            shift = 8 if k == 7 else 2 * step * (1 - 2 * way)
            got = self.slot((t + 1 - 2 * (t % 2) - shift + 32) % 16)
            arrival(got, self.cs.at[k], self.cr.at[k]).wait_recv()

    def settle(self):
        for copy in self.sent:
            copy.wait_send()


ALL, NONE = ((0, 1), (0, 1)), ((), ())


class Sweep:
    OFFSETS = (0, -1, 1, 2)

    def __init__(self, part, full, sp, rp, ss, rs):
        y, x, t = coords()
        self.sent = []
        self.sp, self.rp, self.ss, self.rs = sp, rp, ss, rs
        self.first, self.then = (along_x, along_y) if part == 0 else (along_y, along_x)
        self.base = 8 * part

        def block(p, s, half=None):
            rng = pl.ds(self.base, 8) if half is None else pl.ds(self.base + 4 * half, 4)
            dy, dx = (s, p) if part == 0 else (p, s)
            return full.at[(y + dy + SIDE) % SIDE, (x + dx + SIDE) % SIDE, rng]

        self.block = block

    def push(self, ref, ssem, rsem, peer):
        self.sent.append(send(ref, ref, ssem, rsem, peer))

    def start(self):
        own = self.block(0, 0)
        for k in range(2):
            self.push(own, self.sp.at[k], self.rp.at[k], self.first(1 - 2 * k))

    def across(self, q):
        own = self.block(self.OFFSETS[q], 0)
        for k in range(2):
            self.push(own, self.ss.at[q, k], self.rs.at[q, k], self.then(1 - 2 * k))

    def relay(self):
        for k in range(2):
            off = 2 * k - 1
            arrival(self.block(off, 0), self.sp.at[k], self.rp.at[k]).wait_recv()
            half = self.block(off, 0, k)
            self.push(half, self.sp.at[2 + k], self.rp.at[2 + k], self.first(1 - 2 * k))

    def relay_across(self, q):
        p = self.OFFSETS[q]
        for k in range(2):
            off = 2 * k - 1
            arrival(self.block(p, off), self.ss.at[q, k], self.rs.at[q, k]).wait_recv()
            half = self.block(p, off, k)
            self.push(half, self.ss.at[q, 2 + k], self.rs.at[q, 2 + k], self.then(1 - 2 * k))

    def far(self):
        for k in range(2):
            arrival(self.block(2, 0, k), self.sp.at[2 + k], self.rp.at[2 + k]).wait_recv()

    def last(self):
        for q in range(4):
            for k in range(2):
                arrival(
                    self.block(self.OFFSETS[q], 2, k), self.ss.at[q, 2 + k], self.rs.at[q, 2 + k]
                ).wait_recv()


def step_kernel(
    tokens, target, bias, near, wq, wk, wv, wo, bv, bo, pv, po, pb,
    nv, no, coef,
    tok16, tgt16, tok, n16, diff, diffs, rows, gqk, gvt, nx, ny, uall,
    bvv, bov, pvv, pov, nearv, biasv,
    pq, pt, rq, rv, accq, accv, qk, vt, probs, mix, full,
    acc1, acc2, err, terr, errt, terrt, bp, ra, rb, sa, sb, qa, qb, done, bt,
    co, rc, sc, rz, tx, vb, gx, gy, cxf, cyf, cxb, cyb, hx, hy, cv, cw, one, two,
    ls, ps, pr, ws, wr, ds, dr, zs, zr, cs, cr, us, ur, vs, vr, xs, xr, ts, tr,
    as_, ar, bs, br, s1, r1, s2, r2, s3, r3, s4, r4, s5, r5, s6, r6, s7, r7, o1, i1, o2, i2,
):
    y, x, t = coords()
    c = t % 2
    z = t // 2
    me = y * SIDE + x
    full_width = 16 * WIDE
    features = 16 * BLOCK
    scale_out = 1.0 / math.sqrt(full_width)
    scale_value = 1.0 / math.sqrt(features)
    factor = loss_gain * full_width / (16 * COUNT)
    entries = 2.0 * features * full_width

    plane = [(i, j) for i in range(SIDE) for j in range(SIDE) if i or j]
    barrier = pltpu.get_barrier_semaphore()
    for i, j in plane:
        pl.semaphore_signal(barrier, inc=1, device_id=at(y + i, x + j, t), device_id_type=MESH)
    for k in range(1, 16):
        pl.semaphore_signal(barrier, inc=1, device_id=along_t(k), device_id_type=MESH)

    some = pl.ds(pl.multiple_of(t * ROWS, ROWS), ROWS)
    far = (t + 8) % 16
    some_far = pl.ds(pl.multiple_of(far * ROWS, ROWS), ROWS)
    left, right = pl.ds(0, WIDE), pl.ds(WIDE, WIDE)
    loads = [
        (tokens.at[some], tok16.at[0]),
        (tokens.at[some_far], tok16.at[1]),
        (target.at[some], tgt16),
        (wq, gqk.at[y, :, left]),
        (wk, gqk.at[y, :, right]),
        (wv, gvt.at[x, :, left]),
        (bv, bvv),
        (tokens, tok),
        (wo, uall.at[t, :, pl.ds(0, BLOCK)]),
        (bo, bov),
        (near, nearv),
        (bias.at[:, 0], biasv.at[0]),
        (bias.at[:, 1], biasv.at[1]),
        (pv, pvv),
        (po, pov),
    ]
    loads = [pltpu.make_async_copy(a, b, ls.at[k]) for k, (a, b) in enumerate(loads)]
    for copy in loads:
        copy.start()

    for copy in loads[:3]:
        copy.wait()
    for i in range(2):
        xf = tok16[i].astype(F32)
        inv = lax.rsqrt(jnp.mean(xf * xf, axis=1, keepdims=True) + epsilon)
        for k in range(16):
            part = tok16[i, :, k * BLOCK : (k + 1) * BLOCK].astype(F32)
            n16[i, k // SIDE, k % SIDE] = (part * inv).astype(BF)
            if i == 0:
                diff[k] = part - tgt16[:, k * BLOCK : (k + 1) * BLOCK].astype(F32)
    pl.semaphore_wait(barrier, 30)

    pieces, weights, others = [], [], []

    def pass_rows(i, slot):
        for j in NEAR:
            src, sem = n16.at[i, :, (x + j) % SIDE], (i, j - 1)
            pieces.append(
                send(src, rows.at[j - 1, slot], ps.at[sem], pr.at[sem], along_x(j))
            )
            src, sem = n16.at[i, (y + j) % SIDE], (i, j + 2)
            pieces.append(
                send(src, rows.at[j + 2, slot], ps.at[sem], pr.at[sem], along_y(j))
            )

    pass_rows(0, t)
    for k in (3, 4, 5, 6):
        loads[k].wait()
    gvt[x, :, WIDE:] = bvv[...].astype(BF)
    for j in NEAR:
        weights.append(send(gqk.at[y], gqk.at[y], ws.at[j - 1], wr.at[j - 1], along_y(j)))
        weights.append(send(gvt.at[x], gvt.at[x], ws.at[j + 2], wr.at[j + 2], along_x(j)))
    pass_rows(1, far)
    for k, (i, j) in enumerate(plane):
        yy, xx = (y + i) % SIDE, (x + j) % SIDE
        others.append(
            send(diff.at[yy * SIDE + xx], diffs.at[me], ds.at[k], dr.at[k], (yy * SIDE + xx, t))
        )
    diffs[me] = diff[me]

    ring = Ring(
        lambda n: rows.at[:, n], lambda n, i: rows.at[pl.ds(3 * i, 3), n], zs, zr, cs, cr
    )
    for copy in pieces[:6]:
        copy.wait_recv()
    ring.start()

    loads[7].wait()

    def normalise(r, _):
        at_r = pl.ds(pl.multiple_of(r * ROWS, ROWS), ROWS)
        xf = tok[at_r].astype(F32)
        inv = lax.rsqrt(jnp.mean(xf * xf, axis=1, keepdims=True) + epsilon)
        for b in range(SIDE):
            cut = pl.ds(pl.multiple_of((b * SIDE + x) * BLOCK, HALF), BLOCK)
            nx[b, at_r] = (tok[at_r, cut].astype(F32) * inv).astype(BF)
            cut = pl.ds(pl.multiple_of((y * SIDE + b) * BLOCK, HALF), BLOCK)
            ny[b, at_r] = (tok[at_r, cut].astype(F32) * inv).astype(BF)
        return 0

    lax.fori_loop(0, COUNT // ROWS, normalise, 0)
    ring.step(1, ALL)
    loads[8].wait()
    loads[9].wait()
    uall[t, :, BLOCK:] = bov[...].astype(BF)
    ring.step(2, ALL)
    for copy in pieces[6:]:
        copy.wait_recv()
    ring.core(far, 7)
    for copy in weights:
        copy.wait_recv()
    for lhs, w, acc in ((nx, gqk, accq), (ny, gvt, accv)):
        total = dot(lhs[0], w[0])
        for b in range(1, SIDE):
            total = total + dot(lhs[b], w[b])
        acc[...] = total

    order = []
    for off in (0, -1, 1, -2, 2, 4, -3, 3):
        base = ((z + off + 8) % 8) * 2
        order += [base + c, base + 1 - c]
    partial = []

    def products(part, lo, hi):
        for w, k0, out, got, along in ((gqk, 0, pq, rq, along_x), (gvt, 3, pt, rv, along_y)):
            total = None
            for b in range(SIDE):
                lhs = jnp.concatenate(
                    [rows[k0 + j, n, b] for j in range(3) for n in order[lo:hi]], axis=0
                )
                more = dot(lhs, w[b])
                total = more if total is None else total + more
            size = (hi - lo) * ROWS
            for j in range(3):
                out[j, lo * ROWS : hi * ROWS] = total[j * size : (j + 1) * size].astype(BF)
            cut = pl.ds(lo * ROWS, size)
            for j in NEAR:
                sem = (part, k0 + j - 1)
                partial.append(
                    send(out.at[j - 1, cut], got.at[j - 1, cut], xs.at[sem], xr.at[sem], along(-j))
                )

    ring.cores((0, 1, 2, 3, 4, 7))
    products(0, 0, 12)
    ring.step(3, NONE)
    uring = Ring(
        lambda n: uall.at[n], lambda n, i: uall.at[n, pl.ds(HALF * i, HALF)], us, ur, vs, vr
    )
    uring.start()
    ring.cores((5, 6))
    products(1, 12, 16)
    for copy in partial:
        copy.wait_recv()

    for p, n in enumerate(order):
        at_n = pl.ds(pl.multiple_of(n * ROWS, ROWS), ROWS)
        at_p = slice(p * ROWS, (p + 1) * ROWS)
        total = accq[at_n]
        for j in range(3):
            total = total + rq[j, at_p].astype(F32)
        qk[at_n] = total.astype(BF)
        total = accv[at_n]
        for j in range(3):
            total = total + rv[j, at_p].astype(F32)
        vt[at_n, :WIDE] = total[:, :WIDE].astype(BF)
        vt[at_n, WIDE:] = (total[:, WIDE:] / math.sqrt(features)).astype(BF)

    loads[10].wait()
    loads[11].wait()
    loads[12].wait()
    at_row = lax.broadcasted_iota(jnp.int32, (COUNT, COUNT), 0)
    at_col = lax.broadcasted_iota(jnp.int32, (COUNT, COUNT), 1)
    allowed = (nearv[...] == 1) | (jnp.abs(at_row - at_col) <= 1)
    for h in range(2):
        cut = slice(h * HALF, (h + 1) * HALF)
        cut2 = slice(WIDE + h * HALF, WIDE + (h + 1) * HALF)
        scores = dot_t(qk[:, cut], qk[:, cut2]) / math.sqrt(HEAD_DIM) + biasv[h]
        scores = jnp.where(allowed, scores, -jnp.inf)
        e = jnp.exp(scores - jnp.max(scores, axis=1, keepdims=True))
        p = (e / jnp.sum(e, axis=1, keepdims=True)).astype(BF)
        probs[h] = p
        mix[:, cut] = dot(p, vt[:, cut]).astype(BF)
        mix[:, cut2] = dot(p, vt[:, cut2]).astype(BF)

    moved = []
    for k in range(1, 16):
        to = pl.ds(pl.multiple_of(((t + k) % 16) * ROWS, ROWS), ROWS)
        moved.append(send(mix.at[to], full.at[y, x, t], ts.at[k], tr.at[k], along_t(k)))
    full[y, x, t] = mix[some]
    uring.step(1, ALL)
    for copy in moved:
        copy.wait_recv()
    sweeps = [
        Sweep(0, full, as_.at[0], ar.at[0], bs.at[0], br.at[0]),
        Sweep(1, full, as_.at[1], ar.at[1], bs.at[1], br.at[1]),
    ]
    for sweep in sweeps:
        sweep.start()
    for sweep in sweeps:
        sweep.across(0)
    uring.step(2, ALL)
    for sweep in sweeps:
        sweep.relay()
    for sweep in sweeps:
        sweep.across(1)
        sweep.across(2)
    for sweep in sweeps:
        sweep.relay_across(0)
    uring.step(3, ((0,), (1,)))
    for sweep in sweeps:
        sweep.far()
        sweep.across(3)
    for q in (1, 2):
        for sweep in sweeps:
            sweep.relay_across(q)
    uring.finish()
    for sweep in sweeps:
        sweep.relay_across(3)
    uring.cores(range(8))
    for sweep in sweeps:
        sweep.last()

    acc1[...] = jnp.zeros_like(acc1)
    acc2[...] = jnp.zeros_like(acc2)

    def forward(k, _):
        at_k = pl.ds(k * 4, 4)
        parts = [full[:, :, k * 4 + i].reshape(COUNT, 2 * WIDE) for i in range(4)]
        w = uall[at_k].reshape(4 * WIDE, 2 * BLOCK)
        acc1[...] += dot(jnp.concatenate([p[:, :WIDE] for p in parts], axis=1), w)
        acc2[...] += dot(jnp.concatenate([p[:, WIDE:] for p in parts], axis=1), w[:, :BLOCK])
        return 0

    lax.fori_loop(0, 4, forward, 0)
    for copy in others:
        copy.wait_recv()
    err[...] = ((diffs[...].reshape(COUNT, BLOCK) + acc1[:, :BLOCK]) * factor).astype(BF)
    terr[...] = ((acc1[:, BLOCK:] * scale_out + acc2[...]) * factor).astype(BF)

    def backward(n, _):
        part = dot_t(terr[...], uall[n, :, :BLOCK]) + scale_out * dot_t(err[...], uall[n, :, BLOCK:])
        bp[n] = part.astype(BF).reshape(SIDE, SIDE, ROWS, WIDE)
        return 0

    first_b = []
    for part in range(2):
        lax.fori_loop(4 * part, 4 * part + 4, backward, 0)
        lax.fori_loop(8 + 4 * part, 12 + 4 * part, backward, 0)
        low, high, here = pl.ds(4 * part, 4), pl.ds(8 + 4 * part, 4), pl.ds(4 * part, 4)
        for j in NEAR:
            src, sem = bp.at[low, (y + j) % SIDE], (part, 0, j - 1)
            first_b.append(send(src, ra.at[j - 1, here], s1.at[sem], r1.at[sem], along_y(j)))
            src, sem = bp.at[high, :, (x + j) % SIDE], (part, 1, j - 1)
            first_b.append(send(src, rb.at[j - 1, here], s1.at[sem], r1.at[sem], along_x(j)))

    errt[...] = err[...].astype(F32).T.astype(BF)
    terrt[...] = terr[...].astype(F32).T.astype(BF)

    def outer(n, _):
        both = full[:, :, n].reshape(COUNT, 2 * WIDE)
        part = dot(errt[...], both[:, WIDE:]) + dot(terrt[...], both[:, :WIDE])
        co[n // 2, n % 2] = (part * scale_out).astype(BF)
        return 0

    lax.fori_loop(0, 16, outer, 0)
    swapped = send(co.at[:, 1 - c], rc, s7.at[0], r7.at[0], other_core())

    second_b = []
    for part in range(2):
        for copy in first_b[6 * part : 6 * part + 6]:
            copy.wait_recv()
        a, b = 4 * part, 4 * part + 4
        for i in range(SIDE):
            total = bp[a:b, y, i].astype(F32)
            for j in range(3):
                total = total + ra[j, a:b, i].astype(F32)
            sa[i, a:b] = total.astype(BF)
            total = bp[8 + a : 8 + b, i, x].astype(F32)
            for j in range(3):
                total = total + rb[j, a:b, i].astype(F32)
            sb[i, a:b] = total.astype(BF)
        here = pl.ds(a, 4)
        for j in NEAR:
            src, sem = sa.at[(x + j) % SIDE, here], (part, 0, j - 1)
            second_b.append(send(src, qa.at[j - 1, here], s2.at[sem], r2.at[sem], along_x(j)))
            src, sem = sb.at[(y + j) % SIDE, here], (part, 1, j - 1)
            second_b.append(send(src, qb.at[j - 1, here], s2.at[sem], r2.at[sem], along_y(j)))

    swapped.wait_recv()

    def pair(k, _):
        sc[k] = (co[k, c].astype(F32) + rc[k].astype(F32)).astype(BF)
        return 0

    lax.fori_loop(0, 8, pair, 0)
    shares = []

    def pass_on(step):
        for way in range(2):
            sign = 1 - 2 * way
            slot = (z + sign * (4 - step) + 8) % 8
            if step == 0:
                cut = pl.ds(way * (BLOCK // 2), BLOCK // 2)
                src, dst = sc.at[slot, cut], rz.at[way, 0, cut]
            else:
                shares[2 * (step - 1) + way].wait_recv()
                if step == 1:
                    a, b = way * (BLOCK // 2), (way + 1) * (BLOCK // 2)
                    tx[way, 0] = sc[slot]
                    total = sc[slot, a:b].astype(F32) + rz[way, 0, a:b].astype(F32)
                    tx[way, 0, a:b] = total.astype(BF)
                else:
                    total = sc[slot].astype(F32) + rz[way, step - 1].astype(F32)
                    tx[way, step - 1] = total.astype(BF)
                src, dst = tx.at[way, step - 1], rz.at[way, step]
            shares.append(
                send(src, dst, s4.at[way, step], r4.at[way, step], along_z(sign))
            )

    pass_on(0)
    for copy in second_b:
        copy.wait_recv()
    total = sa[x].astype(F32)
    for j in range(3):
        total = total + qa[j].astype(F32)
    done[0:8] = total.astype(BF)
    total = sb[y].astype(F32)
    for j in range(3):
        total = total + qb[j].astype(F32)
    done[8:16] = total.astype(BF)
    third = []
    for k in range(1, 16):
        third.append(send(done.at[(t + k) % 16], bt.at[t], s3.at[k], r3.at[k], along_t(k)))
    bt[t] = done[t]

    pass_on(1)
    for copy in third:
        copy.wait_recv()
    back = bt[...].reshape(COUNT, WIDE).astype(F32).T.astype(BF)
    fourth = []
    for h in range(2):
        vb[h] = dot(back[h * HALF : (h + 1) * HALF], probs[h]).astype(BF)
        got, along = ((gx, along_x), (gy, along_y))[h]
        for j in NEAR:
            fourth.append(
                send(vb.at[h], got.at[j - 1], s5.at[h, j - 1], r5.at[h, j - 1], along(j))
            )
    pass_on(2)
    for copy in fourth:
        copy.wait_recv()
    fifth = []
    for k in (2, 1, 3, 0):
        for h, own, got, mine, outf, outb, to, along in (
            (0, nx, gx, y, cxf, cxb, hx, along_y),
            (1, ny, gy, x, cyf, cyb, hy, along_x),
        ):
            b = (mine + k) % SIDE
            total = dot(vb[h], own[b])
            for j in range(3):
                total = total + dot(got[j], rows[3 * h + j, :, b].reshape(COUNT, BLOCK))
            total = total * scale_value
            if k == 0:
                outf[...] = total
            else:
                outb[k - 1] = total.astype(BF)
                fifth.append(
                    send(outb.at[k - 1], to.at[k - 1], s6.at[h, k - 1], r6.at[h, k - 1], along(k))
                )
    pass_on(3)
    loads[13].wait()
    loads[14].wait()
    for copy in fifth:
        copy.wait_recv()
    for h, (own, got) in enumerate(((cxf, hx), (cyf, hy))):
        total = own[...]
        for j in range(3):
            total = total + got[j].astype(F32)
        cv[:, h * HALF : (h + 1) * HALF] = total.T
    for copy in shares[6:]:
        copy.wait_recv()
    total = sc[z].astype(F32)
    for way in range(2):
        total = total + rz[way, 3].astype(F32)
    cw[...] = total.T

    def inner(a1, b1, a2, b2):
        total = jnp.zeros((8, 128), F32)
        for a, b in ((a1, b1), (a2, b2)):
            prod = a[...] * b[...]
            prod = jnp.sum(prod.reshape(prod.shape[0] // 8, 8, prod.shape[1]), axis=0)
            for k in range(prod.shape[1] // 128):
                total = total + prod[:, k * 128 : (k + 1) * 128]
        return jnp.sum(total, axis=0, keepdims=True)

    pairs = ((cv, bvv, cw, bov), (cv, cv, cw, cw), (cv, pvv, cw, pov))
    pairs += ((bvv, bvv, bov, bov), (bvv, pvv, bov, pov), (pvv, pvv, pov, pov))
    for k, args in enumerate(pairs):
        one[t, k : k + 1] = inner(*args)
    one[t, 6:8] = jnp.zeros((2, 128), F32)
    rounds = []
    for k in range(1, 16):
        rounds.append(send(one.at[t], one.at[t], o1.at[k], i1.at[k], along_t(k)))
    for copy in rounds:
        copy.wait_recv()
    two[me] = jnp.sum(one[...], axis=0)
    for k, (i, j) in enumerate(plane):
        peer = at(y + i, x + j, t)
        rounds.append(send(two.at[me], two.at[me], o2.at[k], i2.at[k], peer))
    for copy in rounds[15:]:
        copy.wait_recv()
    sums = jnp.sum(jnp.sum(two[...], axis=0), axis=1, keepdims=True) / entries
    beta_before = pb[0, 0]
    cb, cc, cp, bb, bq, pp = (sums[k : k + 1] for k in range(6))
    alpha = cb
    squares = cc + alpha * alpha * bb + beta_before * beta_before * pp
    squares = squares - 2.0 * (alpha * cb + beta_before * (cp - alpha * bq))
    beta = jnp.sqrt(jnp.maximum(squares, 0.0) + epsilon)
    nv[...] = cv[...] - alpha * bvv[...] - beta_before * pvv[...]
    no[...] = cw[...] - alpha * bov[...] - beta_before * pov[...]
    coef[0:1] = jnp.broadcast_to(alpha, (1, 128))
    coef[1:2] = jnp.broadcast_to(beta, (1, 128))
    coef[2:3] = jnp.broadcast_to(1.0 / beta, (1, 128))
    for copy in (
        pieces + weights + others + partial + moved + first_b + second_b
        + third + [swapped] + shares + fourth + fifth + rounds
    ):
        copy.wait_send()
    ring.settle()
    uring.settle()
    for sweep in sweeps:
        for copy in sweep.sent:
            copy.wait_send()


def scale_kernel(rest_value, rest_out, coef, nv, no, out):
    scale = coef[2:3, 0:1]
    nv[...] = rest_value[...] * scale
    no[...] = rest_out[...] * scale
    out[0] = coef[0, 0]
    out[1] = coef[1, 0]


def body(
    tokens,
    target,
    pair_bias,
    neighbours,
    w_query,
    w_key,
    w_value,
    w_out,
    basis_value,
    basis_out,
    prior_value,
    prior_out,
    prior_beta,
):
    def vm(dtype, *dims):
        return pltpu.VMEM(dims, dtype)

    features = 16 * BLOCK
    scratch = [
        vm(BF, 2, ROWS, features),
        vm(BF, ROWS, features),
        vm(BF, COUNT, features),
        vm(BF, 2, SIDE, SIDE, ROWS, BLOCK),
        vm(F32, 16, ROWS, BLOCK),
        vm(F32, 16, ROWS, BLOCK),
        vm(BF, 6, 16, SIDE, ROWS, BLOCK),
        vm(BF, SIDE, BLOCK, 2 * WIDE),
        vm(BF, SIDE, BLOCK, 2 * WIDE),
        vm(BF, SIDE, COUNT, BLOCK),
        vm(BF, SIDE, COUNT, BLOCK),
        vm(BF, 16, WIDE, 2 * BLOCK),
        vm(F32, BLOCK, WIDE),
        vm(F32, WIDE, BLOCK),
        vm(F32, BLOCK, WIDE),
        vm(F32, WIDE, BLOCK),
        vm(jnp.int32, COUNT, COUNT),
        vm(F32, 2, COUNT, COUNT),
        vm(BF, 3, COUNT, 2 * WIDE),
        vm(BF, 3, COUNT, 2 * WIDE),
        vm(BF, 3, COUNT, 2 * WIDE),
        vm(BF, 3, COUNT, 2 * WIDE),
        vm(F32, COUNT, 2 * WIDE),
        vm(F32, COUNT, 2 * WIDE),
        vm(BF, COUNT, 2 * WIDE),
        vm(BF, COUNT, 2 * WIDE),
        vm(BF, 2, COUNT, COUNT),
        vm(BF, COUNT, 2 * WIDE),
        vm(BF, SIDE, SIDE, 16, ROWS, 2 * WIDE),
        vm(F32, COUNT, 2 * BLOCK),
        vm(F32, COUNT, BLOCK),
        vm(BF, COUNT, BLOCK),
        vm(BF, COUNT, BLOCK),
        vm(BF, BLOCK, COUNT),
        vm(BF, BLOCK, COUNT),
        vm(BF, 16, SIDE, SIDE, ROWS, WIDE),
        vm(BF, 3, 8, SIDE, ROWS, WIDE),
        vm(BF, 3, 8, SIDE, ROWS, WIDE),
        vm(BF, SIDE, 8, ROWS, WIDE),
        vm(BF, SIDE, 8, ROWS, WIDE),
        vm(BF, 3, 8, ROWS, WIDE),
        vm(BF, 3, 8, ROWS, WIDE),
        vm(BF, 16, ROWS, WIDE),
        vm(BF, 16, ROWS, WIDE),
        vm(BF, 8, 2, BLOCK, WIDE),
        vm(BF, 8, BLOCK, WIDE),
        vm(BF, 8, BLOCK, WIDE),
        vm(BF, 2, 4, BLOCK, WIDE),
        vm(BF, 2, 3, BLOCK, WIDE),
        vm(BF, 2, HALF, COUNT),
        vm(BF, 3, HALF, COUNT),
        vm(BF, 3, HALF, COUNT),
        vm(F32, HALF, BLOCK),
        vm(F32, HALF, BLOCK),
        vm(BF, 3, HALF, BLOCK),
        vm(BF, 3, HALF, BLOCK),
        vm(BF, 3, HALF, BLOCK),
        vm(BF, 3, HALF, BLOCK),
        vm(F32, BLOCK, WIDE),
        vm(F32, WIDE, BLOCK),
        vm(F32, 16, 8, 128),
        vm(F32, 16, 8, 128),
        DMA((15,)),
        DMA((2, 6)), DMA((2, 6)),
        DMA((6,)), DMA((6,)),
        DMA((15,)), DMA((15,)),
        DMA((2, 3, 2)), DMA((2, 3, 2)), DMA((8,)), DMA((8,)),
        DMA((2, 4, 2)), DMA((2, 4, 2)), DMA((8,)), DMA((8,)),
        DMA((2, 6)), DMA((2, 6)),
        DMA((16,)), DMA((16,)),
        DMA((2, 4)), DMA((2, 4)), DMA((2, 4, 4)), DMA((2, 4, 4)),
        DMA((2, 2, 3)), DMA((2, 2, 3)),
        DMA((2, 2, 3)), DMA((2, 2, 3)),
        DMA((16,)), DMA((16,)),
        DMA((2, 4)), DMA((2, 4)),
        DMA((2, 3)), DMA((2, 3)),
        DMA((2, 3)), DMA((2, 3)),
        DMA((1,)), DMA((1,)),
        DMA((16,)), DMA((16,)), DMA((15,)), DMA((15,)),
    ]
    rest_value, rest_out, coef = pl.pallas_call(
        step_kernel,
        out_shape=(
            jax.ShapeDtypeStruct((BLOCK, WIDE), F32),
            jax.ShapeDtypeStruct((WIDE, BLOCK), F32),
            jax.ShapeDtypeStruct((8, 128), F32),
        ),
        in_specs=[ANY] * 12 + [SMEM],
        out_specs=(VMEM, VMEM, VMEM),
        scratch_shapes=scratch,
        compiler_params=pltpu.CompilerParams(
            collective_id=0, has_side_effects=True, vmem_limit_bytes=58 * 2**20
        ),
    )(
        tokens,
        target,
        pair_bias,
        neighbours,
        w_query,
        w_key,
        w_value,
        w_out,
        basis_value,
        basis_out,
        prior_value,
        prior_out,
        prior_beta.reshape(1, 1),
    )
    return pl.pallas_call(
        scale_kernel,
        out_shape=(
            jax.ShapeDtypeStruct((BLOCK, WIDE), F32),
            jax.ShapeDtypeStruct((WIDE, BLOCK), F32),
            jax.ShapeDtypeStruct((2,), F32),
        ),
        in_specs=[VMEM] * 3,
        out_specs=(VMEM, VMEM, SMEM),
    )(rest_value, rest_out, coef)


def solution(mesh):
    placed = (
        P("dp", None),
        P("dp", None),
        P("dp", "tensor", None),
        P("dp", None),
        P("dp", "tensor"),
        P("dp", "tensor"),
        P("dp", "tensor"),
        P("tensor", "dp"),
        P("dp", "tensor"),
        P("tensor", "dp"),
        P("dp", "tensor"),
        P("tensor", "dp"),
        P(),
    )
    return jax.shard_map(
        body,
        mesh=mesh,
        in_specs=placed,
        out_specs=(P("dp", "tensor"), P("tensor", "dp"), P()),
        check_vma=False,
    )
```

```python
import math

import jax
import jax.numpy as jnp
from jax import lax
from jax.experimental import pallas as pl
from jax.experimental.pallas import tpu as pltpu
from jax.sharding import PartitionSpec as P

HEAD_DIM = 128
SIDE = 4
ROWS = 16

loss_gain = 32.0
epsilon = 1e-06

MESH = pl.DeviceIdType.MESH
BF = jnp.bfloat16
F32 = jnp.float32
VMEM = pl.BlockSpec(memory_space=pltpu.VMEM)
ANY = pl.BlockSpec(memory_space=pl.ANY)
SMEM = pl.BlockSpec(memory_space=pltpu.SMEM)
DMA = pltpu.SemaphoreType.DMA


def coords():
    dp = lax.axis_index("dp")
    t = lax.axis_index("tensor")
    return dp // SIDE, dp % SIDE, t


def at(y, x, t):
    return (((y + 2 * SIDE) % SIDE) * SIDE + (x + 2 * SIDE) % SIDE, (t + 32) % 16)


def along_x(j):
    y, x, t = coords()
    return at(y, x + j, t)


def along_y(j):
    y, x, t = coords()
    return at(y + j, x, t)


def along_t(k):
    y, x, t = coords()
    return at(y, x, t + k)


def along_z(k):
    y, x, t = coords()
    return at(y, x, t + 2 * k)


def other_core():
    y, x, t = coords()
    return at(y, x, t + 1 - 2 * (t % 2))


def greet(peers):
    barrier = pltpu.get_barrier_semaphore()
    for peer in peers:
        pl.semaphore_signal(barrier, inc=1, device_id=peer, device_id_type=MESH)
    pl.semaphore_wait(barrier, len(peers))


def send(src, dst, ssem, rsem, peer):
    copy = pltpu.make_async_remote_copy(
        src_ref=src,
        dst_ref=dst,
        send_sem=ssem,
        recv_sem=rsem,
        device_id=peer,
        device_id_type=MESH,
    )
    copy.start()
    return copy


NEAR = (1, 3, 2)
WIDE = 256
HALF = 128
BLOCK = 384
COUNT = 256


def dot(a, b):
    return jnp.dot(a, b, preferred_element_type=F32)


def dot_t(a, b):
    return lax.dot_general(a, b, (((1,), (1,)), ((), ())), preferred_element_type=F32)


def arrival(ref, ssem, rsem):
    y, x, t = coords()
    return pltpu.make_async_remote_copy(
        src_ref=ref,
        dst_ref=ref,
        send_sem=ssem,
        recv_sem=rsem,
        device_id=at(y, x, t + 2),
        device_id_type=MESH,
    )


class Ring:
    def __init__(self, slot, part, zs, zr, cs, cr):
        self.slot, self.part = slot, part
        self.zs, self.zr, self.cs, self.cr = zs, zr, cs, cr
        self.sent = []

    def start(self):
        y, x, t = coords()
        for i in range(2):
            own = self.part(t, i)
            for way in range(2):
                sem = (way, 0, i)
                self.sent.append(
                    send(own, own, self.zs.at[sem], self.zr.at[sem], along_z(1 - 2 * way))
                )
        self.core(t, 0)

    def core(self, slot, k):
        got = self.slot(slot)
        self.sent.append(send(got, got, self.cs.at[k], self.cr.at[k], other_core()))

    def step(self, step, onward):
        y, x, t = coords()
        slots = [(t - 2 * (1 - 2 * way) * step + 32) % 16 for way in range(2)]
        for i in range(2):
            for way in range(2):
                part = self.part(slots[way], i)
                sem = (way, step - 1, i)
                arrival(part, self.zs.at[sem], self.zr.at[sem]).wait_recv()
                if i in onward[way]:
                    sem = (way, step, i)
                    self.sent.append(
                        send(part, part, self.zs.at[sem], self.zr.at[sem], along_z(1 - 2 * way))
                    )
        for way in range(2):
            self.core(slots[way], 2 * step - 1 + way)

    def finish(self):
        y, x, t = coords()
        far = (t + 8) % 16
        for way in range(2):
            sem = (way, 3, way)
            arrival(self.part(far, way), self.zs.at[sem], self.zr.at[sem]).wait_recv()
        self.core(far, 7)

    def cores(self, some):
        y, x, t = coords()
        for k in some:
            step, way = (k + 1) // 2, (k + 1) % 2
            shift = 8 if k == 7 else 2 * step * (1 - 2 * way)
            got = self.slot((t + 1 - 2 * (t % 2) - shift + 32) % 16)
            arrival(got, self.cs.at[k], self.cr.at[k]).wait_recv()

    def settle(self):
        for copy in self.sent:
            copy.wait_send()


ALL, NONE = ((0, 1), (0, 1)), ((), ())


class Sweep:
    OFFSETS = (0, -1, 1, 2)

    def __init__(self, part, full, sp, rp, ss, rs):
        y, x, t = coords()
        self.sent = []
        self.sp, self.rp, self.ss, self.rs = sp, rp, ss, rs
        self.first, self.then = (along_x, along_y) if part == 0 else (along_y, along_x)
        self.base = 8 * part

        def block(p, s, half=None):
            rng = pl.ds(self.base, 8) if half is None else pl.ds(self.base + 4 * half, 4)
            dy, dx = (s, p) if part == 0 else (p, s)
            return full.at[(y + dy + SIDE) % SIDE, (x + dx + SIDE) % SIDE, rng]

        self.block = block

    def push(self, ref, ssem, rsem, peer):
        self.sent.append(send(ref, ref, ssem, rsem, peer))

    def start(self):
        own = self.block(0, 0)
        for k in range(2):
            self.push(own, self.sp.at[k], self.rp.at[k], self.first(1 - 2 * k))

    def across(self, q):
        own = self.block(self.OFFSETS[q], 0)
        for k in range(2):
            self.push(own, self.ss.at[q, k], self.rs.at[q, k], self.then(1 - 2 * k))

    def relay(self):
        for k in range(2):
            off = 2 * k - 1
            arrival(self.block(off, 0), self.sp.at[k], self.rp.at[k]).wait_recv()
            half = self.block(off, 0, k)
            self.push(half, self.sp.at[2 + k], self.rp.at[2 + k], self.first(1 - 2 * k))

    def relay_across(self, q):
        p = self.OFFSETS[q]
        for k in range(2):
            off = 2 * k - 1
            arrival(self.block(p, off), self.ss.at[q, k], self.rs.at[q, k]).wait_recv()
            half = self.block(p, off, k)
            self.push(half, self.ss.at[q, 2 + k], self.rs.at[q, 2 + k], self.then(1 - 2 * k))

    def far(self):
        for k in range(2):
            arrival(self.block(2, 0, k), self.sp.at[2 + k], self.rp.at[2 + k]).wait_recv()

    def last(self):
        for q in range(4):
            for k in range(2):
                arrival(
                    self.block(self.OFFSETS[q], 2, k), self.ss.at[q, 2 + k], self.rs.at[q, 2 + k]
                ).wait_recv()


def step_kernel(
    tokens, target, bias, near, wq, wk, wv, wo, bv, bo, pv, po, pb,
    nv, no, coef,
    tok16, tgt16, tok, n16, diff, diffs, rows, gqk, gvt, nx, ny, uall,
    bvv, bov, pvv, pov, nearv, biasv,
    pq, pt, rq, rv, accq, accv, qk, vt, probs, mix, full,
    acc1, acc2, err, terr, errt, terrt, bp, ra, rb, sa, sb, qa, qb, done, bt,
    co, rc, sc, rz, tx, vb, gx, gy, cxf, cyf, cxb, cyb, hx, hy, cv, cw, one, two,
    ls, ps, pr, ws, wr, ds, dr, zs, zr, cs, cr, us, ur, vs, vr, xs, xr, ts, tr,
    as_, ar, bs, br, s1, r1, s2, r2, s3, r3, s4, r4, s5, r5, s6, r6, s7, r7, o1, i1, o2, i2,
):
    y, x, t = coords()
    c = t % 2
    z = t // 2
    me = y * SIDE + x
    full_width = 16 * WIDE
    features = 16 * BLOCK
    scale_out = 1.0 / math.sqrt(full_width)
    scale_value = 1.0 / math.sqrt(features)
    factor = loss_gain * full_width / (16 * COUNT)
    entries = 2.0 * features * full_width

    plane = [(i, j) for i in range(SIDE) for j in range(SIDE) if i or j]
    barrier = pltpu.get_barrier_semaphore()
    for i, j in plane:
        pl.semaphore_signal(barrier, inc=1, device_id=at(y + i, x + j, t), device_id_type=MESH)
    for k in range(1, 16):
        pl.semaphore_signal(barrier, inc=1, device_id=along_t(k), device_id_type=MESH)

    some = pl.ds(pl.multiple_of(t * ROWS, ROWS), ROWS)
    far = (t + 8) % 16
    some_far = pl.ds(pl.multiple_of(far * ROWS, ROWS), ROWS)
    left, right = pl.ds(0, WIDE), pl.ds(WIDE, WIDE)
    loads = [
        (tokens.at[some], tok16.at[0]),
        (tokens.at[some_far], tok16.at[1]),
        (target.at[some], tgt16),
        (wq, gqk.at[y, :, left]),
        (wk, gqk.at[y, :, right]),
        (wv, gvt.at[x, :, left]),
        (bv, bvv),
        (tokens, tok),
        (wo, uall.at[t, :, pl.ds(0, BLOCK)]),
        (bo, bov),
        (near, nearv),
        (bias.at[:, 0], biasv.at[0]),
        (bias.at[:, 1], biasv.at[1]),
        (pv, pvv),
        (po, pov),
    ]
    loads = [pltpu.make_async_copy(a, b, ls.at[k]) for k, (a, b) in enumerate(loads)]
    for copy in loads:
        copy.start()

    for copy in loads[:3]:
        copy.wait()
    for i in range(2):
        xf = tok16[i].astype(F32)
        inv = lax.rsqrt(jnp.mean(xf * xf, axis=1, keepdims=True) + epsilon)
        for k in range(16):
            part = tok16[i, :, k * BLOCK : (k + 1) * BLOCK].astype(F32)
            n16[i, k // SIDE, k % SIDE] = (part * inv).astype(BF)
            if i == 0:
                diff[k] = part - tgt16[:, k * BLOCK : (k + 1) * BLOCK].astype(F32)
    pl.semaphore_wait(barrier, 30)

    pieces, weights, others = [], [], []

    def pass_rows(i, slot):
        for j in NEAR:
            src, sem = n16.at[i, :, (x + j) % SIDE], (i, j - 1)
            pieces.append(
                send(src, rows.at[j - 1, slot], ps.at[sem], pr.at[sem], along_x(j))
            )
            src, sem = n16.at[i, (y + j) % SIDE], (i, j + 2)
            pieces.append(
                send(src, rows.at[j + 2, slot], ps.at[sem], pr.at[sem], along_y(j))
            )

    pass_rows(0, t)
    for k in (3, 4, 5, 6):
        loads[k].wait()
    gvt[x, :, WIDE:] = bvv[...].astype(BF)
    lines = (
        (gqk, y, along_y, 0),
        (gvt, x, along_x, 1),
    )

    def pass_weights(held, mine, along, k, way, off, rng, sem):
        ref = held.at[(mine + off + SIDE) % SIDE, rng]
        weights.append(send(ref, ref, ws.at[k, sem], wr.at[k, sem], along(1 - 2 * way)))

    for way in range(2):
        for line in lines:
            pass_weights(*line, way, 0, pl.ds(0, BLOCK), way)
    pass_rows(1, far)
    diffs[me] = diff[me]

    ring = Ring(
        lambda n: rows.at[:, n], lambda n, i: rows.at[pl.ds(3 * i, 3), n], zs, zr, cs, cr
    )
    for copy in pieces[:6]:
        copy.wait_recv()
    ring.start()

    loads[7].wait()

    def normalise(r, _):
        at_r = pl.ds(pl.multiple_of(r * ROWS, ROWS), ROWS)
        xf = tok[at_r].astype(F32)
        inv = lax.rsqrt(jnp.mean(xf * xf, axis=1, keepdims=True) + epsilon)
        for b in range(SIDE):
            cut = pl.ds(pl.multiple_of((b * SIDE + x) * BLOCK, HALF), BLOCK)
            nx[b, at_r] = (tok[at_r, cut].astype(F32) * inv).astype(BF)
            cut = pl.ds(pl.multiple_of((y * SIDE + b) * BLOCK, HALF), BLOCK)
            ny[b, at_r] = (tok[at_r, cut].astype(F32) * inv).astype(BF)
        return 0

    lax.fori_loop(0, COUNT // ROWS, normalise, 0)
    for way in range(2):
        for k, line in enumerate(lines):
            weights[2 * way + k].wait_recv()
            half = pl.ds(way * (BLOCK // 2), BLOCK // 2)
            pass_weights(*line, way, 2 * way - 1, half, 2 + way)
    ring.step(1, ALL)
    loads[8].wait()
    loads[9].wait()
    uall[t, :, BLOCK:] = bov[...].astype(BF)
    ring.step(2, ALL)
    for copy in pieces[6:]:
        copy.wait_recv()
    ring.core(far, 7)
    for copy in weights[4:]:
        copy.wait_recv()

    order = []
    for off in (0, -1, 1, -2, 2, 4, -3, 3):
        base = ((z + off + 8) % 8) * 2
        order += [base + c, base + 1 - c]
    partial = []

    def products(part, lo, hi):
        for w, k0, out, got, along in ((gqk, 0, pq, rq, along_x), (gvt, 3, pt, rv, along_y)):
            total = None
            for b in range(SIDE):
                lhs = jnp.concatenate(
                    [rows[k0 + j, n, b] for j in range(3) for n in order[lo:hi]], axis=0
                )
                more = dot(lhs, w[b])
                total = more if total is None else total + more
            size = (hi - lo) * ROWS
            for j in range(3):
                out[j, lo * ROWS : hi * ROWS] = total[j * size : (j + 1) * size].astype(BF)
            cut = pl.ds(lo * ROWS, size)
            for j in NEAR:
                sem = (part, k0 + j - 1)
                partial.append(
                    send(out.at[j - 1, cut], got.at[j - 1, cut], xs.at[sem], xr.at[sem], along(-j))
                )

    ring.cores((0, 1, 2, 3, 4, 7))
    products(0, 0, 12)
    for lhs, w, acc in ((nx, gqk, accq), (ny, gvt, accv)):
        total = dot(lhs[0], w[0])
        for b in range(1, SIDE):
            total = total + dot(lhs[b], w[b])
        acc[...] = total
    ring.step(3, NONE)
    uring = Ring(
        lambda n: uall.at[n], lambda n, i: uall.at[n, pl.ds(HALF * i, HALF)], us, ur, vs, vr
    )
    uring.start()
    ring.cores((5, 6))
    products(1, 12, 16)
    for copy in partial:
        copy.wait_recv()

    for p, n in enumerate(order):
        at_n = pl.ds(pl.multiple_of(n * ROWS, ROWS), ROWS)
        at_p = slice(p * ROWS, (p + 1) * ROWS)
        total = accq[at_n]
        for j in range(3):
            total = total + rq[j, at_p].astype(F32)
        qk[at_n] = total.astype(BF)
        total = accv[at_n]
        for j in range(3):
            total = total + rv[j, at_p].astype(F32)
        vt[at_n, :WIDE] = total[:, :WIDE].astype(BF)
        vt[at_n, WIDE:] = (total[:, WIDE:] / math.sqrt(features)).astype(BF)

    for k, (i, j) in enumerate(plane):
        yy, xx = (y + i) % SIDE, (x + j) % SIDE
        others.append(
            send(diff.at[yy * SIDE + xx], diffs.at[me], ds.at[k], dr.at[k], (yy * SIDE + xx, t))
        )

    loads[10].wait()
    loads[11].wait()
    loads[12].wait()
    at_row = lax.broadcasted_iota(jnp.int32, (COUNT, COUNT), 0)
    at_col = lax.broadcasted_iota(jnp.int32, (COUNT, COUNT), 1)
    allowed = (nearv[...] == 1) | (jnp.abs(at_row - at_col) <= 1)
    for h in range(2):
        cut = slice(h * HALF, (h + 1) * HALF)
        cut2 = slice(WIDE + h * HALF, WIDE + (h + 1) * HALF)
        scores = dot_t(qk[:, cut], qk[:, cut2]) / math.sqrt(HEAD_DIM) + biasv[h]
        scores = jnp.where(allowed, scores, -jnp.inf)
        e = jnp.exp(scores - jnp.max(scores, axis=1, keepdims=True))
        p = (e / jnp.sum(e, axis=1, keepdims=True)).astype(BF)
        probs[h] = p
        mix[:, cut] = dot(p, vt[:, cut]).astype(BF)
        mix[:, cut2] = dot(p, vt[:, cut2]).astype(BF)

    moved = []
    for k in range(1, 16):
        to = pl.ds(pl.multiple_of(((t + k) % 16) * ROWS, ROWS), ROWS)
        moved.append(send(mix.at[to], full.at[y, x, t], ts.at[k], tr.at[k], along_t(k)))
    full[y, x, t] = mix[some]
    uring.step(1, ALL)
    for copy in moved:
        copy.wait_recv()
    sweeps = [
        Sweep(0, full, as_.at[0], ar.at[0], bs.at[0], br.at[0]),
        Sweep(1, full, as_.at[1], ar.at[1], bs.at[1], br.at[1]),
    ]
    for sweep in sweeps:
        sweep.start()
    for sweep in sweeps:
        sweep.across(0)
    uring.step(2, ALL)
    for sweep in sweeps:
        sweep.relay()
    for sweep in sweeps:
        sweep.across(1)
        sweep.across(2)
    for sweep in sweeps:
        sweep.relay_across(0)
    uring.step(3, ((0,), (1,)))
    for sweep in sweeps:
        sweep.far()
        sweep.across(3)
    for q in (1, 2):
        for sweep in sweeps:
            sweep.relay_across(q)
    uring.finish()
    for sweep in sweeps:
        sweep.relay_across(3)
    uring.cores(range(8))
    for sweep in sweeps:
        sweep.last()

    acc1[...] = jnp.zeros_like(acc1)
    acc2[...] = jnp.zeros_like(acc2)

    def forward(k, _):
        at_k = pl.ds(k * 4, 4)
        parts = [full[:, :, k * 4 + i].reshape(COUNT, 2 * WIDE) for i in range(4)]
        w = uall[at_k].reshape(4 * WIDE, 2 * BLOCK)
        acc1[...] += dot(jnp.concatenate([p[:, :WIDE] for p in parts], axis=1), w)
        acc2[...] += dot(jnp.concatenate([p[:, WIDE:] for p in parts], axis=1), w[:, :BLOCK])
        return 0

    lax.fori_loop(0, 4, forward, 0)
    for copy in others:
        copy.wait_recv()
    err[...] = ((diffs[...].reshape(COUNT, BLOCK) + acc1[:, :BLOCK]) * factor).astype(BF)
    terr[...] = ((acc1[:, BLOCK:] * scale_out + acc2[...]) * factor).astype(BF)

    def backward(n, _):
        part = dot_t(terr[...], uall[n, :, :BLOCK]) + scale_out * dot_t(err[...], uall[n, :, BLOCK:])
        bp[n] = part.astype(BF).reshape(SIDE, SIDE, ROWS, WIDE)
        return 0

    first_b = []
    for part in range(2):
        lax.fori_loop(4 * part, 4 * part + 4, backward, 0)
        lax.fori_loop(8 + 4 * part, 12 + 4 * part, backward, 0)
        low, high, here = pl.ds(4 * part, 4), pl.ds(8 + 4 * part, 4), pl.ds(4 * part, 4)
        for j in NEAR:
            src, sem = bp.at[low, (y + j) % SIDE], (part, 0, j - 1)
            first_b.append(send(src, ra.at[j - 1, here], s1.at[sem], r1.at[sem], along_y(j)))
            src, sem = bp.at[high, :, (x + j) % SIDE], (part, 1, j - 1)
            first_b.append(send(src, rb.at[j - 1, here], s1.at[sem], r1.at[sem], along_x(j)))

    errt[...] = err[...].astype(F32).T.astype(BF)
    terrt[...] = terr[...].astype(F32).T.astype(BF)

    def outer(n, _):
        both = full[:, :, n].reshape(COUNT, 2 * WIDE)
        part = dot(errt[...], both[:, WIDE:]) + dot(terrt[...], both[:, :WIDE])
        co[n // 2, n % 2] = (part * scale_out).astype(BF)
        return 0

    lax.fori_loop(0, 16, outer, 0)
    swapped = send(co.at[:, 1 - c], rc, s7.at[0], r7.at[0], other_core())

    second_b = []
    for part in range(2):
        for copy in first_b[6 * part : 6 * part + 6]:
            copy.wait_recv()
        a, b = 4 * part, 4 * part + 4
        for i in range(SIDE):
            total = bp[a:b, y, i].astype(F32)
            for j in range(3):
                total = total + ra[j, a:b, i].astype(F32)
            sa[i, a:b] = total.astype(BF)
            total = bp[8 + a : 8 + b, i, x].astype(F32)
            for j in range(3):
                total = total + rb[j, a:b, i].astype(F32)
            sb[i, a:b] = total.astype(BF)
        here = pl.ds(a, 4)
        for j in NEAR:
            src, sem = sa.at[(x + j) % SIDE, here], (part, 0, j - 1)
            second_b.append(send(src, qa.at[j - 1, here], s2.at[sem], r2.at[sem], along_x(j)))
            src, sem = sb.at[(y + j) % SIDE, here], (part, 1, j - 1)
            second_b.append(send(src, qb.at[j - 1, here], s2.at[sem], r2.at[sem], along_y(j)))

    swapped.wait_recv()

    def pair(k, _):
        sc[k] = (co[k, c].astype(F32) + rc[k].astype(F32)).astype(BF)
        return 0

    lax.fori_loop(0, 8, pair, 0)
    shares = []

    def pass_on(step):
        for way in range(2):
            sign = 1 - 2 * way
            slot = (z + sign * (4 - step) + 8) % 8
            if step == 0:
                cut = pl.ds(way * (BLOCK // 2), BLOCK // 2)
                src, dst = sc.at[slot, cut], rz.at[way, 0, cut]
            else:
                shares[2 * (step - 1) + way].wait_recv()
                if step == 1:
                    a, b = way * (BLOCK // 2), (way + 1) * (BLOCK // 2)
                    tx[way, 0] = sc[slot]
                    total = sc[slot, a:b].astype(F32) + rz[way, 0, a:b].astype(F32)
                    tx[way, 0, a:b] = total.astype(BF)
                else:
                    total = sc[slot].astype(F32) + rz[way, step - 1].astype(F32)
                    tx[way, step - 1] = total.astype(BF)
                src, dst = tx.at[way, step - 1], rz.at[way, step]
            shares.append(
                send(src, dst, s4.at[way, step], r4.at[way, step], along_z(sign))
            )

    pass_on(0)
    for copy in second_b:
        copy.wait_recv()
    total = sa[x].astype(F32)
    for j in range(3):
        total = total + qa[j].astype(F32)
    done[0:8] = total.astype(BF)
    total = sb[y].astype(F32)
    for j in range(3):
        total = total + qb[j].astype(F32)
    done[8:16] = total.astype(BF)
    third = []
    for k in range(1, 16):
        third.append(send(done.at[(t + k) % 16], bt.at[t], s3.at[k], r3.at[k], along_t(k)))
    bt[t] = done[t]

    pass_on(1)
    for copy in third:
        copy.wait_recv()
    back = bt[...].reshape(COUNT, WIDE).astype(F32).T.astype(BF)
    fourth = []
    for h in range(2):
        vb[h] = dot(back[h * HALF : (h + 1) * HALF], probs[h]).astype(BF)
        got, along = ((gx, along_x), (gy, along_y))[h]
        for j in NEAR:
            fourth.append(
                send(vb.at[h], got.at[j - 1], s5.at[h, j - 1], r5.at[h, j - 1], along(j))
            )
    pass_on(2)
    loads[13].wait()
    loads[14].wait()
    def inner(a1, b1, a2, b2):
        total = jnp.zeros((8, 128), F32)
        for a, b in ((a1, b1), (a2, b2)):
            prod = a[...] * b[...]
            prod = jnp.sum(prod.reshape(prod.shape[0] // 8, 8, prod.shape[1]), axis=0)
            for k in range(prod.shape[1] // 128):
                total = total + prod[:, k * 128 : (k + 1) * 128]
        return jnp.sum(total, axis=0, keepdims=True)

    pairs = ((bvv, bvv, bov, bov), (bvv, pvv, bov, pov), (pvv, pvv, pov, pov))
    for k, args in enumerate(pairs):
        one[t, 3 + k : 4 + k] = inner(*args)
    one[t, 6:8] = jnp.zeros((2, 128), F32)
    for copy in fourth:
        copy.wait_recv()
    fifth = []
    for k in (2, 1, 3, 0):
        for h, own, got, mine, outf, outb, to, along in (
            (0, nx, gx, y, cxf, cxb, hx, along_y),
            (1, ny, gy, x, cyf, cyb, hy, along_x),
        ):
            b = (mine + k) % SIDE
            total = dot(vb[h], own[b])
            for j in range(3):
                total = total + dot(got[j], rows[3 * h + j, :, b].reshape(COUNT, BLOCK))
            total = total * scale_value
            if k == 0:
                outf[...] = total
            else:
                outb[k - 1] = total.astype(BF)
                fifth.append(
                    send(outb.at[k - 1], to.at[k - 1], s6.at[h, k - 1], r6.at[h, k - 1], along(k))
                )
    pass_on(3)
    for copy in fifth:
        copy.wait_recv()
    for h, (own, got) in enumerate(((cxf, hx), (cyf, hy))):
        total = own[...]
        for j in range(3):
            total = total + got[j].astype(F32)
        cv[:, h * HALF : (h + 1) * HALF] = total.T
    for copy in shares[6:]:
        copy.wait_recv()
    total = sc[z].astype(F32)
    for way in range(2):
        total = total + rz[way, 3].astype(F32)
    cw[...] = total.T

    pairs = ((cv, bvv, cw, bov), (cv, cv, cw, cw), (cv, pvv, cw, pov))
    for k, args in enumerate(pairs):
        one[t, k : k + 1] = inner(*args)
    rounds = []
    for k in range(1, 16):
        rounds.append(send(one.at[t], one.at[t], o1.at[k], i1.at[k], along_t(k)))
    for copy in rounds:
        copy.wait_recv()
    two[me] = jnp.sum(one[...], axis=0)
    for k, (i, j) in enumerate(plane):
        peer = at(y + i, x + j, t)
        rounds.append(send(two.at[me], two.at[me], o2.at[k], i2.at[k], peer))
    for copy in rounds[15:]:
        copy.wait_recv()
    sums = jnp.sum(jnp.sum(two[...], axis=0), axis=1, keepdims=True) / entries
    beta_before = pb[0, 0]
    cb, cc, cp, bb, bq, pp = (sums[k : k + 1] for k in range(6))
    alpha = cb
    squares = cc + alpha * alpha * bb + beta_before * beta_before * pp
    squares = squares - 2.0 * (alpha * cb + beta_before * (cp - alpha * bq))
    beta = jnp.sqrt(jnp.maximum(squares, 0.0) + epsilon)
    nv[...] = cv[...] - alpha * bvv[...] - beta_before * pvv[...]
    no[...] = cw[...] - alpha * bov[...] - beta_before * pov[...]
    coef[0:1] = jnp.broadcast_to(alpha, (1, 128))
    coef[1:2] = jnp.broadcast_to(beta, (1, 128))
    coef[2:3] = jnp.broadcast_to(1.0 / beta, (1, 128))
    for copy in (
        pieces + weights + others + partial + moved + first_b + second_b
        + third + [swapped] + shares + fourth + fifth + rounds
    ):
        copy.wait_send()
    ring.settle()
    uring.settle()
    for sweep in sweeps:
        for copy in sweep.sent:
            copy.wait_send()


def scale_kernel(rest_value, rest_out, coef, nv, no, out):
    scale = coef[2:3, 0:1]
    nv[...] = rest_value[...] * scale
    no[...] = rest_out[...] * scale
    out[0] = coef[0, 0]
    out[1] = coef[1, 0]


def body(
    tokens,
    target,
    pair_bias,
    neighbours,
    w_query,
    w_key,
    w_value,
    w_out,
    basis_value,
    basis_out,
    prior_value,
    prior_out,
    prior_beta,
):
    def vm(dtype, *dims):
        return pltpu.VMEM(dims, dtype)

    features = 16 * BLOCK
    scratch = [
        vm(BF, 2, ROWS, features),
        vm(BF, ROWS, features),
        vm(BF, COUNT, features),
        vm(BF, 2, SIDE, SIDE, ROWS, BLOCK),
        vm(F32, 16, ROWS, BLOCK),
        vm(F32, 16, ROWS, BLOCK),
        vm(BF, 6, 16, SIDE, ROWS, BLOCK),
        vm(BF, SIDE, BLOCK, 2 * WIDE),
        vm(BF, SIDE, BLOCK, 2 * WIDE),
        vm(BF, SIDE, COUNT, BLOCK),
        vm(BF, SIDE, COUNT, BLOCK),
        vm(BF, 16, WIDE, 2 * BLOCK),
        vm(F32, BLOCK, WIDE),
        vm(F32, WIDE, BLOCK),
        vm(F32, BLOCK, WIDE),
        vm(F32, WIDE, BLOCK),
        vm(jnp.int32, COUNT, COUNT),
        vm(F32, 2, COUNT, COUNT),
        vm(BF, 3, COUNT, 2 * WIDE),
        vm(BF, 3, COUNT, 2 * WIDE),
        vm(BF, 3, COUNT, 2 * WIDE),
        vm(BF, 3, COUNT, 2 * WIDE),
        vm(F32, COUNT, 2 * WIDE),
        vm(F32, COUNT, 2 * WIDE),
        vm(BF, COUNT, 2 * WIDE),
        vm(BF, COUNT, 2 * WIDE),
        vm(BF, 2, COUNT, COUNT),
        vm(BF, COUNT, 2 * WIDE),
        vm(BF, SIDE, SIDE, 16, ROWS, 2 * WIDE),
        vm(F32, COUNT, 2 * BLOCK),
        vm(F32, COUNT, BLOCK),
        vm(BF, COUNT, BLOCK),
        vm(BF, COUNT, BLOCK),
        vm(BF, BLOCK, COUNT),
        vm(BF, BLOCK, COUNT),
        vm(BF, 16, SIDE, SIDE, ROWS, WIDE),
        vm(BF, 3, 8, SIDE, ROWS, WIDE),
        vm(BF, 3, 8, SIDE, ROWS, WIDE),
        vm(BF, SIDE, 8, ROWS, WIDE),
        vm(BF, SIDE, 8, ROWS, WIDE),
        vm(BF, 3, 8, ROWS, WIDE),
        vm(BF, 3, 8, ROWS, WIDE),
        vm(BF, 16, ROWS, WIDE),
        vm(BF, 16, ROWS, WIDE),
        vm(BF, 8, 2, BLOCK, WIDE),
        vm(BF, 8, BLOCK, WIDE),
        vm(BF, 8, BLOCK, WIDE),
        vm(BF, 2, 4, BLOCK, WIDE),
        vm(BF, 2, 3, BLOCK, WIDE),
        vm(BF, 2, HALF, COUNT),
        vm(BF, 3, HALF, COUNT),
        vm(BF, 3, HALF, COUNT),
        vm(F32, HALF, BLOCK),
        vm(F32, HALF, BLOCK),
        vm(BF, 3, HALF, BLOCK),
        vm(BF, 3, HALF, BLOCK),
        vm(BF, 3, HALF, BLOCK),
        vm(BF, 3, HALF, BLOCK),
        vm(F32, BLOCK, WIDE),
        vm(F32, WIDE, BLOCK),
        vm(F32, 16, 8, 128),
        vm(F32, 16, 8, 128),
        DMA((15,)),
        DMA((2, 6)), DMA((2, 6)),
        DMA((2, 4)), DMA((2, 4)),
        DMA((15,)), DMA((15,)),
        DMA((2, 3, 2)), DMA((2, 3, 2)), DMA((8,)), DMA((8,)),
        DMA((2, 4, 2)), DMA((2, 4, 2)), DMA((8,)), DMA((8,)),
        DMA((2, 6)), DMA((2, 6)),
        DMA((16,)), DMA((16,)),
        DMA((2, 4)), DMA((2, 4)), DMA((2, 4, 4)), DMA((2, 4, 4)),
        DMA((2, 2, 3)), DMA((2, 2, 3)),
        DMA((2, 2, 3)), DMA((2, 2, 3)),
        DMA((16,)), DMA((16,)),
        DMA((2, 4)), DMA((2, 4)),
        DMA((2, 3)), DMA((2, 3)),
        DMA((2, 3)), DMA((2, 3)),
        DMA((1,)), DMA((1,)),
        DMA((16,)), DMA((16,)), DMA((15,)), DMA((15,)),
    ]
    rest_value, rest_out, coef = pl.pallas_call(
        step_kernel,
        out_shape=(
            jax.ShapeDtypeStruct((BLOCK, WIDE), F32),
            jax.ShapeDtypeStruct((WIDE, BLOCK), F32),
            jax.ShapeDtypeStruct((8, 128), F32),
        ),
        in_specs=[ANY] * 12 + [SMEM],
        out_specs=(VMEM, VMEM, VMEM),
        scratch_shapes=scratch,
        compiler_params=pltpu.CompilerParams(
            collective_id=0, has_side_effects=True, vmem_limit_bytes=58 * 2**20
        ),
    )(
        tokens,
        target,
        pair_bias,
        neighbours,
        w_query,
        w_key,
        w_value,
        w_out,
        basis_value,
        basis_out,
        prior_value,
        prior_out,
        prior_beta.reshape(1, 1),
    )
    return pl.pallas_call(
        scale_kernel,
        out_shape=(
            jax.ShapeDtypeStruct((BLOCK, WIDE), F32),
            jax.ShapeDtypeStruct((WIDE, BLOCK), F32),
            jax.ShapeDtypeStruct((2,), F32),
        ),
        in_specs=[VMEM] * 3,
        out_specs=(VMEM, VMEM, SMEM),
    )(rest_value, rest_out, coef)


def solution(mesh):
    placed = (
        P("dp", None),
        P("dp", None),
        P("dp", "tensor", None),
        P("dp", None),
        P("dp", "tensor"),
        P("dp", "tensor"),
        P("dp", "tensor"),
        P("tensor", "dp"),
        P("dp", "tensor"),
        P("tensor", "dp"),
        P("dp", "tensor"),
        P("tensor", "dp"),
        P(),
    )
    return jax.shard_map(
        body,
        mesh=mesh,
        in_specs=placed,
        out_specs=(P("dp", "tensor"), P("tensor", "dp"), P()),
        check_vma=False,
    )
```

```python
import math

import jax
import jax.numpy as jnp
from jax import lax
from jax.experimental import pallas as pl
from jax.experimental.pallas import tpu as pltpu
from jax.sharding import PartitionSpec as P

HEAD_DIM = 128
SIDE = 4
ROWS = 16

loss_gain = 32.0
epsilon = 1e-06

MESH = pl.DeviceIdType.MESH
BF = jnp.bfloat16
F32 = jnp.float32
VMEM = pl.BlockSpec(memory_space=pltpu.VMEM)
ANY = pl.BlockSpec(memory_space=pl.ANY)
SMEM = pl.BlockSpec(memory_space=pltpu.SMEM)
DMA = pltpu.SemaphoreType.DMA


def coords():
    dp = lax.axis_index("dp")
    t = lax.axis_index("tensor")
    return dp // SIDE, dp % SIDE, t


def at(y, x, t):
    return (((y + 2 * SIDE) % SIDE) * SIDE + (x + 2 * SIDE) % SIDE, (t + 32) % 16)


def along_x(j):
    y, x, t = coords()
    return at(y, x + j, t)


def along_y(j):
    y, x, t = coords()
    return at(y + j, x, t)


def along_t(k):
    y, x, t = coords()
    return at(y, x, t + k)


def along_z(k):
    y, x, t = coords()
    return at(y, x, t + 2 * k)


def other_core():
    y, x, t = coords()
    return at(y, x, t + 1 - 2 * (t % 2))


def greet(peers):
    barrier = pltpu.get_barrier_semaphore()
    for peer in peers:
        pl.semaphore_signal(barrier, inc=1, device_id=peer, device_id_type=MESH)
    pl.semaphore_wait(barrier, len(peers))


def send(src, dst, ssem, rsem, peer):
    copy = pltpu.make_async_remote_copy(
        src_ref=src,
        dst_ref=dst,
        send_sem=ssem,
        recv_sem=rsem,
        device_id=peer,
        device_id_type=MESH,
    )
    copy.start()
    return copy


NEAR = (1, 3, 2)
WIDE = 256
HALF = 128
BLOCK = 384
COUNT = 256


def dot(a, b):
    return jnp.dot(a, b, preferred_element_type=F32)


def dot_t(a, b):
    return lax.dot_general(a, b, (((1,), (1,)), ((), ())), preferred_element_type=F32)


def arrival(ref, ssem, rsem):
    y, x, t = coords()
    return pltpu.make_async_remote_copy(
        src_ref=ref,
        dst_ref=ref,
        send_sem=ssem,
        recv_sem=rsem,
        device_id=at(y, x, t + 2),
        device_id_type=MESH,
    )


class Ring:
    def __init__(self, slot, part, zs, zr, cs, cr):
        self.slot, self.part = slot, part
        self.zs, self.zr, self.cs, self.cr = zs, zr, cs, cr
        self.sent = []

    def start(self):
        y, x, t = coords()
        for i in range(2):
            own = self.part(t, i)
            for way in range(2):
                sem = (way, 0, i)
                self.sent.append(
                    send(own, own, self.zs.at[sem], self.zr.at[sem], along_z(1 - 2 * way))
                )
        self.core(t, 0)

    def core(self, slot, k):
        got = self.slot(slot)
        self.sent.append(send(got, got, self.cs.at[k], self.cr.at[k], other_core()))

    def step(self, step, onward):
        y, x, t = coords()
        slots = [(t - 2 * (1 - 2 * way) * step + 32) % 16 for way in range(2)]
        for i in range(2):
            for way in range(2):
                part = self.part(slots[way], i)
                sem = (way, step - 1, i)
                arrival(part, self.zs.at[sem], self.zr.at[sem]).wait_recv()
                if i in onward[way]:
                    sem = (way, step, i)
                    self.sent.append(
                        send(part, part, self.zs.at[sem], self.zr.at[sem], along_z(1 - 2 * way))
                    )
        for way in range(2):
            self.core(slots[way], 2 * step - 1 + way)

    def finish(self):
        y, x, t = coords()
        far = (t + 8) % 16
        for way in range(2):
            sem = (way, 3, way)
            arrival(self.part(far, way), self.zs.at[sem], self.zr.at[sem]).wait_recv()
        self.core(far, 7)

    def cores(self, some):
        y, x, t = coords()
        for k in some:
            step, way = (k + 1) // 2, (k + 1) % 2
            shift = 8 if k == 7 else 2 * step * (1 - 2 * way)
            got = self.slot((t + 1 - 2 * (t % 2) - shift + 32) % 16)
            arrival(got, self.cs.at[k], self.cr.at[k]).wait_recv()

    def settle(self):
        for copy in self.sent:
            copy.wait_send()


ALL, NONE = ((0, 1), (0, 1)), ((), ())


class Sweep:
    OFFSETS = (0, -1, 1, 2)

    def __init__(self, part, full, sp, rp, ss, rs):
        y, x, t = coords()
        self.sent = []
        self.sp, self.rp, self.ss, self.rs = sp, rp, ss, rs
        self.first, self.then = (along_x, along_y) if part == 0 else (along_y, along_x)
        self.base = 8 * part

        def block(p, s, half=None):
            rng = pl.ds(self.base, 8) if half is None else pl.ds(self.base + 4 * half, 4)
            dy, dx = (s, p) if part == 0 else (p, s)
            return full.at[(y + dy + SIDE) % SIDE, (x + dx + SIDE) % SIDE, rng]

        self.block = block

    def push(self, ref, ssem, rsem, peer):
        self.sent.append(send(ref, ref, ssem, rsem, peer))

    def start(self):
        own = self.block(0, 0)
        for k in range(2):
            self.push(own, self.sp.at[k], self.rp.at[k], self.first(1 - 2 * k))

    def across(self, q):
        own = self.block(self.OFFSETS[q], 0)
        for k in range(2):
            self.push(own, self.ss.at[q, k], self.rs.at[q, k], self.then(1 - 2 * k))

    def relay(self):
        for k in range(2):
            off = 2 * k - 1
            arrival(self.block(off, 0), self.sp.at[k], self.rp.at[k]).wait_recv()
            half = self.block(off, 0, k)
            self.push(half, self.sp.at[2 + k], self.rp.at[2 + k], self.first(1 - 2 * k))

    def relay_across(self, q):
        p = self.OFFSETS[q]
        for k in range(2):
            off = 2 * k - 1
            arrival(self.block(p, off), self.ss.at[q, k], self.rs.at[q, k]).wait_recv()
            half = self.block(p, off, k)
            self.push(half, self.ss.at[q, 2 + k], self.rs.at[q, 2 + k], self.then(1 - 2 * k))

    def far(self):
        for k in range(2):
            arrival(self.block(2, 0, k), self.sp.at[2 + k], self.rp.at[2 + k]).wait_recv()

    def last(self):
        for q in range(4):
            for k in range(2):
                arrival(
                    self.block(self.OFFSETS[q], 2, k), self.ss.at[q, 2 + k], self.rs.at[q, 2 + k]
                ).wait_recv()


def step_kernel(
    tokens, target, bias, near, wq, wk, wv, wo, bv, bo, pv, po, pb,
    nv, no, coef,
    tok16, tgt16, tok, n16, diff, diffs, rows, gqk, gvt, nx, ny, uall,
    bvv, bov, pvv, pov, nearv, biasv,
    pq, pt, rq, rv, accq, accv, qk, vt, probs, mix, full,
    acc1, acc2, err, terr, errt, terrt, bp, ra, rb, sa, sb, qa, qb, done, bt,
    co, rc, sc, rz, tx, vb, gx, gy, cxf, cyf, cxb, cyb, hx, hy, cv, cw, one, two,
    ls, ps, pr, ws, wr, ds, dr, zs, zr, cs, cr, us, ur, vs, vr, xs, xr, ts, tr,
    as_, ar, bs, br, s1, r1, s2, r2, s3, r3, s4, r4, s5, r5, s6, r6, s7, r7, o1, i1, o2, i2,
):
    y, x, t = coords()
    c = t % 2
    z = t // 2
    me = y * SIDE + x
    full_width = 16 * WIDE
    features = 16 * BLOCK
    scale_out = 1.0 / math.sqrt(full_width)
    scale_value = 1.0 / math.sqrt(features)
    factor = loss_gain * full_width / (16 * COUNT)
    entries = 2.0 * features * full_width

    plane = [(i, j) for i in range(SIDE) for j in range(SIDE) if i or j]
    barrier = pltpu.get_barrier_semaphore()
    for i, j in plane:
        pl.semaphore_signal(barrier, inc=1, device_id=at(y + i, x + j, t), device_id_type=MESH)
    for k in range(1, 16):
        pl.semaphore_signal(barrier, inc=1, device_id=along_t(k), device_id_type=MESH)

    some = pl.ds(pl.multiple_of(t * ROWS, ROWS), ROWS)
    far = (t + 8) % 16
    some_far = pl.ds(pl.multiple_of(far * ROWS, ROWS), ROWS)
    left, right = pl.ds(0, WIDE), pl.ds(WIDE, WIDE)
    loads = [
        (tokens.at[some], tok16.at[0]),
        (tokens.at[some_far], tok16.at[1]),
        (target.at[some], tgt16),
        (wq, gqk.at[y, :, left]),
        (wk, gqk.at[y, :, right]),
        (wv, gvt.at[x, :, left]),
        (bv, bvv),
        (tokens, tok),
        (wo, uall.at[t, :, pl.ds(0, BLOCK)]),
        (bo, bov),
        (near, nearv),
        (bias.at[:, 0], biasv.at[0]),
        (bias.at[:, 1], biasv.at[1]),
        (pv, pvv),
        (po, pov),
    ]
    loads = [pltpu.make_async_copy(a, b, ls.at[k]) for k, (a, b) in enumerate(loads)]
    for copy in loads:
        copy.start()

    for copy in loads[:3]:
        copy.wait()
    for i in range(2):
        xf = tok16[i].astype(F32)
        inv = lax.rsqrt(jnp.mean(xf * xf, axis=1, keepdims=True) + epsilon)
        for k in range(16):
            part = tok16[i, :, k * BLOCK : (k + 1) * BLOCK].astype(F32)
            n16[i, k // SIDE, k % SIDE] = (part * inv).astype(BF)
            if i == 0:
                diff[k] = part - tgt16[:, k * BLOCK : (k + 1) * BLOCK].astype(F32)
    pl.semaphore_wait(barrier, 30)

    pieces, weights, others = [], [], []

    def pass_rows(i, slot):
        for j in NEAR:
            src, sem = n16.at[i, :, (x + j) % SIDE], (i, j - 1)
            pieces.append(
                send(src, rows.at[j - 1, slot], ps.at[sem], pr.at[sem], along_x(j))
            )
            src, sem = n16.at[i, (y + j) % SIDE], (i, j + 2)
            pieces.append(
                send(src, rows.at[j + 2, slot], ps.at[sem], pr.at[sem], along_y(j))
            )

    pass_rows(0, t)
    for k in (3, 4, 5, 6):
        loads[k].wait()
    gvt[x, :, WIDE:] = bvv[...].astype(BF)
    lines = (
        (gqk, y, along_y, 0),
        (gvt, x, along_x, 1),
    )

    def pass_weights(held, mine, along, k, way, off, rng, sem):
        ref = held.at[(mine + off + SIDE) % SIDE, rng]
        weights.append(send(ref, ref, ws.at[k, sem], wr.at[k, sem], along(1 - 2 * way)))

    for way in range(2):
        for line in lines:
            pass_weights(*line, way, 0, pl.ds(0, BLOCK), way)
    pass_rows(1, far)
    diffs[me] = diff[me]

    ring = Ring(
        lambda n: rows.at[:, n], lambda n, i: rows.at[pl.ds(3 * i, 3), n], zs, zr, cs, cr
    )
    for copy in pieces[:6]:
        copy.wait_recv()
    ring.start()

    loads[7].wait()

    def normalise(r, _):
        at_r = pl.ds(pl.multiple_of(r * ROWS, ROWS), ROWS)
        xf = tok[at_r].astype(F32)
        inv = lax.rsqrt(jnp.mean(xf * xf, axis=1, keepdims=True) + epsilon)
        for b in range(SIDE):
            cut = pl.ds(pl.multiple_of((b * SIDE + x) * BLOCK, HALF), BLOCK)
            nx[b, at_r] = (tok[at_r, cut].astype(F32) * inv).astype(BF)
            cut = pl.ds(pl.multiple_of((y * SIDE + b) * BLOCK, HALF), BLOCK)
            ny[b, at_r] = (tok[at_r, cut].astype(F32) * inv).astype(BF)
        return 0

    lax.fori_loop(0, COUNT // ROWS, normalise, 0)
    for way in range(2):
        for k, line in enumerate(lines):
            weights[2 * way + k].wait_recv()
            half = pl.ds(way * (BLOCK // 2), BLOCK // 2)
            pass_weights(*line, way, 2 * way - 1, half, 2 + way)
    ring.step(1, ALL)
    loads[8].wait()
    loads[9].wait()
    uall[t, :, BLOCK:] = bov[...].astype(BF)
    ring.step(2, ALL)
    for copy in pieces[6:]:
        copy.wait_recv()
    ring.core(far, 7)
    for copy in weights[4:]:
        copy.wait_recv()

    order = []
    for off in (0, -1, 1, 4, -2, 2, -3, 3):
        base = ((z + off + 8) % 8) * 2
        order += [base + c, base + 1 - c]
    partial = []

    def products(part, lo, hi):
        for w, k0, out, got, along in ((gqk, 0, pq, rq, along_x), (gvt, 3, pt, rv, along_y)):
            total = None
            for b in range(SIDE):
                lhs = jnp.concatenate(
                    [rows[k0 + j, n, b] for j in range(3) for n in order[lo:hi]], axis=0
                )
                more = dot(lhs, w[b])
                total = more if total is None else total + more
            size = (hi - lo) * ROWS
            for j in range(3):
                out[j, lo * ROWS : hi * ROWS] = total[j * size : (j + 1) * size].astype(BF)
            cut = pl.ds(lo * ROWS, size)
            for j in NEAR:
                sem = (part, k0 + j - 1)
                partial.append(
                    send(out.at[j - 1, cut], got.at[j - 1, cut], xs.at[sem], xr.at[sem], along(-j))
                )

    ring.cores((0, 1, 2, 7))
    products(0, 0, 8)
    ring.cores((3, 4))
    products(1, 8, 12)
    for lhs, w, acc in ((nx, gqk, accq), (ny, gvt, accv)):
        total = dot(lhs[0], w[0])
        for b in range(1, SIDE):
            total = total + dot(lhs[b], w[b])
        acc[...] = total
    ring.step(3, NONE)
    uring = Ring(
        lambda n: uall.at[n], lambda n, i: uall.at[n, pl.ds(HALF * i, HALF)], us, ur, vs, vr
    )
    uring.start()
    ring.cores((5, 6))
    products(2, 12, 16)
    for copy in partial:
        copy.wait_recv()

    for p, n in enumerate(order):
        at_n = pl.ds(pl.multiple_of(n * ROWS, ROWS), ROWS)
        at_p = slice(p * ROWS, (p + 1) * ROWS)
        total = accq[at_n]
        for j in range(3):
            total = total + rq[j, at_p].astype(F32)
        qk[at_n] = total.astype(BF)
        total = accv[at_n]
        for j in range(3):
            total = total + rv[j, at_p].astype(F32)
        vt[at_n, :WIDE] = total[:, :WIDE].astype(BF)
        vt[at_n, WIDE:] = (total[:, WIDE:] / math.sqrt(features)).astype(BF)

    for k, (i, j) in enumerate(plane):
        yy, xx = (y + i) % SIDE, (x + j) % SIDE
        others.append(
            send(diff.at[yy * SIDE + xx], diffs.at[me], ds.at[k], dr.at[k], (yy * SIDE + xx, t))
        )

    loads[10].wait()
    loads[11].wait()
    loads[12].wait()
    at_row = lax.broadcasted_iota(jnp.int32, (COUNT, COUNT), 0)
    at_col = lax.broadcasted_iota(jnp.int32, (COUNT, COUNT), 1)
    allowed = (nearv[...] == 1) | (jnp.abs(at_row - at_col) <= 1)
    for h in range(2):
        cut = slice(h * HALF, (h + 1) * HALF)
        cut2 = slice(WIDE + h * HALF, WIDE + (h + 1) * HALF)
        scores = dot_t(qk[:, cut], qk[:, cut2]) / math.sqrt(HEAD_DIM) + biasv[h]
        scores = jnp.where(allowed, scores, -jnp.inf)
        e = jnp.exp(scores - jnp.max(scores, axis=1, keepdims=True))
        p = (e / jnp.sum(e, axis=1, keepdims=True)).astype(BF)
        probs[h] = p
        mix[:, cut] = dot(p, vt[:, cut]).astype(BF)
        mix[:, cut2] = dot(p, vt[:, cut2]).astype(BF)

    moved = []
    for k in range(1, 16):
        to = pl.ds(pl.multiple_of(((t + k) % 16) * ROWS, ROWS), ROWS)
        moved.append(send(mix.at[to], full.at[y, x, t], ts.at[k], tr.at[k], along_t(k)))
    full[y, x, t] = mix[some]
    uring.step(1, ALL)
    for copy in moved:
        copy.wait_recv()
    sweeps = [
        Sweep(0, full, as_.at[0], ar.at[0], bs.at[0], br.at[0]),
        Sweep(1, full, as_.at[1], ar.at[1], bs.at[1], br.at[1]),
    ]
    for sweep in sweeps:
        sweep.start()
    for sweep in sweeps:
        sweep.across(0)
    uring.step(2, ALL)
    for sweep in sweeps:
        sweep.relay()
    for sweep in sweeps:
        sweep.across(1)
        sweep.across(2)
    for sweep in sweeps:
        sweep.relay_across(0)
    uring.step(3, ((0,), (1,)))
    for sweep in sweeps:
        sweep.far()
        sweep.across(3)
    for q in (1, 2):
        for sweep in sweeps:
            sweep.relay_across(q)
    uring.finish()
    for sweep in sweeps:
        sweep.relay_across(3)
    uring.cores(range(8))
    for sweep in sweeps:
        sweep.last()

    acc1[...] = jnp.zeros_like(acc1)
    acc2[...] = jnp.zeros_like(acc2)

    def forward(k, _):
        at_k = pl.ds(k * 4, 4)
        parts = [full[:, :, k * 4 + i].reshape(COUNT, 2 * WIDE) for i in range(4)]
        w = uall[at_k].reshape(4 * WIDE, 2 * BLOCK)
        acc1[...] += dot(jnp.concatenate([p[:, :WIDE] for p in parts], axis=1), w)
        acc2[...] += dot(jnp.concatenate([p[:, WIDE:] for p in parts], axis=1), w[:, :BLOCK])
        return 0

    lax.fori_loop(0, 4, forward, 0)
    for copy in others:
        copy.wait_recv()
    err[...] = ((diffs[...].reshape(COUNT, BLOCK) + acc1[:, :BLOCK]) * factor).astype(BF)
    terr[...] = ((acc1[:, BLOCK:] * scale_out + acc2[...]) * factor).astype(BF)

    def backward(n, _):
        part = dot_t(terr[...], uall[n, :, :BLOCK]) + scale_out * dot_t(err[...], uall[n, :, BLOCK:])
        bp[n] = part.astype(BF).reshape(SIDE, SIDE, ROWS, WIDE)
        return 0

    first_b = []
    cuts = ((0, 3), (3, 8))
    for part, (a, b) in enumerate(cuts):
        here = pl.ds(a, b - a)
        lax.fori_loop(a, b, backward, 0)
        for j in NEAR:
            src, sem = bp.at[here, (y + j) % SIDE], (part, 0, j - 1)
            first_b.append(send(src, ra.at[j - 1, here], s1.at[sem], r1.at[sem], along_y(j)))
        lax.fori_loop(8 + a, 8 + b, backward, 0)
        for j in NEAR:
            src, sem = bp.at[pl.ds(8 + a, b - a), :, (x + j) % SIDE], (part, 1, j - 1)
            first_b.append(send(src, rb.at[j - 1, here], s1.at[sem], r1.at[sem], along_x(j)))

    errt[...] = err[...].astype(F32).T.astype(BF)
    terrt[...] = terr[...].astype(F32).T.astype(BF)

    def outer(n, _):
        both = full[:, :, n].reshape(COUNT, 2 * WIDE)
        part = dot(errt[...], both[:, WIDE:]) + dot(terrt[...], both[:, :WIDE])
        co[n // 2, n % 2] = (part * scale_out).astype(BF)
        return 0

    lax.fori_loop(0, 16, outer, 0)
    swapped = send(co.at[:, 1 - c], rc, s7.at[0], r7.at[0], other_core())

    second_b = []
    for part, (a, b) in enumerate(cuts):
        for copy in first_b[6 * part : 6 * part + 6]:
            copy.wait_recv()
        for i in range(SIDE):
            total = bp[a:b, y, i].astype(F32)
            for j in range(3):
                total = total + ra[j, a:b, i].astype(F32)
            sa[i, a:b] = total.astype(BF)
            total = bp[8 + a : 8 + b, i, x].astype(F32)
            for j in range(3):
                total = total + rb[j, a:b, i].astype(F32)
            sb[i, a:b] = total.astype(BF)
        here = pl.ds(a, b - a)
        for j in NEAR:
            src, sem = sa.at[(x + j) % SIDE, here], (part, 0, j - 1)
            second_b.append(send(src, qa.at[j - 1, here], s2.at[sem], r2.at[sem], along_x(j)))
            src, sem = sb.at[(y + j) % SIDE, here], (part, 1, j - 1)
            second_b.append(send(src, qb.at[j - 1, here], s2.at[sem], r2.at[sem], along_y(j)))

    swapped.wait_recv()

    def pair(k, _):
        sc[k] = (co[k, c].astype(F32) + rc[k].astype(F32)).astype(BF)
        return 0

    lax.fori_loop(0, 8, pair, 0)
    shares = []

    def pass_on(step):
        for way in range(2):
            sign = 1 - 2 * way
            slot = (z + sign * (4 - step) + 8) % 8
            if step == 0:
                cut = pl.ds(way * (BLOCK // 2), BLOCK // 2)
                src, dst = sc.at[slot, cut], rz.at[way, 0, cut]
            else:
                shares[2 * (step - 1) + way].wait_recv()
                if step == 1:
                    a, b = way * (BLOCK // 2), (way + 1) * (BLOCK // 2)
                    tx[way, 0] = sc[slot]
                    total = sc[slot, a:b].astype(F32) + rz[way, 0, a:b].astype(F32)
                    tx[way, 0, a:b] = total.astype(BF)
                else:
                    total = sc[slot].astype(F32) + rz[way, step - 1].astype(F32)
                    tx[way, step - 1] = total.astype(BF)
                src, dst = tx.at[way, step - 1], rz.at[way, step]
            shares.append(
                send(src, dst, s4.at[way, step], r4.at[way, step], along_z(sign))
            )

    pass_on(0)
    for copy in second_b:
        copy.wait_recv()
    total = sa[x].astype(F32)
    for j in range(3):
        total = total + qa[j].astype(F32)
    done[0:8] = total.astype(BF)
    total = sb[y].astype(F32)
    for j in range(3):
        total = total + qb[j].astype(F32)
    done[8:16] = total.astype(BF)
    third = []
    for k in range(1, 16):
        third.append(send(done.at[(t + k) % 16], bt.at[t], s3.at[k], r3.at[k], along_t(k)))
    bt[t] = done[t]

    pass_on(1)
    for copy in third:
        copy.wait_recv()
    back = bt[...].reshape(COUNT, WIDE).astype(F32).T.astype(BF)
    fourth = []
    for h in range(2):
        vb[h] = dot(back[h * HALF : (h + 1) * HALF], probs[h]).astype(BF)
        got, along = ((gx, along_x), (gy, along_y))[h]
        for j in NEAR:
            fourth.append(
                send(vb.at[h], got.at[j - 1], s5.at[h, j - 1], r5.at[h, j - 1], along(j))
            )
    pass_on(2)
    loads[13].wait()
    loads[14].wait()
    def inner(a1, b1, a2, b2):
        total = jnp.zeros((8, 128), F32)
        for a, b in ((a1, b1), (a2, b2)):
            prod = a[...] * b[...]
            prod = jnp.sum(prod.reshape(prod.shape[0] // 8, 8, prod.shape[1]), axis=0)
            for k in range(prod.shape[1] // 128):
                total = total + prod[:, k * 128 : (k + 1) * 128]
        return jnp.sum(total, axis=0, keepdims=True)

    pairs = ((bvv, bvv, bov, bov), (bvv, pvv, bov, pov), (pvv, pvv, pov, pov))
    for k, args in enumerate(pairs):
        one[t, 3 + k : 4 + k] = inner(*args)
    one[t, 6:8] = jnp.zeros((2, 128), F32)
    for copy in fourth:
        copy.wait_recv()
    fifth = []
    for k in (2, 1, 3, 0):
        for h, own, got, mine, outf, outb, to, along in (
            (0, nx, gx, y, cxf, cxb, hx, along_y),
            (1, ny, gy, x, cyf, cyb, hy, along_x),
        ):
            b = (mine + k) % SIDE
            total = dot(vb[h], own[b])
            for j in range(3):
                total = total + dot(got[j], rows[3 * h + j, :, b].reshape(COUNT, BLOCK))
            total = total * scale_value
            if k == 0:
                outf[...] = total
            else:
                outb[k - 1] = total.astype(BF)
                fifth.append(
                    send(outb.at[k - 1], to.at[k - 1], s6.at[h, k - 1], r6.at[h, k - 1], along(k))
                )
    pass_on(3)
    for copy in fifth:
        copy.wait_recv()
    for h, (own, got) in enumerate(((cxf, hx), (cyf, hy))):
        total = own[...]
        for j in range(3):
            total = total + got[j].astype(F32)
        cv[:, h * HALF : (h + 1) * HALF] = total.T
    for copy in shares[6:]:
        copy.wait_recv()
    total = sc[z].astype(F32)
    for way in range(2):
        total = total + rz[way, 3].astype(F32)
    cw[...] = total.T

    pairs = ((cv, bvv, cw, bov), (cv, cv, cw, cw), (cv, pvv, cw, pov))
    for k, args in enumerate(pairs):
        one[t, k : k + 1] = inner(*args)
    rounds = []
    for k in range(1, 16):
        rounds.append(send(one.at[t], one.at[t], o1.at[k], i1.at[k], along_t(k)))
    for copy in rounds:
        copy.wait_recv()
    two[me] = jnp.sum(one[...], axis=0)
    for k, (i, j) in enumerate(plane):
        peer = at(y + i, x + j, t)
        rounds.append(send(two.at[me], two.at[me], o2.at[k], i2.at[k], peer))
    for copy in rounds[15:]:
        copy.wait_recv()
    sums = jnp.sum(jnp.sum(two[...], axis=0), axis=1, keepdims=True) / entries
    beta_before = pb[0, 0]
    cb, cc, cp, bb, bq, pp = (sums[k : k + 1] for k in range(6))
    alpha = cb
    squares = cc + alpha * alpha * bb + beta_before * beta_before * pp
    squares = squares - 2.0 * (alpha * cb + beta_before * (cp - alpha * bq))
    beta = jnp.sqrt(jnp.maximum(squares, 0.0) + epsilon)
    nv[...] = cv[...] - alpha * bvv[...] - beta_before * pvv[...]
    no[...] = cw[...] - alpha * bov[...] - beta_before * pov[...]
    coef[0:1] = jnp.broadcast_to(alpha, (1, 128))
    coef[1:2] = jnp.broadcast_to(beta, (1, 128))
    coef[2:3] = jnp.broadcast_to(1.0 / beta, (1, 128))
    for copy in (
        pieces + weights + others + partial + moved + first_b + second_b
        + third + [swapped] + shares + fourth + fifth + rounds
    ):
        copy.wait_send()
    ring.settle()
    uring.settle()
    for sweep in sweeps:
        for copy in sweep.sent:
            copy.wait_send()


def scale_kernel(rest_value, rest_out, coef, nv, no, out):
    scale = coef[2:3, 0:1]
    nv[...] = rest_value[...] * scale
    no[...] = rest_out[...] * scale
    out[0] = coef[0, 0]
    out[1] = coef[1, 0]


def body(
    tokens,
    target,
    pair_bias,
    neighbours,
    w_query,
    w_key,
    w_value,
    w_out,
    basis_value,
    basis_out,
    prior_value,
    prior_out,
    prior_beta,
):
    def vm(dtype, *dims):
        return pltpu.VMEM(dims, dtype)

    features = 16 * BLOCK
    scratch = [
        vm(BF, 2, ROWS, features),
        vm(BF, ROWS, features),
        vm(BF, COUNT, features),
        vm(BF, 2, SIDE, SIDE, ROWS, BLOCK),
        vm(F32, 16, ROWS, BLOCK),
        vm(F32, 16, ROWS, BLOCK),
        vm(BF, 6, 16, SIDE, ROWS, BLOCK),
        vm(BF, SIDE, BLOCK, 2 * WIDE),
        vm(BF, SIDE, BLOCK, 2 * WIDE),
        vm(BF, SIDE, COUNT, BLOCK),
        vm(BF, SIDE, COUNT, BLOCK),
        vm(BF, 16, WIDE, 2 * BLOCK),
        vm(F32, BLOCK, WIDE),
        vm(F32, WIDE, BLOCK),
        vm(F32, BLOCK, WIDE),
        vm(F32, WIDE, BLOCK),
        vm(jnp.int32, COUNT, COUNT),
        vm(F32, 2, COUNT, COUNT),
        vm(BF, 3, COUNT, 2 * WIDE),
        vm(BF, 3, COUNT, 2 * WIDE),
        vm(BF, 3, COUNT, 2 * WIDE),
        vm(BF, 3, COUNT, 2 * WIDE),
        vm(F32, COUNT, 2 * WIDE),
        vm(F32, COUNT, 2 * WIDE),
        vm(BF, COUNT, 2 * WIDE),
        vm(BF, COUNT, 2 * WIDE),
        vm(BF, 2, COUNT, COUNT),
        vm(BF, COUNT, 2 * WIDE),
        vm(BF, SIDE, SIDE, 16, ROWS, 2 * WIDE),
        vm(F32, COUNT, 2 * BLOCK),
        vm(F32, COUNT, BLOCK),
        vm(BF, COUNT, BLOCK),
        vm(BF, COUNT, BLOCK),
        vm(BF, BLOCK, COUNT),
        vm(BF, BLOCK, COUNT),
        vm(BF, 16, SIDE, SIDE, ROWS, WIDE),
        vm(BF, 3, 8, SIDE, ROWS, WIDE),
        vm(BF, 3, 8, SIDE, ROWS, WIDE),
        vm(BF, SIDE, 8, ROWS, WIDE),
        vm(BF, SIDE, 8, ROWS, WIDE),
        vm(BF, 3, 8, ROWS, WIDE),
        vm(BF, 3, 8, ROWS, WIDE),
        vm(BF, 16, ROWS, WIDE),
        vm(BF, 16, ROWS, WIDE),
        vm(BF, 8, 2, BLOCK, WIDE),
        vm(BF, 8, BLOCK, WIDE),
        vm(BF, 8, BLOCK, WIDE),
        vm(BF, 2, 4, BLOCK, WIDE),
        vm(BF, 2, 3, BLOCK, WIDE),
        vm(BF, 2, HALF, COUNT),
        vm(BF, 3, HALF, COUNT),
        vm(BF, 3, HALF, COUNT),
        vm(F32, HALF, BLOCK),
        vm(F32, HALF, BLOCK),
        vm(BF, 3, HALF, BLOCK),
        vm(BF, 3, HALF, BLOCK),
        vm(BF, 3, HALF, BLOCK),
        vm(BF, 3, HALF, BLOCK),
        vm(F32, BLOCK, WIDE),
        vm(F32, WIDE, BLOCK),
        vm(F32, 16, 8, 128),
        vm(F32, 16, 8, 128),
        DMA((15,)),
        DMA((2, 6)), DMA((2, 6)),
        DMA((2, 4)), DMA((2, 4)),
        DMA((15,)), DMA((15,)),
        DMA((2, 3, 2)), DMA((2, 3, 2)), DMA((8,)), DMA((8,)),
        DMA((2, 4, 2)), DMA((2, 4, 2)), DMA((8,)), DMA((8,)),
        DMA((3, 6)), DMA((3, 6)),
        DMA((16,)), DMA((16,)),
        DMA((2, 4)), DMA((2, 4)), DMA((2, 4, 4)), DMA((2, 4, 4)),
        DMA((2, 2, 3)), DMA((2, 2, 3)),
        DMA((2, 2, 3)), DMA((2, 2, 3)),
        DMA((16,)), DMA((16,)),
        DMA((2, 4)), DMA((2, 4)),
        DMA((2, 3)), DMA((2, 3)),
        DMA((2, 3)), DMA((2, 3)),
        DMA((1,)), DMA((1,)),
        DMA((16,)), DMA((16,)), DMA((15,)), DMA((15,)),
    ]
    rest_value, rest_out, coef = pl.pallas_call(
        step_kernel,
        out_shape=(
            jax.ShapeDtypeStruct((BLOCK, WIDE), F32),
            jax.ShapeDtypeStruct((WIDE, BLOCK), F32),
            jax.ShapeDtypeStruct((8, 128), F32),
        ),
        in_specs=[ANY] * 12 + [SMEM],
        out_specs=(VMEM, VMEM, VMEM),
        scratch_shapes=scratch,
        compiler_params=pltpu.CompilerParams(
            collective_id=0, has_side_effects=True, vmem_limit_bytes=58 * 2**20
        ),
    )(
        tokens,
        target,
        pair_bias,
        neighbours,
        w_query,
        w_key,
        w_value,
        w_out,
        basis_value,
        basis_out,
        prior_value,
        prior_out,
        prior_beta.reshape(1, 1),
    )
    return pl.pallas_call(
        scale_kernel,
        out_shape=(
            jax.ShapeDtypeStruct((BLOCK, WIDE), F32),
            jax.ShapeDtypeStruct((WIDE, BLOCK), F32),
            jax.ShapeDtypeStruct((2,), F32),
        ),
        in_specs=[VMEM] * 3,
        out_specs=(VMEM, VMEM, SMEM),
    )(rest_value, rest_out, coef)


def solution(mesh):
    placed = (
        P("dp", None),
        P("dp", None),
        P("dp", "tensor", None),
        P("dp", None),
        P("dp", "tensor"),
        P("dp", "tensor"),
        P("dp", "tensor"),
        P("tensor", "dp"),
        P("dp", "tensor"),
        P("tensor", "dp"),
        P("dp", "tensor"),
        P("tensor", "dp"),
        P(),
    )
    return jax.shard_map(
        body,
        mesh=mesh,
        in_specs=placed,
        out_specs=(P("dp", "tensor"), P("tensor", "dp"), P()),
        check_vma=False,
    )
```

```python
import math

import jax
import jax.numpy as jnp
from jax import lax
from jax.experimental import pallas as pl
from jax.experimental.pallas import tpu as pltpu
from jax.sharding import PartitionSpec as P

HEAD_DIM = 128
SIDE = 4
ROWS = 16

loss_gain = 32.0
epsilon = 1e-06

MESH = pl.DeviceIdType.MESH
BF = jnp.bfloat16
F32 = jnp.float32
VMEM = pl.BlockSpec(memory_space=pltpu.VMEM)
ANY = pl.BlockSpec(memory_space=pl.ANY)
SMEM = pl.BlockSpec(memory_space=pltpu.SMEM)
DMA = pltpu.SemaphoreType.DMA


def coords():
    dp = lax.axis_index("dp")
    t = lax.axis_index("tensor")
    return dp // SIDE, dp % SIDE, t


def at(y, x, t):
    return (((y + 2 * SIDE) % SIDE) * SIDE + (x + 2 * SIDE) % SIDE, (t + 32) % 16)


def along_x(j):
    y, x, t = coords()
    return at(y, x + j, t)


def along_y(j):
    y, x, t = coords()
    return at(y + j, x, t)


def along_t(k):
    y, x, t = coords()
    return at(y, x, t + k)


def along_z(k):
    y, x, t = coords()
    return at(y, x, t + 2 * k)


def other_core():
    y, x, t = coords()
    return at(y, x, t + 1 - 2 * (t % 2))


def greet(peers):
    barrier = pltpu.get_barrier_semaphore()
    for peer in peers:
        pl.semaphore_signal(barrier, inc=1, device_id=peer, device_id_type=MESH)
    pl.semaphore_wait(barrier, len(peers))


def send(src, dst, ssem, rsem, peer):
    copy = pltpu.make_async_remote_copy(
        src_ref=src,
        dst_ref=dst,
        send_sem=ssem,
        recv_sem=rsem,
        device_id=peer,
        device_id_type=MESH,
    )
    copy.start()
    return copy


NEAR = (2, 1, 3)
AROUND = (8, 7, 9, 6, 10, 5, 11, 4, 12, 3, 13, 2, 14, 1, 15)
WIDE = 256
HALF = 128
BLOCK = 384
COUNT = 256


def dot(a, b):
    return jnp.dot(a, b, preferred_element_type=F32)


def dot_t(a, b):
    return lax.dot_general(a, b, (((1,), (1,)), ((), ())), preferred_element_type=F32)


def arrival(ref, ssem, rsem):
    y, x, t = coords()
    return pltpu.make_async_remote_copy(
        src_ref=ref,
        dst_ref=ref,
        send_sem=ssem,
        recv_sem=rsem,
        device_id=at(y, x, t + 2),
        device_id_type=MESH,
    )


class Ring:
    def __init__(self, slot, part, zs, zr, cs, cr):
        self.slot, self.part = slot, part
        self.zs, self.zr, self.cs, self.cr = zs, zr, cs, cr
        self.sent = []

    def start(self):
        y, x, t = coords()
        for i in range(2):
            own = self.part(t, i)
            for way in range(2):
                sem = (way, 0, i)
                self.sent.append(
                    send(own, own, self.zs.at[sem], self.zr.at[sem], along_z(1 - 2 * way))
                )
        self.core(t, 0)

    def core(self, slot, k):
        got = self.slot(slot)
        self.sent.append(send(got, got, self.cs.at[k], self.cr.at[k], other_core()))

    def step(self, step, onward):
        y, x, t = coords()
        slots = [(t - 2 * (1 - 2 * way) * step + 32) % 16 for way in range(2)]
        for i in range(2):
            for way in range(2):
                part = self.part(slots[way], i)
                sem = (way, step - 1, i)
                arrival(part, self.zs.at[sem], self.zr.at[sem]).wait_recv()
                if i in onward[way]:
                    sem = (way, step, i)
                    self.sent.append(
                        send(part, part, self.zs.at[sem], self.zr.at[sem], along_z(1 - 2 * way))
                    )
        for way in range(2):
            self.core(slots[way], 2 * step - 1 + way)

    def finish(self):
        y, x, t = coords()
        far = (t + 8) % 16
        for way in range(2):
            sem = (way, 3, way)
            arrival(self.part(far, way), self.zs.at[sem], self.zr.at[sem]).wait_recv()
        self.core(far, 7)

    def cores(self, some):
        y, x, t = coords()
        for k in some:
            step, way = (k + 1) // 2, (k + 1) % 2
            shift = 8 if k == 7 else 2 * step * (1 - 2 * way)
            got = self.slot((t + 1 - 2 * (t % 2) - shift + 32) % 16)
            arrival(got, self.cs.at[k], self.cr.at[k]).wait_recv()

    def settle(self):
        for copy in self.sent:
            copy.wait_send()


ALL, NONE = ((0, 1), (0, 1)), ((), ())


class Sweep:
    OFFSETS = (0, -1, 1, 2)

    def __init__(self, part, full, sp, rp, ss, rs):
        y, x, t = coords()
        self.sent = []
        self.sp, self.rp, self.ss, self.rs = sp, rp, ss, rs
        self.first, self.then = (along_x, along_y) if part == 0 else (along_y, along_x)
        self.base = 8 * part

        def block(p, s, half=None):
            rng = pl.ds(self.base, 8) if half is None else pl.ds(self.base + 4 * half, 4)
            dy, dx = (s, p) if part == 0 else (p, s)
            return full.at[(y + dy + SIDE) % SIDE, (x + dx + SIDE) % SIDE, rng]

        self.block = block

    def push(self, ref, ssem, rsem, peer):
        self.sent.append(send(ref, ref, ssem, rsem, peer))

    def start(self):
        own = self.block(0, 0)
        for k in range(2):
            self.push(own, self.sp.at[k], self.rp.at[k], self.first(1 - 2 * k))

    def across(self, q):
        own = self.block(self.OFFSETS[q], 0)
        for k in range(2):
            self.push(own, self.ss.at[q, k], self.rs.at[q, k], self.then(1 - 2 * k))

    def relay(self):
        for k in range(2):
            off = 2 * k - 1
            arrival(self.block(off, 0), self.sp.at[k], self.rp.at[k]).wait_recv()
            half = self.block(off, 0, k)
            self.push(half, self.sp.at[2 + k], self.rp.at[2 + k], self.first(1 - 2 * k))

    def relay_across(self, q):
        p = self.OFFSETS[q]
        for k in range(2):
            off = 2 * k - 1
            arrival(self.block(p, off), self.ss.at[q, k], self.rs.at[q, k]).wait_recv()
            half = self.block(p, off, k)
            self.push(half, self.ss.at[q, 2 + k], self.rs.at[q, 2 + k], self.then(1 - 2 * k))

    def far(self):
        for k in range(2):
            arrival(self.block(2, 0, k), self.sp.at[2 + k], self.rp.at[2 + k]).wait_recv()

    def last(self):
        for q in range(4):
            for k in range(2):
                arrival(
                    self.block(self.OFFSETS[q], 2, k), self.ss.at[q, 2 + k], self.rs.at[q, 2 + k]
                ).wait_recv()


def step_kernel(
    tokens, target, bias, near, wq, wk, wv, wo, bv, bo, pv, po, pb,
    nv, no, coef,
    tok16, tgt16, tok, n16, diff, diffs, rows, gqk, gvt, nx, ny, uall,
    bvv, bov, pvv, pov, nearv, biasv,
    pq, pt, rq, rv, accq, accv, qk, vt, probs, mix, full,
    acc1, acc2, err, terr, errt, terrt, bp, ra, rb, sa, sb, qa, qb, done, bt,
    co, rc, sc, rz, tx, vb, gx, gy, cxf, cyf, cxb, cyb, hx, hy, cv, cw, one, two,
    ls, ps, pr, ws, wr, ds, dr, zs, zr, cs, cr, us, ur, vs, vr, xs, xr, ts, tr,
    as_, ar, bs, br, s1, r1, s2, r2, s3, r3, s4, r4, s5, r5, s6, r6, s7, r7, o1, i1, o2, i2,
):
    y, x, t = coords()
    c = t % 2
    z = t // 2
    me = y * SIDE + x
    full_width = 16 * WIDE
    features = 16 * BLOCK
    scale_out = 1.0 / math.sqrt(full_width)
    scale_value = 1.0 / math.sqrt(features)
    factor = loss_gain * full_width / (16 * COUNT)
    entries = 2.0 * features * full_width

    plane = [(i, j) for i in (2, 1, 3, 0) for j in (2, 1, 3, 0) if i or j]
    barrier = pltpu.get_barrier_semaphore()
    for i, j in plane:
        pl.semaphore_signal(barrier, inc=1, device_id=at(y + i, x + j, t), device_id_type=MESH)
    for k in AROUND:
        pl.semaphore_signal(barrier, inc=1, device_id=along_t(k), device_id_type=MESH)

    some = pl.ds(pl.multiple_of(t * ROWS, ROWS), ROWS)
    far = (t + 8) % 16
    some_far = pl.ds(pl.multiple_of(far * ROWS, ROWS), ROWS)
    left, right = pl.ds(0, WIDE), pl.ds(WIDE, WIDE)
    loads = [
        (tokens.at[some], tok16.at[0]),
        (tokens.at[some_far], tok16.at[1]),
        (target.at[some], tgt16),
        (wq, gqk.at[y, :, left]),
        (wk, gqk.at[y, :, right]),
        (wv, gvt.at[x, :, left]),
        (bv, bvv),
        (tokens, tok),
        (wo, uall.at[t, :, pl.ds(0, BLOCK)]),
        (bo, bov),
        (near, nearv),
        (bias.at[:, 0], biasv.at[0]),
        (bias.at[:, 1], biasv.at[1]),
        (pv, pvv),
        (po, pov),
    ]
    loads = [pltpu.make_async_copy(a, b, ls.at[k]) for k, (a, b) in enumerate(loads)]
    for copy in loads:
        copy.start()

    for copy in loads[:3]:
        copy.wait()
    for i in range(2):
        xf = tok16[i].astype(F32)
        inv = lax.rsqrt(jnp.mean(xf * xf, axis=1, keepdims=True) + epsilon)
        for k in range(16):
            part = tok16[i, :, k * BLOCK : (k + 1) * BLOCK].astype(F32)
            n16[i, k // SIDE, k % SIDE] = (part * inv).astype(BF)
            if i == 0:
                diff[k] = part - tgt16[:, k * BLOCK : (k + 1) * BLOCK].astype(F32)
    pl.semaphore_wait(barrier, 30)

    pieces, weights, others = [], [], []

    def pass_rows(i, slot):
        for j in NEAR:
            src, sem = n16.at[i, :, (x + j) % SIDE], (i, j - 1)
            pieces.append(
                send(src, rows.at[j - 1, slot], ps.at[sem], pr.at[sem], along_x(j))
            )
            src, sem = n16.at[i, (y + j) % SIDE], (i, j + 2)
            pieces.append(
                send(src, rows.at[j + 2, slot], ps.at[sem], pr.at[sem], along_y(j))
            )

    pass_rows(0, t)
    for k in (3, 4, 5, 6):
        loads[k].wait()
    gvt[x, :, WIDE:] = bvv[...].astype(BF)
    lines = (
        (gqk, y, along_y, 0),
        (gvt, x, along_x, 1),
    )

    def pass_weights(held, mine, along, k, way, off, rng, sem):
        ref = held.at[(mine + off + SIDE) % SIDE, rng]
        weights.append(send(ref, ref, ws.at[k, sem], wr.at[k, sem], along(1 - 2 * way)))

    for way in range(2):
        for line in lines:
            pass_weights(*line, way, 0, pl.ds(0, BLOCK), way)
    pass_rows(1, far)
    diffs[me] = diff[me]

    ring = Ring(
        lambda n: rows.at[:, n], lambda n, i: rows.at[pl.ds(3 * i, 3), n], zs, zr, cs, cr
    )
    for copy in pieces[:6]:
        copy.wait_recv()
    ring.start()

    loads[7].wait()

    def normalise(r, _):
        at_r = pl.ds(pl.multiple_of(r * ROWS, ROWS), ROWS)
        xf = tok[at_r].astype(F32)
        inv = lax.rsqrt(jnp.mean(xf * xf, axis=1, keepdims=True) + epsilon)
        for b in range(SIDE):
            cut = pl.ds(pl.multiple_of((b * SIDE + x) * BLOCK, HALF), BLOCK)
            nx[b, at_r] = (tok[at_r, cut].astype(F32) * inv).astype(BF)
            cut = pl.ds(pl.multiple_of((y * SIDE + b) * BLOCK, HALF), BLOCK)
            ny[b, at_r] = (tok[at_r, cut].astype(F32) * inv).astype(BF)
        return 0

    lax.fori_loop(0, COUNT // ROWS, normalise, 0)
    for way in range(2):
        for k, line in enumerate(lines):
            weights[2 * way + k].wait_recv()
            half = pl.ds(way * (BLOCK // 2), BLOCK // 2)
            pass_weights(*line, way, 2 * way - 1, half, 2 + way)
    ring.step(1, ALL)
    loads[8].wait()
    loads[9].wait()
    uall[t, :, BLOCK:] = bov[...].astype(BF)
    ring.step(2, ALL)
    for copy in pieces[6:]:
        copy.wait_recv()
    ring.core(far, 7)
    for copy in weights[4:]:
        copy.wait_recv()

    order = []
    for off in (0, -1, 1, 4, -2, 2, -3, 3):
        base = ((z + off + 8) % 8) * 2
        order += [base + c, base + 1 - c]
    partial = []

    def products(part, lo, hi):
        for w, k0, out, got, along in ((gqk, 0, pq, rq, along_x), (gvt, 3, pt, rv, along_y)):
            total = None
            for b in range(SIDE):
                lhs = jnp.concatenate(
                    [rows[k0 + j, n, b] for j in range(3) for n in order[lo:hi]], axis=0
                )
                more = dot(lhs, w[b])
                total = more if total is None else total + more
            size = (hi - lo) * ROWS
            for j in range(3):
                out[j, lo * ROWS : hi * ROWS] = total[j * size : (j + 1) * size].astype(BF)
            cut = pl.ds(lo * ROWS, size)
            for j in NEAR:
                sem = (part, k0 + j - 1)
                partial.append(
                    send(out.at[j - 1, cut], got.at[j - 1, cut], xs.at[sem], xr.at[sem], along(-j))
                )

    ring.cores((0, 1, 2, 7))
    products(0, 0, 8)
    ring.cores((3, 4))
    products(1, 8, 12)
    for lhs, w, acc in ((nx, gqk, accq), (ny, gvt, accv)):
        total = dot(lhs[0], w[0])
        for b in range(1, SIDE):
            total = total + dot(lhs[b], w[b])
        acc[...] = total
    ring.step(3, NONE)
    uring = Ring(
        lambda n: uall.at[n], lambda n, i: uall.at[n, pl.ds(HALF * i, HALF)], us, ur, vs, vr
    )
    uring.start()
    ring.cores((5, 6))
    products(2, 12, 16)
    for copy in partial:
        copy.wait_recv()

    for p, n in enumerate(order):
        at_n = pl.ds(pl.multiple_of(n * ROWS, ROWS), ROWS)
        at_p = slice(p * ROWS, (p + 1) * ROWS)
        total = accq[at_n]
        for j in range(3):
            total = total + rq[j, at_p].astype(F32)
        qk[at_n] = total.astype(BF)
        total = accv[at_n]
        for j in range(3):
            total = total + rv[j, at_p].astype(F32)
        vt[at_n, :WIDE] = total[:, :WIDE].astype(BF)
        vt[at_n, WIDE:] = (total[:, WIDE:] / math.sqrt(features)).astype(BF)

    for k, (i, j) in enumerate(plane):
        yy, xx = (y + i) % SIDE, (x + j) % SIDE
        others.append(
            send(diff.at[yy * SIDE + xx], diffs.at[me], ds.at[k], dr.at[k], (yy * SIDE + xx, t))
        )

    loads[10].wait()
    loads[11].wait()
    loads[12].wait()
    at_row = lax.broadcasted_iota(jnp.int32, (COUNT, COUNT), 0)
    at_col = lax.broadcasted_iota(jnp.int32, (COUNT, COUNT), 1)
    allowed = (nearv[...] == 1) | (jnp.abs(at_row - at_col) <= 1)
    for h in range(2):
        cut = slice(h * HALF, (h + 1) * HALF)
        cut2 = slice(WIDE + h * HALF, WIDE + (h + 1) * HALF)
        scores = dot_t(qk[:, cut], qk[:, cut2]) / math.sqrt(HEAD_DIM) + biasv[h]
        scores = jnp.where(allowed, scores, -jnp.inf)
        e = jnp.exp(scores - jnp.max(scores, axis=1, keepdims=True))
        p = (e / jnp.sum(e, axis=1, keepdims=True)).astype(BF)
        probs[h] = p
        mix[:, cut] = dot(p, vt[:, cut]).astype(BF)
        mix[:, cut2] = dot(p, vt[:, cut2]).astype(BF)

    moved = []
    for k in AROUND:
        to = pl.ds(pl.multiple_of(((t + k) % 16) * ROWS, ROWS), ROWS)
        moved.append(send(mix.at[to], full.at[y, x, t], ts.at[k], tr.at[k], along_t(k)))
    full[y, x, t] = mix[some]
    uring.step(1, ALL)
    for copy in moved:
        copy.wait_recv()
    sweeps = [
        Sweep(0, full, as_.at[0], ar.at[0], bs.at[0], br.at[0]),
        Sweep(1, full, as_.at[1], ar.at[1], bs.at[1], br.at[1]),
    ]
    for sweep in sweeps:
        sweep.start()
    for sweep in sweeps:
        sweep.across(0)
    for sweep in sweeps:
        sweep.relay()
    for sweep in sweeps:
        sweep.across(1)
        sweep.across(2)
    uring.step(2, ALL)
    for sweep in sweeps:
        sweep.relay_across(0)
    uring.step(3, ((0,), (1,)))
    for sweep in sweeps:
        sweep.far()
        sweep.across(3)
    for q in (1, 2):
        for sweep in sweeps:
            sweep.relay_across(q)
    uring.finish()
    for sweep in sweeps:
        sweep.relay_across(3)
    uring.cores(range(8))
    for sweep in sweeps:
        sweep.last()

    acc1[...] = jnp.zeros_like(acc1)
    acc2[...] = jnp.zeros_like(acc2)

    def forward(k, _):
        at_k = pl.ds(k * 4, 4)
        parts = [full[:, :, k * 4 + i].reshape(COUNT, 2 * WIDE) for i in range(4)]
        w = uall[at_k].reshape(4 * WIDE, 2 * BLOCK)
        acc1[...] += dot(jnp.concatenate([p[:, :WIDE] for p in parts], axis=1), w)
        acc2[...] += dot(jnp.concatenate([p[:, WIDE:] for p in parts], axis=1), w[:, :BLOCK])
        return 0

    lax.fori_loop(0, 4, forward, 0)
    for copy in others:
        copy.wait_recv()
    err[...] = ((diffs[...].reshape(COUNT, BLOCK) + acc1[:, :BLOCK]) * factor).astype(BF)
    terr[...] = ((acc1[:, BLOCK:] * scale_out + acc2[...]) * factor).astype(BF)

    def backward(n, _):
        part = dot_t(terr[...], uall[n, :, :BLOCK]) + scale_out * dot_t(err[...], uall[n, :, BLOCK:])
        bp[n] = part.astype(BF).reshape(SIDE, SIDE, ROWS, WIDE)
        return 0

    first_b = []
    cuts = ((0, 3), (3, 8))
    for part, (a, b) in enumerate(cuts):
        here = pl.ds(a, b - a)
        lax.fori_loop(a, b, backward, 0)
        for j in NEAR:
            src, sem = bp.at[here, (y + j) % SIDE], (part, 0, j - 1)
            first_b.append(send(src, ra.at[j - 1, here], s1.at[sem], r1.at[sem], along_y(j)))
        lax.fori_loop(8 + a, 8 + b, backward, 0)
        for j in NEAR:
            src, sem = bp.at[pl.ds(8 + a, b - a), :, (x + j) % SIDE], (part, 1, j - 1)
            first_b.append(send(src, rb.at[j - 1, here], s1.at[sem], r1.at[sem], along_x(j)))

    errt[...] = err[...].astype(F32).T.astype(BF)
    terrt[...] = terr[...].astype(F32).T.astype(BF)

    def outer(n, _):
        both = full[:, :, n].reshape(COUNT, 2 * WIDE)
        part = dot(errt[...], both[:, WIDE:]) + dot(terrt[...], both[:, :WIDE])
        co[n // 2, n % 2] = (part * scale_out).astype(BF)
        return 0

    lax.fori_loop(0, 16, outer, 0)
    swapped = send(co.at[:, 1 - c], rc, s7.at[0], r7.at[0], other_core())

    second_b = []
    for part, (a, b) in enumerate(cuts):
        for copy in first_b[6 * part : 6 * part + 6]:
            copy.wait_recv()
        for i in range(SIDE):
            total = bp[a:b, y, i].astype(F32)
            for j in range(3):
                total = total + ra[j, a:b, i].astype(F32)
            sa[i, a:b] = total.astype(BF)
            total = bp[8 + a : 8 + b, i, x].astype(F32)
            for j in range(3):
                total = total + rb[j, a:b, i].astype(F32)
            sb[i, a:b] = total.astype(BF)
        here = pl.ds(a, b - a)
        for j in NEAR:
            src, sem = sa.at[(x + j) % SIDE, here], (part, 0, j - 1)
            second_b.append(send(src, qa.at[j - 1, here], s2.at[sem], r2.at[sem], along_x(j)))
            src, sem = sb.at[(y + j) % SIDE, here], (part, 1, j - 1)
            second_b.append(send(src, qb.at[j - 1, here], s2.at[sem], r2.at[sem], along_y(j)))

    swapped.wait_recv()

    def pair(k, _):
        sc[k] = (co[k, c].astype(F32) + rc[k].astype(F32)).astype(BF)
        return 0

    lax.fori_loop(0, 8, pair, 0)
    shares = []

    def pass_on(step):
        for way in range(2):
            sign = 1 - 2 * way
            slot = (z + sign * (4 - step) + 8) % 8
            if step == 0:
                cut = pl.ds(way * (BLOCK // 2), BLOCK // 2)
                src, dst = sc.at[slot, cut], rz.at[way, 0, cut]
            else:
                shares[2 * (step - 1) + way].wait_recv()
                if step == 1:
                    a, b = way * (BLOCK // 2), (way + 1) * (BLOCK // 2)
                    tx[way, 0] = sc[slot]
                    total = sc[slot, a:b].astype(F32) + rz[way, 0, a:b].astype(F32)
                    tx[way, 0, a:b] = total.astype(BF)
                else:
                    total = sc[slot].astype(F32) + rz[way, step - 1].astype(F32)
                    tx[way, step - 1] = total.astype(BF)
                src, dst = tx.at[way, step - 1], rz.at[way, step]
            shares.append(
                send(src, dst, s4.at[way, step], r4.at[way, step], along_z(sign))
            )

    pass_on(0)
    for copy in second_b:
        copy.wait_recv()
    total = sa[x].astype(F32)
    for j in range(3):
        total = total + qa[j].astype(F32)
    done[0:8] = total.astype(BF)
    total = sb[y].astype(F32)
    for j in range(3):
        total = total + qb[j].astype(F32)
    done[8:16] = total.astype(BF)
    third = []
    for k in AROUND:
        third.append(send(done.at[(t + k) % 16], bt.at[t], s3.at[k], r3.at[k], along_t(k)))
    bt[t] = done[t]

    pass_on(1)
    for copy in third:
        copy.wait_recv()
    back = bt[...].reshape(COUNT, WIDE).astype(F32).T.astype(BF)
    fourth = []
    for h in range(2):
        vb[h] = dot(back[h * HALF : (h + 1) * HALF], probs[h]).astype(BF)
        got, along = ((gx, along_x), (gy, along_y))[h]
        for j in NEAR:
            fourth.append(
                send(vb.at[h], got.at[j - 1], s5.at[h, j - 1], r5.at[h, j - 1], along(j))
            )
    pass_on(2)
    loads[13].wait()
    loads[14].wait()
    def inner(a1, b1, a2, b2):
        total = jnp.zeros((8, 128), F32)
        for a, b in ((a1, b1), (a2, b2)):
            prod = a[...] * b[...]
            prod = jnp.sum(prod.reshape(prod.shape[0] // 8, 8, prod.shape[1]), axis=0)
            for k in range(prod.shape[1] // 128):
                total = total + prod[:, k * 128 : (k + 1) * 128]
        return jnp.sum(total, axis=0, keepdims=True)

    pairs = ((bvv, bvv, bov, bov), (bvv, pvv, bov, pov), (pvv, pvv, pov, pov))
    for k, args in enumerate(pairs):
        one[t, 3 + k : 4 + k] = inner(*args)
    one[t, 6:8] = jnp.zeros((2, 128), F32)
    for copy in fourth:
        copy.wait_recv()
    fifth = []
    for k in (2, 1, 3, 0):
        for h, own, got, mine, outf, outb, to, along in (
            (0, nx, gx, y, cxf, cxb, hx, along_y),
            (1, ny, gy, x, cyf, cyb, hy, along_x),
        ):
            b = (mine + k) % SIDE
            total = dot(vb[h], own[b])
            for j in range(3):
                total = total + dot(got[j], rows[3 * h + j, :, b].reshape(COUNT, BLOCK))
            total = total * scale_value
            if k == 0:
                outf[...] = total
            else:
                outb[k - 1] = total.astype(BF)
                fifth.append(
                    send(outb.at[k - 1], to.at[k - 1], s6.at[h, k - 1], r6.at[h, k - 1], along(k))
                )
    pass_on(3)
    for copy in fifth:
        copy.wait_recv()
    for h, (own, got) in enumerate(((cxf, hx), (cyf, hy))):
        total = own[...]
        for j in range(3):
            total = total + got[j].astype(F32)
        cv[:, h * HALF : (h + 1) * HALF] = total.T
    for copy in shares[6:]:
        copy.wait_recv()
    total = sc[z].astype(F32)
    for way in range(2):
        total = total + rz[way, 3].astype(F32)
    cw[...] = total.T

    pairs = ((cv, bvv, cw, bov), (cv, cv, cw, cw), (cv, pvv, cw, pov))
    for k, args in enumerate(pairs):
        one[t, k : k + 1] = inner(*args)
    rounds = []
    for k in AROUND:
        rounds.append(send(one.at[t], one.at[t], o1.at[k], i1.at[k], along_t(k)))
    for copy in rounds:
        copy.wait_recv()
    two[me] = jnp.sum(one[...], axis=0)
    for k, (i, j) in enumerate(plane):
        peer = at(y + i, x + j, t)
        rounds.append(send(two.at[me], two.at[me], o2.at[k], i2.at[k], peer))
    for copy in rounds[15:]:
        copy.wait_recv()
    sums = jnp.sum(jnp.sum(two[...], axis=0), axis=1, keepdims=True) / entries
    beta_before = pb[0, 0]
    cb, cc, cp, bb, bq, pp = (sums[k : k + 1] for k in range(6))
    alpha = cb
    squares = cc + alpha * alpha * bb + beta_before * beta_before * pp
    squares = squares - 2.0 * (alpha * cb + beta_before * (cp - alpha * bq))
    beta = jnp.sqrt(jnp.maximum(squares, 0.0) + epsilon)
    nv[...] = cv[...] - alpha * bvv[...] - beta_before * pvv[...]
    no[...] = cw[...] - alpha * bov[...] - beta_before * pov[...]
    coef[0:1] = jnp.broadcast_to(alpha, (1, 128))
    coef[1:2] = jnp.broadcast_to(beta, (1, 128))
    coef[2:3] = jnp.broadcast_to(1.0 / beta, (1, 128))
    for copy in (
        pieces + weights + others + partial + moved + first_b + second_b
        + third + [swapped] + shares + fourth + fifth + rounds
    ):
        copy.wait_send()
    ring.settle()
    uring.settle()
    for sweep in sweeps:
        for copy in sweep.sent:
            copy.wait_send()


def scale_kernel(rest_value, rest_out, coef, nv, no, out):
    scale = coef[2:3, 0:1]
    nv[...] = rest_value[...] * scale
    no[...] = rest_out[...] * scale
    out[0] = coef[0, 0]
    out[1] = coef[1, 0]


def body(
    tokens,
    target,
    pair_bias,
    neighbours,
    w_query,
    w_key,
    w_value,
    w_out,
    basis_value,
    basis_out,
    prior_value,
    prior_out,
    prior_beta,
):
    def vm(dtype, *dims):
        return pltpu.VMEM(dims, dtype)

    features = 16 * BLOCK
    scratch = [
        vm(BF, 2, ROWS, features),
        vm(BF, ROWS, features),
        vm(BF, COUNT, features),
        vm(BF, 2, SIDE, SIDE, ROWS, BLOCK),
        vm(F32, 16, ROWS, BLOCK),
        vm(F32, 16, ROWS, BLOCK),
        vm(BF, 6, 16, SIDE, ROWS, BLOCK),
        vm(BF, SIDE, BLOCK, 2 * WIDE),
        vm(BF, SIDE, BLOCK, 2 * WIDE),
        vm(BF, SIDE, COUNT, BLOCK),
        vm(BF, SIDE, COUNT, BLOCK),
        vm(BF, 16, WIDE, 2 * BLOCK),
        vm(F32, BLOCK, WIDE),
        vm(F32, WIDE, BLOCK),
        vm(F32, BLOCK, WIDE),
        vm(F32, WIDE, BLOCK),
        vm(jnp.int32, COUNT, COUNT),
        vm(F32, 2, COUNT, COUNT),
        vm(BF, 3, COUNT, 2 * WIDE),
        vm(BF, 3, COUNT, 2 * WIDE),
        vm(BF, 3, COUNT, 2 * WIDE),
        vm(BF, 3, COUNT, 2 * WIDE),
        vm(F32, COUNT, 2 * WIDE),
        vm(F32, COUNT, 2 * WIDE),
        vm(BF, COUNT, 2 * WIDE),
        vm(BF, COUNT, 2 * WIDE),
        vm(BF, 2, COUNT, COUNT),
        vm(BF, COUNT, 2 * WIDE),
        vm(BF, SIDE, SIDE, 16, ROWS, 2 * WIDE),
        vm(F32, COUNT, 2 * BLOCK),
        vm(F32, COUNT, BLOCK),
        vm(BF, COUNT, BLOCK),
        vm(BF, COUNT, BLOCK),
        vm(BF, BLOCK, COUNT),
        vm(BF, BLOCK, COUNT),
        vm(BF, 16, SIDE, SIDE, ROWS, WIDE),
        vm(BF, 3, 8, SIDE, ROWS, WIDE),
        vm(BF, 3, 8, SIDE, ROWS, WIDE),
        vm(BF, SIDE, 8, ROWS, WIDE),
        vm(BF, SIDE, 8, ROWS, WIDE),
        vm(BF, 3, 8, ROWS, WIDE),
        vm(BF, 3, 8, ROWS, WIDE),
        vm(BF, 16, ROWS, WIDE),
        vm(BF, 16, ROWS, WIDE),
        vm(BF, 8, 2, BLOCK, WIDE),
        vm(BF, 8, BLOCK, WIDE),
        vm(BF, 8, BLOCK, WIDE),
        vm(BF, 2, 4, BLOCK, WIDE),
        vm(BF, 2, 3, BLOCK, WIDE),
        vm(BF, 2, HALF, COUNT),
        vm(BF, 3, HALF, COUNT),
        vm(BF, 3, HALF, COUNT),
        vm(F32, HALF, BLOCK),
        vm(F32, HALF, BLOCK),
        vm(BF, 3, HALF, BLOCK),
        vm(BF, 3, HALF, BLOCK),
        vm(BF, 3, HALF, BLOCK),
        vm(BF, 3, HALF, BLOCK),
        vm(F32, BLOCK, WIDE),
        vm(F32, WIDE, BLOCK),
        vm(F32, 16, 8, 128),
        vm(F32, 16, 8, 128),
        DMA((15,)),
        DMA((2, 6)), DMA((2, 6)),
        DMA((2, 4)), DMA((2, 4)),
        DMA((15,)), DMA((15,)),
        DMA((2, 3, 2)), DMA((2, 3, 2)), DMA((8,)), DMA((8,)),
        DMA((2, 4, 2)), DMA((2, 4, 2)), DMA((8,)), DMA((8,)),
        DMA((3, 6)), DMA((3, 6)),
        DMA((16,)), DMA((16,)),
        DMA((2, 4)), DMA((2, 4)), DMA((2, 4, 4)), DMA((2, 4, 4)),
        DMA((2, 2, 3)), DMA((2, 2, 3)),
        DMA((2, 2, 3)), DMA((2, 2, 3)),
        DMA((16,)), DMA((16,)),
        DMA((2, 4)), DMA((2, 4)),
        DMA((2, 3)), DMA((2, 3)),
        DMA((2, 3)), DMA((2, 3)),
        DMA((1,)), DMA((1,)),
        DMA((16,)), DMA((16,)), DMA((15,)), DMA((15,)),
    ]
    rest_value, rest_out, coef = pl.pallas_call(
        step_kernel,
        out_shape=(
            jax.ShapeDtypeStruct((BLOCK, WIDE), F32),
            jax.ShapeDtypeStruct((WIDE, BLOCK), F32),
            jax.ShapeDtypeStruct((8, 128), F32),
        ),
        in_specs=[ANY] * 12 + [SMEM],
        out_specs=(VMEM, VMEM, VMEM),
        scratch_shapes=scratch,
        compiler_params=pltpu.CompilerParams(
            collective_id=0, has_side_effects=True, vmem_limit_bytes=58 * 2**20
        ),
    )(
        tokens,
        target,
        pair_bias,
        neighbours,
        w_query,
        w_key,
        w_value,
        w_out,
        basis_value,
        basis_out,
        prior_value,
        prior_out,
        prior_beta.reshape(1, 1),
    )
    return pl.pallas_call(
        scale_kernel,
        out_shape=(
            jax.ShapeDtypeStruct((BLOCK, WIDE), F32),
            jax.ShapeDtypeStruct((WIDE, BLOCK), F32),
            jax.ShapeDtypeStruct((2,), F32),
        ),
        in_specs=[VMEM] * 3,
        out_specs=(VMEM, VMEM, SMEM),
    )(rest_value, rest_out, coef)


def solution(mesh):
    placed = (
        P("dp", None),
        P("dp", None),
        P("dp", "tensor", None),
        P("dp", None),
        P("dp", "tensor"),
        P("dp", "tensor"),
        P("dp", "tensor"),
        P("tensor", "dp"),
        P("dp", "tensor"),
        P("tensor", "dp"),
        P("dp", "tensor"),
        P("tensor", "dp"),
        P(),
    )
    return jax.shard_map(
        body,
        mesh=mesh,
        in_specs=placed,
        out_specs=(P("dp", "tensor"), P("tensor", "dp"), P()),
        check_vma=False,
    )
```

```python
import math

import jax
import jax.numpy as jnp
from jax import lax
from jax.experimental import pallas as pl
from jax.experimental.pallas import tpu as pltpu
from jax.sharding import PartitionSpec as P

HEAD_DIM = 128
SIDE = 4
ROWS = 16

loss_gain = 32.0
epsilon = 1e-06

MESH = pl.DeviceIdType.MESH
BF = jnp.bfloat16
F32 = jnp.float32
VMEM = pl.BlockSpec(memory_space=pltpu.VMEM)
ANY = pl.BlockSpec(memory_space=pl.ANY)
SMEM = pl.BlockSpec(memory_space=pltpu.SMEM)
DMA = pltpu.SemaphoreType.DMA


def coords():
    dp = lax.axis_index("dp")
    t = lax.axis_index("tensor")
    return dp // SIDE, dp % SIDE, t


def at(y, x, t):
    return (((y + 2 * SIDE) % SIDE) * SIDE + (x + 2 * SIDE) % SIDE, (t + 32) % 16)


def along_x(j):
    y, x, t = coords()
    return at(y, x + j, t)


def along_y(j):
    y, x, t = coords()
    return at(y + j, x, t)


def along_t(k):
    y, x, t = coords()
    return at(y, x, t + k)


def along_z(k):
    y, x, t = coords()
    return at(y, x, t + 2 * k)


def other_core():
    y, x, t = coords()
    return at(y, x, t + 1 - 2 * (t % 2))


def greet(peers):
    barrier = pltpu.get_barrier_semaphore()
    for peer in peers:
        pl.semaphore_signal(barrier, inc=1, device_id=peer, device_id_type=MESH)
    pl.semaphore_wait(barrier, len(peers))


def send(src, dst, ssem, rsem, peer):
    copy = pltpu.make_async_remote_copy(
        src_ref=src,
        dst_ref=dst,
        send_sem=ssem,
        recv_sem=rsem,
        device_id=peer,
        device_id_type=MESH,
    )
    copy.start()
    return copy


NEAR = (2, 1, 3)
AROUND = (8, 7, 9, 6, 10, 5, 11, 4, 12, 3, 13, 2, 14, 1, 15)
WIDE = 256
HALF = 128
BLOCK = 384
COUNT = 256


def dot(a, b):
    return jnp.dot(a, b, preferred_element_type=F32)


def dot_t(a, b):
    return lax.dot_general(a, b, (((1,), (1,)), ((), ())), preferred_element_type=F32)


def arrival(ref, ssem, rsem):
    y, x, t = coords()
    return pltpu.make_async_remote_copy(
        src_ref=ref,
        dst_ref=ref,
        send_sem=ssem,
        recv_sem=rsem,
        device_id=at(y, x, t + 2),
        device_id_type=MESH,
    )


class Ring:
    def __init__(self, slot, part, zs, zr, cs, cr):
        self.slot, self.part = slot, part
        self.zs, self.zr, self.cs, self.cr = zs, zr, cs, cr
        self.sent = []

    def start(self):
        y, x, t = coords()
        for i in range(2):
            own = self.part(t, i)
            for way in range(2):
                sem = (way, 0, i)
                self.sent.append(
                    send(own, own, self.zs.at[sem], self.zr.at[sem], along_z(1 - 2 * way))
                )
        self.core(t, 0)

    def core(self, slot, k):
        got = self.slot(slot)
        self.sent.append(send(got, got, self.cs.at[k], self.cr.at[k], other_core()))

    def step(self, step, onward):
        y, x, t = coords()
        slots = [(t - 2 * (1 - 2 * way) * step + 32) % 16 for way in range(2)]
        for i in range(2):
            for way in range(2):
                part = self.part(slots[way], i)
                sem = (way, step - 1, i)
                arrival(part, self.zs.at[sem], self.zr.at[sem]).wait_recv()
                if i in onward[way]:
                    sem = (way, step, i)
                    self.sent.append(
                        send(part, part, self.zs.at[sem], self.zr.at[sem], along_z(1 - 2 * way))
                    )
        for way in range(2):
            self.core(slots[way], 2 * step - 1 + way)

    def finish(self):
        y, x, t = coords()
        far = (t + 8) % 16
        for way in range(2):
            sem = (way, 3, way)
            arrival(self.part(far, way), self.zs.at[sem], self.zr.at[sem]).wait_recv()
        self.core(far, 7)

    def cores(self, some):
        y, x, t = coords()
        for k in some:
            step, way = (k + 1) // 2, (k + 1) % 2
            shift = 8 if k == 7 else 2 * step * (1 - 2 * way)
            got = self.slot((t + 1 - 2 * (t % 2) - shift + 32) % 16)
            arrival(got, self.cs.at[k], self.cr.at[k]).wait_recv()

    def settle(self):
        for copy in self.sent:
            copy.wait_send()


ALL, NONE = ((0, 1), (0, 1)), ((), ())


class Sweep:
    OFFSETS = (0, -1, 1, 2)

    def __init__(self, part, full, sp, rp, ss, rs):
        y, x, t = coords()
        self.sent = []
        self.sp, self.rp, self.ss, self.rs = sp, rp, ss, rs
        self.first, self.then = (along_x, along_y) if part == 0 else (along_y, along_x)
        self.base = 8 * part

        def block(p, s, half=None):
            rng = pl.ds(self.base, 8) if half is None else pl.ds(self.base + 4 * half, 4)
            dy, dx = (s, p) if part == 0 else (p, s)
            return full.at[(y + dy + SIDE) % SIDE, (x + dx + SIDE) % SIDE, rng]

        self.block = block

    def push(self, ref, ssem, rsem, peer):
        self.sent.append(send(ref, ref, ssem, rsem, peer))

    def start(self):
        own = self.block(0, 0)
        for k in range(2):
            self.push(own, self.sp.at[k], self.rp.at[k], self.first(1 - 2 * k))

    def across(self, q):
        own = self.block(self.OFFSETS[q], 0)
        for k in range(2):
            self.push(own, self.ss.at[q, k], self.rs.at[q, k], self.then(1 - 2 * k))

    def relay(self):
        for k in range(2):
            off = 2 * k - 1
            arrival(self.block(off, 0), self.sp.at[k], self.rp.at[k]).wait_recv()
            half = self.block(off, 0, k)
            self.push(half, self.sp.at[2 + k], self.rp.at[2 + k], self.first(1 - 2 * k))

    def relay_across(self, q):
        p = self.OFFSETS[q]
        for k in range(2):
            off = 2 * k - 1
            arrival(self.block(p, off), self.ss.at[q, k], self.rs.at[q, k]).wait_recv()
            half = self.block(p, off, k)
            self.push(half, self.ss.at[q, 2 + k], self.rs.at[q, 2 + k], self.then(1 - 2 * k))

    def far(self):
        for k in range(2):
            arrival(self.block(2, 0, k), self.sp.at[2 + k], self.rp.at[2 + k]).wait_recv()

    def last(self):
        for q in range(4):
            for k in range(2):
                arrival(
                    self.block(self.OFFSETS[q], 2, k), self.ss.at[q, 2 + k], self.rs.at[q, 2 + k]
                ).wait_recv()


def step_kernel(
    tokens, target, bias, near, wq, wk, wv, wo, bv, bo, pv, po, pb,
    nv, no, coef,
    tok16, tgt16, tok, n16, diff, diffs, rows, gqk, gvt, nx, ny, uall,
    bvv, bov, pvv, pov, nearv, biasv,
    pq, pt, rq, rv, accq, accv, qk, vt, probs, mix, full,
    acc1, acc2, err, terr, errt, terrt, bp, ra, rb, sa, sb, qa, qb, done, bt,
    co, rc, sc, rz, tx, vb, gx, gy, cxf, cyf, cxb, cyb, hx, hy, cv, cw, one, two,
    ls, ps, pr, ws, wr, ds, dr, zs, zr, cs, cr, us, ur, vs, vr, xs, xr, ts, tr,
    as_, ar, bs, br, s1, r1, s2, r2, s3, r3, s4, r4, s5, r5, s6, r6, s7, r7, o1, i1, o2, i2,
):
    y, x, t = coords()
    c = t % 2
    z = t // 2
    me = y * SIDE + x
    full_width = 16 * WIDE
    features = 16 * BLOCK
    scale_out = 1.0 / math.sqrt(full_width)
    scale_value = 1.0 / math.sqrt(features)
    factor = loss_gain * full_width / (16 * COUNT)
    entries = 2.0 * features * full_width

    plane = [(i, j) for i in (2, 1, 3, 0) for j in (2, 1, 3, 0) if i or j]
    barrier = pltpu.get_barrier_semaphore()
    for i, j in plane:
        pl.semaphore_signal(barrier, inc=1, device_id=at(y + i, x + j, t), device_id_type=MESH)
    for k in AROUND:
        pl.semaphore_signal(barrier, inc=1, device_id=along_t(k), device_id_type=MESH)

    some = pl.ds(pl.multiple_of(t * ROWS, ROWS), ROWS)
    far = (t + 8) % 16
    some_far = pl.ds(pl.multiple_of(far * ROWS, ROWS), ROWS)
    left, right = pl.ds(0, WIDE), pl.ds(WIDE, WIDE)
    loads = [
        (tokens.at[some], tok16.at[0]),
        (tokens.at[some_far], tok16.at[1]),
        (target.at[some], tgt16),
        (wq, gqk.at[y, :, left]),
        (wk, gqk.at[y, :, right]),
        (wv, gvt.at[x, :, left]),
        (bv, bvv),
        (tokens, tok),
        (wo, uall.at[t, :, pl.ds(0, BLOCK)]),
        (bo, bov),
        (near, nearv),
        (bias.at[:, 0], biasv.at[0]),
        (bias.at[:, 1], biasv.at[1]),
        (pv, pvv),
        (po, pov),
    ]
    loads = [pltpu.make_async_copy(a, b, ls.at[k]) for k, (a, b) in enumerate(loads)]
    for copy in loads:
        copy.start()

    for copy in loads[:3]:
        copy.wait()
    for i in range(2):
        xf = tok16[i].astype(F32)
        inv = lax.rsqrt(jnp.mean(xf * xf, axis=1, keepdims=True) + epsilon)
        for k in range(16):
            part = tok16[i, :, k * BLOCK : (k + 1) * BLOCK].astype(F32)
            n16[i, k // SIDE, k % SIDE] = (part * inv).astype(BF)
            if i == 0:
                diff[k] = part - tgt16[:, k * BLOCK : (k + 1) * BLOCK].astype(F32)
    pl.semaphore_wait(barrier, 30)

    pieces, weights, others = [], [], []

    def pass_rows(i, slot):
        for j in NEAR:
            src, sem = n16.at[i, :, (x + j) % SIDE], (i, j - 1)
            pieces.append(
                send(src, rows.at[j - 1, slot], ps.at[sem], pr.at[sem], along_x(j))
            )
            src, sem = n16.at[i, (y + j) % SIDE], (i, j + 2)
            pieces.append(
                send(src, rows.at[j + 2, slot], ps.at[sem], pr.at[sem], along_y(j))
            )

    pass_rows(0, t)
    for k in (3, 4, 5, 6):
        loads[k].wait()
    gvt[x, :, WIDE:] = bvv[...].astype(BF)
    lines = (
        (gqk, y, along_y, 0),
        (gvt, x, along_x, 1),
    )

    def pass_weights(held, mine, along, k, way, off, rng, sem):
        ref = held.at[(mine + off + SIDE) % SIDE, rng]
        weights.append(send(ref, ref, ws.at[k, sem], wr.at[k, sem], along(1 - 2 * way)))

    for way in range(2):
        for line in lines:
            pass_weights(*line, way, 0, pl.ds(0, BLOCK), way)
    pass_rows(1, far)
    diffs[me] = diff[me]

    ring = Ring(
        lambda n: rows.at[:, n], lambda n, i: rows.at[pl.ds(3 * i, 3), n], zs, zr, cs, cr
    )
    for copy in pieces[:6]:
        copy.wait_recv()
    ring.start()

    loads[7].wait()

    def normalise(r, _):
        at_r = pl.ds(pl.multiple_of(r * ROWS, ROWS), ROWS)
        xf = tok[at_r].astype(F32)
        inv = lax.rsqrt(jnp.mean(xf * xf, axis=1, keepdims=True) + epsilon)
        for b in range(SIDE):
            cut = pl.ds(pl.multiple_of((b * SIDE + x) * BLOCK, HALF), BLOCK)
            nx[b, at_r] = (tok[at_r, cut].astype(F32) * inv).astype(BF)
            cut = pl.ds(pl.multiple_of((y * SIDE + b) * BLOCK, HALF), BLOCK)
            ny[b, at_r] = (tok[at_r, cut].astype(F32) * inv).astype(BF)
        return 0

    lax.fori_loop(0, COUNT // ROWS, normalise, 0)
    for way in range(2):
        for k, line in enumerate(lines):
            weights[2 * way + k].wait_recv()
            half = pl.ds(way * (BLOCK // 2), BLOCK // 2)
            pass_weights(*line, way, 2 * way - 1, half, 2 + way)
    ring.step(1, ALL)
    loads[8].wait()
    loads[9].wait()
    uall[t, :, BLOCK:] = bov[...].astype(BF)
    ring.step(2, ALL)
    for copy in pieces[6:]:
        copy.wait_recv()
    ring.core(far, 7)
    for copy in weights[4:]:
        copy.wait_recv()

    order = []
    for off in (0, -1, 1, 4, -2, 2, -3, 3):
        base = ((z + off + 8) % 8) * 2
        order += [base + c, base + 1 - c]
    partial = []

    def products(part, lo, hi):
        for w, k0, out, got, along in ((gqk, 0, pq, rq, along_x), (gvt, 3, pt, rv, along_y)):
            total = None
            for b in range(SIDE):
                lhs = jnp.concatenate(
                    [rows[k0 + j, n, b] for j in range(3) for n in order[lo:hi]], axis=0
                )
                more = dot(lhs, w[b])
                total = more if total is None else total + more
            size = (hi - lo) * ROWS
            for j in range(3):
                out[j, lo * ROWS : hi * ROWS] = total[j * size : (j + 1) * size].astype(BF)
            cut = pl.ds(lo * ROWS, size)
            for j in NEAR:
                sem = (part, k0 + j - 1)
                partial.append(
                    send(out.at[j - 1, cut], got.at[j - 1, cut], xs.at[sem], xr.at[sem], along(-j))
                )

    ring.cores((0, 1, 2, 7))
    products(0, 0, 8)
    ring.cores((3, 4))
    products(1, 8, 12)
    for lhs, w, acc in ((nx, gqk, accq), (ny, gvt, accv)):
        total = dot(lhs[0], w[0])
        for b in range(1, SIDE):
            total = total + dot(lhs[b], w[b])
        acc[...] = total
    ring.step(3, NONE)
    uring = Ring(
        lambda n: uall.at[n], lambda n, i: uall.at[n, pl.ds(HALF * i, HALF)], us, ur, vs, vr
    )
    uring.start()
    ring.cores((5, 6))
    products(2, 12, 16)
    for copy in partial:
        copy.wait_recv()

    for p, n in enumerate(order):
        at_n = pl.ds(pl.multiple_of(n * ROWS, ROWS), ROWS)
        at_p = slice(p * ROWS, (p + 1) * ROWS)
        total = accq[at_n]
        for j in range(3):
            total = total + rq[j, at_p].astype(F32)
        qk[at_n] = total.astype(BF)
        total = accv[at_n]
        for j in range(3):
            total = total + rv[j, at_p].astype(F32)
        vt[at_n, :WIDE] = total[:, :WIDE].astype(BF)
        vt[at_n, WIDE:] = (total[:, WIDE:] / math.sqrt(features)).astype(BF)

    loads[10].wait()
    loads[11].wait()
    loads[12].wait()
    at_row = lax.broadcasted_iota(jnp.int32, (COUNT, COUNT), 0)
    at_col = lax.broadcasted_iota(jnp.int32, (COUNT, COUNT), 1)
    allowed = (nearv[...] == 1) | (jnp.abs(at_row - at_col) <= 1)
    for h in range(2):
        cut = slice(h * HALF, (h + 1) * HALF)
        cut2 = slice(WIDE + h * HALF, WIDE + (h + 1) * HALF)
        scores = dot_t(qk[:, cut], qk[:, cut2]) / math.sqrt(HEAD_DIM) + biasv[h]
        scores = jnp.where(allowed, scores, -jnp.inf)
        e = jnp.exp(scores - jnp.max(scores, axis=1, keepdims=True))
        p = (e / jnp.sum(e, axis=1, keepdims=True)).astype(BF)
        probs[h] = p
        mix[:, cut] = dot(p, vt[:, cut]).astype(BF)
        mix[:, cut2] = dot(p, vt[:, cut2]).astype(BF)

    moved = []
    for k in AROUND:
        to = pl.ds(pl.multiple_of(((t + k) % 16) * ROWS, ROWS), ROWS)
        moved.append(send(mix.at[to], full.at[y, x, t], ts.at[k], tr.at[k], along_t(k)))
    full[y, x, t] = mix[some]
    uring.step(1, ALL)

    for k, (i, j) in enumerate(plane):
        yy, xx = (y + i) % SIDE, (x + j) % SIDE
        others.append(
            send(diff.at[yy * SIDE + xx], diffs.at[me], ds.at[k], dr.at[k], (yy * SIDE + xx, t))
        )
    for copy in moved:
        copy.wait_recv()
    sweeps = [
        Sweep(0, full, as_.at[0], ar.at[0], bs.at[0], br.at[0]),
        Sweep(1, full, as_.at[1], ar.at[1], bs.at[1], br.at[1]),
    ]
    for sweep in sweeps:
        sweep.start()
    for sweep in sweeps:
        sweep.across(0)
    for sweep in sweeps:
        sweep.relay()
    for sweep in sweeps:
        sweep.across(1)
        sweep.across(2)
    uring.step(2, ALL)
    for sweep in sweeps:
        sweep.relay_across(0)
    uring.step(3, ((0,), (1,)))
    for sweep in sweeps:
        sweep.far()
        sweep.across(3)
    for q in (1, 2):
        for sweep in sweeps:
            sweep.relay_across(q)
    uring.finish()
    for sweep in sweeps:
        sweep.relay_across(3)
    uring.cores(range(8))
    for sweep in sweeps:
        sweep.last()

    acc1[...] = jnp.zeros_like(acc1)
    acc2[...] = jnp.zeros_like(acc2)

    def forward(k, _):
        at_k = pl.ds(k * 4, 4)
        parts = [full[:, :, k * 4 + i].reshape(COUNT, 2 * WIDE) for i in range(4)]
        w = uall[at_k].reshape(4 * WIDE, 2 * BLOCK)
        acc1[...] += dot(jnp.concatenate([p[:, :WIDE] for p in parts], axis=1), w)
        acc2[...] += dot(jnp.concatenate([p[:, WIDE:] for p in parts], axis=1), w[:, :BLOCK])
        return 0

    lax.fori_loop(0, 4, forward, 0)
    for copy in others:
        copy.wait_recv()
    err[...] = ((diffs[...].reshape(COUNT, BLOCK) + acc1[:, :BLOCK]) * factor).astype(BF)
    terr[...] = ((acc1[:, BLOCK:] * scale_out + acc2[...]) * factor).astype(BF)

    def backward(n, _):
        part = dot_t(terr[...], uall[n, :, :BLOCK]) + scale_out * dot_t(err[...], uall[n, :, BLOCK:])
        bp[n] = part.astype(BF).reshape(SIDE, SIDE, ROWS, WIDE)
        return 0

    first_b = []
    cuts = ((0, 3), (3, 8))
    for part, (a, b) in enumerate(cuts):
        here = pl.ds(a, b - a)
        lax.fori_loop(a, b, backward, 0)
        for j in NEAR:
            src, sem = bp.at[here, (y + j) % SIDE], (part, 0, j - 1)
            first_b.append(send(src, ra.at[j - 1, here], s1.at[sem], r1.at[sem], along_y(j)))
        lax.fori_loop(8 + a, 8 + b, backward, 0)
        for j in NEAR:
            src, sem = bp.at[pl.ds(8 + a, b - a), :, (x + j) % SIDE], (part, 1, j - 1)
            first_b.append(send(src, rb.at[j - 1, here], s1.at[sem], r1.at[sem], along_x(j)))

    errt[...] = err[...].astype(F32).T.astype(BF)
    terrt[...] = terr[...].astype(F32).T.astype(BF)

    def outer(n, _):
        both = full[:, :, n].reshape(COUNT, 2 * WIDE)
        part = dot(errt[...], both[:, WIDE:]) + dot(terrt[...], both[:, :WIDE])
        co[n // 2, n % 2] = (part * scale_out).astype(BF)
        return 0

    lax.fori_loop(0, 16, outer, 0)
    swapped = send(co.at[:, 1 - c], rc, s7.at[0], r7.at[0], other_core())


    def pair(k, _):
        sc[k] = (co[k, c].astype(F32) + rc[k].astype(F32)).astype(BF)
        return 0

    shares = []

    def pass_on(step):
        for way in range(2):
            sign = 1 - 2 * way
            slot = (z + sign * (4 - step) + 8) % 8
            if step == 0:
                cut = pl.ds(way * (BLOCK // 2), BLOCK // 2)
                src, dst = sc.at[slot, cut], rz.at[way, 0, cut]
            else:
                shares[2 * (step - 1) + way].wait_recv()
                if step == 1:
                    a, b = way * (BLOCK // 2), (way + 1) * (BLOCK // 2)
                    tx[way, 0] = sc[slot]
                    total = sc[slot, a:b].astype(F32) + rz[way, 0, a:b].astype(F32)
                    tx[way, 0, a:b] = total.astype(BF)
                else:
                    total = sc[slot].astype(F32) + rz[way, step - 1].astype(F32)
                    tx[way, step - 1] = total.astype(BF)
                src, dst = tx.at[way, step - 1], rz.at[way, step]
            shares.append(
                send(src, dst, s4.at[way, step], r4.at[way, step], along_z(sign))
            )


    second_b = []
    for part, (a, b) in enumerate(cuts):
        for copy in first_b[6 * part : 6 * part + 6]:
            copy.wait_recv()
        for i in range(SIDE):
            total = bp[a:b, y, i].astype(F32)
            for j in range(3):
                total = total + ra[j, a:b, i].astype(F32)
            sa[i, a:b] = total.astype(BF)
            total = bp[8 + a : 8 + b, i, x].astype(F32)
            for j in range(3):
                total = total + rb[j, a:b, i].astype(F32)
            sb[i, a:b] = total.astype(BF)
        here = pl.ds(a, b - a)
        for j in NEAR:
            src, sem = sa.at[(x + j) % SIDE, here], (part, 0, j - 1)
            second_b.append(send(src, qa.at[j - 1, here], s2.at[sem], r2.at[sem], along_x(j)))
            src, sem = sb.at[(y + j) % SIDE, here], (part, 1, j - 1)
            second_b.append(send(src, qb.at[j - 1, here], s2.at[sem], r2.at[sem], along_y(j)))
        if part == 0:
            swapped.wait_recv()
            lax.fori_loop(0, 8, pair, 0)
            pass_on(0)
    pass_on(1)
    for copy in second_b:
        copy.wait_recv()
    total = sa[x].astype(F32)
    for j in range(3):
        total = total + qa[j].astype(F32)
    done[0:8] = total.astype(BF)
    total = sb[y].astype(F32)
    for j in range(3):
        total = total + qb[j].astype(F32)
    done[8:16] = total.astype(BF)
    third = []
    for k in AROUND:
        third.append(send(done.at[(t + k) % 16], bt.at[t], s3.at[k], r3.at[k], along_t(k)))
    bt[t] = done[t]

    pass_on(2)
    for copy in third:
        copy.wait_recv()
    back = bt[...].reshape(COUNT, WIDE).astype(F32).T.astype(BF)
    fourth = []
    for h in range(2):
        vb[h] = dot(back[h * HALF : (h + 1) * HALF], probs[h]).astype(BF)
        got, along = ((gx, along_x), (gy, along_y))[h]
        for j in NEAR:
            fourth.append(
                send(vb.at[h], got.at[j - 1], s5.at[h, j - 1], r5.at[h, j - 1], along(j))
            )
    pass_on(3)
    loads[13].wait()
    loads[14].wait()
    def inner(a1, b1, a2, b2):
        total = jnp.zeros((8, 128), F32)
        for a, b in ((a1, b1), (a2, b2)):
            prod = a[...] * b[...]
            prod = jnp.sum(prod.reshape(prod.shape[0] // 8, 8, prod.shape[1]), axis=0)
            for k in range(prod.shape[1] // 128):
                total = total + prod[:, k * 128 : (k + 1) * 128]
        return jnp.sum(total, axis=0, keepdims=True)

    pairs = ((bvv, bvv, bov, bov), (bvv, pvv, bov, pov), (pvv, pvv, pov, pov))
    for k, args in enumerate(pairs):
        one[t, 3 + k : 4 + k] = inner(*args)
    one[t, 6:8] = jnp.zeros((2, 128), F32)
    for copy in fourth:
        copy.wait_recv()
    fifth = []
    for k in (2, 1, 3, 0):
        for h, own, got, mine, outf, outb, to, along in (
            (0, nx, gx, y, cxf, cxb, hx, along_y),
            (1, ny, gy, x, cyf, cyb, hy, along_x),
        ):
            b = (mine + k) % SIDE
            total = dot(vb[h], own[b])
            for j in range(3):
                total = total + dot(got[j], rows[3 * h + j, :, b].reshape(COUNT, BLOCK))
            total = total * scale_value
            if k == 0:
                outf[...] = total
            else:
                outb[k - 1] = total.astype(BF)
                fifth.append(
                    send(outb.at[k - 1], to.at[k - 1], s6.at[h, k - 1], r6.at[h, k - 1], along(k))
                )
    for copy in fifth:
        copy.wait_recv()
    for h, (own, got) in enumerate(((cxf, hx), (cyf, hy))):
        total = own[...]
        for j in range(3):
            total = total + got[j].astype(F32)
        cv[:, h * HALF : (h + 1) * HALF] = total.T
    for copy in shares[6:]:
        copy.wait_recv()
    total = sc[z].astype(F32)
    for way in range(2):
        total = total + rz[way, 3].astype(F32)
    cw[...] = total.T

    pairs = ((cv, bvv, cw, bov), (cv, cv, cw, cw), (cv, pvv, cw, pov))
    for k, args in enumerate(pairs):
        one[t, k : k + 1] = inner(*args)
    rounds = []
    for k in AROUND:
        rounds.append(send(one.at[t], one.at[t], o1.at[k], i1.at[k], along_t(k)))
    for copy in rounds:
        copy.wait_recv()
    two[me] = jnp.sum(one[...], axis=0)
    for k, (i, j) in enumerate(plane):
        peer = at(y + i, x + j, t)
        rounds.append(send(two.at[me], two.at[me], o2.at[k], i2.at[k], peer))
    for copy in rounds[15:]:
        copy.wait_recv()
    sums = jnp.sum(jnp.sum(two[...], axis=0), axis=1, keepdims=True) / entries
    beta_before = pb[0, 0]
    cb, cc, cp, bb, bq, pp = (sums[k : k + 1] for k in range(6))
    alpha = cb
    squares = cc + alpha * alpha * bb + beta_before * beta_before * pp
    squares = squares - 2.0 * (alpha * cb + beta_before * (cp - alpha * bq))
    beta = jnp.sqrt(jnp.maximum(squares, 0.0) + epsilon)
    nv[...] = cv[...] - alpha * bvv[...] - beta_before * pvv[...]
    no[...] = cw[...] - alpha * bov[...] - beta_before * pov[...]
    coef[0:1] = jnp.broadcast_to(alpha, (1, 128))
    coef[1:2] = jnp.broadcast_to(beta, (1, 128))
    coef[2:3] = jnp.broadcast_to(1.0 / beta, (1, 128))
    for copy in (
        pieces + weights + others + partial + moved + first_b + second_b
        + third + [swapped] + shares + fourth + fifth + rounds
    ):
        copy.wait_send()
    ring.settle()
    uring.settle()
    for sweep in sweeps:
        for copy in sweep.sent:
            copy.wait_send()


def scale_kernel(rest_value, rest_out, coef, nv, no, out):
    scale = coef[2:3, 0:1]
    nv[...] = rest_value[...] * scale
    no[...] = rest_out[...] * scale
    out[0] = coef[0, 0]
    out[1] = coef[1, 0]


def body(
    tokens,
    target,
    pair_bias,
    neighbours,
    w_query,
    w_key,
    w_value,
    w_out,
    basis_value,
    basis_out,
    prior_value,
    prior_out,
    prior_beta,
):
    def vm(dtype, *dims):
        return pltpu.VMEM(dims, dtype)

    features = 16 * BLOCK
    scratch = [
        vm(BF, 2, ROWS, features),
        vm(BF, ROWS, features),
        vm(BF, COUNT, features),
        vm(BF, 2, SIDE, SIDE, ROWS, BLOCK),
        vm(F32, 16, ROWS, BLOCK),
        vm(F32, 16, ROWS, BLOCK),
        vm(BF, 6, 16, SIDE, ROWS, BLOCK),
        vm(BF, SIDE, BLOCK, 2 * WIDE),
        vm(BF, SIDE, BLOCK, 2 * WIDE),
        vm(BF, SIDE, COUNT, BLOCK),
        vm(BF, SIDE, COUNT, BLOCK),
        vm(BF, 16, WIDE, 2 * BLOCK),
        vm(F32, BLOCK, WIDE),
        vm(F32, WIDE, BLOCK),
        vm(F32, BLOCK, WIDE),
        vm(F32, WIDE, BLOCK),
        vm(jnp.int32, COUNT, COUNT),
        vm(F32, 2, COUNT, COUNT),
        vm(BF, 3, COUNT, 2 * WIDE),
        vm(BF, 3, COUNT, 2 * WIDE),
        vm(BF, 3, COUNT, 2 * WIDE),
        vm(BF, 3, COUNT, 2 * WIDE),
        vm(F32, COUNT, 2 * WIDE),
        vm(F32, COUNT, 2 * WIDE),
        vm(BF, COUNT, 2 * WIDE),
        vm(BF, COUNT, 2 * WIDE),
        vm(BF, 2, COUNT, COUNT),
        vm(BF, COUNT, 2 * WIDE),
        vm(BF, SIDE, SIDE, 16, ROWS, 2 * WIDE),
        vm(F32, COUNT, 2 * BLOCK),
        vm(F32, COUNT, BLOCK),
        vm(BF, COUNT, BLOCK),
        vm(BF, COUNT, BLOCK),
        vm(BF, BLOCK, COUNT),
        vm(BF, BLOCK, COUNT),
        vm(BF, 16, SIDE, SIDE, ROWS, WIDE),
        vm(BF, 3, 8, SIDE, ROWS, WIDE),
        vm(BF, 3, 8, SIDE, ROWS, WIDE),
        vm(BF, SIDE, 8, ROWS, WIDE),
        vm(BF, SIDE, 8, ROWS, WIDE),
        vm(BF, 3, 8, ROWS, WIDE),
        vm(BF, 3, 8, ROWS, WIDE),
        vm(BF, 16, ROWS, WIDE),
        vm(BF, 16, ROWS, WIDE),
        vm(BF, 8, 2, BLOCK, WIDE),
        vm(BF, 8, BLOCK, WIDE),
        vm(BF, 8, BLOCK, WIDE),
        vm(BF, 2, 4, BLOCK, WIDE),
        vm(BF, 2, 3, BLOCK, WIDE),
        vm(BF, 2, HALF, COUNT),
        vm(BF, 3, HALF, COUNT),
        vm(BF, 3, HALF, COUNT),
        vm(F32, HALF, BLOCK),
        vm(F32, HALF, BLOCK),
        vm(BF, 3, HALF, BLOCK),
        vm(BF, 3, HALF, BLOCK),
        vm(BF, 3, HALF, BLOCK),
        vm(BF, 3, HALF, BLOCK),
        vm(F32, BLOCK, WIDE),
        vm(F32, WIDE, BLOCK),
        vm(F32, 16, 8, 128),
        vm(F32, 16, 8, 128),
        DMA((15,)),
        DMA((2, 6)), DMA((2, 6)),
        DMA((2, 4)), DMA((2, 4)),
        DMA((15,)), DMA((15,)),
        DMA((2, 3, 2)), DMA((2, 3, 2)), DMA((8,)), DMA((8,)),
        DMA((2, 4, 2)), DMA((2, 4, 2)), DMA((8,)), DMA((8,)),
        DMA((3, 6)), DMA((3, 6)),
        DMA((16,)), DMA((16,)),
        DMA((2, 4)), DMA((2, 4)), DMA((2, 4, 4)), DMA((2, 4, 4)),
        DMA((2, 2, 3)), DMA((2, 2, 3)),
        DMA((2, 2, 3)), DMA((2, 2, 3)),
        DMA((16,)), DMA((16,)),
        DMA((2, 4)), DMA((2, 4)),
        DMA((2, 3)), DMA((2, 3)),
        DMA((2, 3)), DMA((2, 3)),
        DMA((1,)), DMA((1,)),
        DMA((16,)), DMA((16,)), DMA((15,)), DMA((15,)),
    ]
    rest_value, rest_out, coef = pl.pallas_call(
        step_kernel,
        out_shape=(
            jax.ShapeDtypeStruct((BLOCK, WIDE), F32),
            jax.ShapeDtypeStruct((WIDE, BLOCK), F32),
            jax.ShapeDtypeStruct((8, 128), F32),
        ),
        in_specs=[ANY] * 12 + [SMEM],
        out_specs=(VMEM, VMEM, VMEM),
        scratch_shapes=scratch,
        compiler_params=pltpu.CompilerParams(
            collective_id=0, has_side_effects=True, vmem_limit_bytes=58 * 2**20
        ),
    )(
        tokens,
        target,
        pair_bias,
        neighbours,
        w_query,
        w_key,
        w_value,
        w_out,
        basis_value,
        basis_out,
        prior_value,
        prior_out,
        prior_beta.reshape(1, 1),
    )
    return pl.pallas_call(
        scale_kernel,
        out_shape=(
            jax.ShapeDtypeStruct((BLOCK, WIDE), F32),
            jax.ShapeDtypeStruct((WIDE, BLOCK), F32),
            jax.ShapeDtypeStruct((2,), F32),
        ),
        in_specs=[VMEM] * 3,
        out_specs=(VMEM, VMEM, SMEM),
    )(rest_value, rest_out, coef)


def solution(mesh):
    placed = (
        P("dp", None),
        P("dp", None),
        P("dp", "tensor", None),
        P("dp", None),
        P("dp", "tensor"),
        P("dp", "tensor"),
        P("dp", "tensor"),
        P("tensor", "dp"),
        P("dp", "tensor"),
        P("tensor", "dp"),
        P("dp", "tensor"),
        P("tensor", "dp"),
        P(),
    )
    return jax.shard_map(
        body,
        mesh=mesh,
        in_specs=placed,
        out_specs=(P("dp", "tensor"), P("tensor", "dp"), P()),
        check_vma=False,
    )
```
